32 devices in a mesh: dp: 16 (over z, y, x), shard: 2 (over core).
Axes of the slice: x: 2, y: 2, z: 4, core: 2. Of those that a mesh axis runs over, the one named last changes fastest.
Arguments:
- tokens: bfloat16 [16, 1024, 512], P('dp', 'shard'), may hold values from -6 to 6
- segments: int32 [16, 1024], P('dp'), may hold values from 0 to 6, as said below
- fill_length: int32 [16], P('dp'), may hold values from 640 to 1024
- query_weight: bfloat16 [512, 512], P(('dp', 'shard')), may hold values from -0.375 to 0.375
- key_weight: bfloat16 [512, 512], P(('dp', 'shard')), may hold values from -0.375 to 0.375
- value_weight: bfloat16 [512, 512], P(('dp', 'shard')), may hold values from -0.25 to 0.25
- output_weight: bfloat16 [512, 512], P(('dp', 'shard')), may hold values from -1.5 to 1.5
- query_bias: bfloat16 [512], P(('dp', 'shard')), may hold values from -4 to 4
- value_bias: bfloat16 [512], P(('dp', 'shard')), may hold values from -4 to 4
- output_bias: bfloat16 [512], P(('dp', 'shard')), may hold values from -6 to 6
- inner_weight: bfloat16 [512, 2048], P(('dp', 'shard')), may hold values from -0.25 to 0.25
- inner_bias: bfloat16 [2048], P(('dp', 'shard')), may hold values from -6 to 6
- outer_weight: bfloat16 [2048, 512], P(('dp', 'shard')), may hold values from -0.125 to 0.125
- outer_bias: bfloat16 [512], P(('dp', 'shard')), may hold values from -6 to 6
- residual_gates: float32 [2], replicated, may hold values from 0.5 to 1.5
- cotangent: bfloat16 [16, 1024, 512], P('dp', 'shard'), may hold values from -6 to 6
Outputs:
- layer_output: bfloat16 [16, 1024, 512], P('dp', 'shard')
- token_grads: float32 [16, 1024, 512], P('dp', 'shard')
- grad_query_weight: float32 [512, 512], P(('dp', 'shard'))
- grad_key_weight: float32 [512, 512], P(('dp', 'shard'))
- grad_value_weight: float32 [512, 512], P(('dp', 'shard'))
- grad_output_weight: float32 [512, 512], P(('dp', 'shard'))
- grad_query_bias: float32 [512], P(('dp', 'shard'))
- grad_value_bias: float32 [512], P(('dp', 'shard'))
- grad_output_bias: float32 [512], P(('dp', 'shard'))
- grad_inner_weight: float32 [512, 2048], P(('dp', 'shard'))
- grad_inner_bias: float32 [2048], P(('dp', 'shard'))
- grad_outer_weight: float32 [2048, 512], P(('dp', 'shard'))
- grad_outer_bias: float32 [512], P(('dp', 'shard'))
- grad_residual_gates: float32 [2], replicated
The draws below stay inside these ranges and needn't reach their ends.
Inputs may be any that keep to these rules, and one draw needn't show every extreme that they name: `segments`: numbers never fall along a row; positions with one number form one packed sentence pair.
All inputs are finite; a program needn't handle non-finite values.
Results may differ from the reference program's by a relative error of at most 0.012.
The reference program's roundings to bfloat16 on the way count: a program that leaves them out, or rounds other values in their place, can miss the bound.
Values may be sent and summed in bfloat16 or wider, within the bound.
A program may use at most 128 MiB of HBM per device.

```python
import jax
import jax.numpy as jnp
from jax import lax

D = 512
HEADS = 8
FF = 2048
HEAD_DIM = 64
SEQ = 1024
ROWS = 16


def draw_segments(key, part):
    key = jax.random.fold_in(key, 7)
    left_key, right_key = jax.random.split(key)
    left_cuts = jax.random.randint(left_key, (ROWS, 1, 3), 1, 3 * SEQ // 8)
    right_cuts = jax.random.randint(right_key, (ROWS, 1, 3), 5 * SEQ // 8, SEQ)
    places = jnp.arange(SEQ, dtype=jnp.int32)[None, :, None]
    counted = jnp.sum((places >= left_cuts).astype(jnp.int32), axis=2) + jnp.sum((places >= right_cuts).astype(jnp.int32), axis=2)
    return counted.astype(jnp.int32)


def with_ends(drawn, own_key, least, high):
    longest = drawn.shape.index(max(drawn.shape))
    spots = []
    for shift in (0, 1):
        where = [jax.random.randint(jax.random.fold_in(own_key, axis), (), 0, length) for axis, length in enumerate(drawn.shape)]
        where[longest] = (where[longest] + shift) % drawn.shape[longest]
        spots.append(tuple(where))
    return drawn.at[spots[0]].set(least).at[spots[1]].set(high)


def strengthened(drawn, stream_key, source, target, parts, factor):
    def block_of(axis_at):
        return (jnp.arange(drawn.shape[axis_at]) // (drawn.shape[axis_at] // parts)).reshape((-1,) + (1,) * (drawn.ndim - 1 - axis_at))

    first = jax.random.permutation(stream_key, parts)[block_of(target)]
    second = (block_of(target) + parts // 2) % parts
    return jnp.where((block_of(source) == first) | (block_of(source) == second), factor * drawn, drawn)


def level_of(rng, shape, pieces, low, largest):
    def one(dim, shards_of):
        steps = jax.random.uniform(jax.random.fold_in(jax.random.fold_in(rng, 6), dim), (shards_of,), jnp.float32, low / len(pieces), largest / len(pieces))
        return jnp.repeat(jnp.exp(steps), shape[dim] // shards_of).reshape((-1,) + (1,) * (len(shape) - dim - 1))

    loudness = one(*pieces[0])
    for cut in pieces[1:]:
        loudness = loudness * one(*cut)
    return loudness


def scatter_about(key, shape, scale, most, pieces=(), kind=jnp.bfloat16):
    array = scale * jax.random.normal(key, shape, jnp.float32)
    if pieces:
        array = array * level_of(key, shape, pieces, -0.22, 0.18)
    return jnp.clip(array, -most, most).astype(kind)


def noise_with(key, dims, width, reach, shards, heavy, kind=jnp.bfloat16):
    values = width * jax.random.normal(key, dims, jnp.float32)
    if shards:
        values = values * level_of(key, dims, shards, -0.22, 0.18)
    return jnp.clip(strengthened(values, jax.random.fold_in(key, 3), *heavy), -reach, reach).astype(kind)


def setup_inputs(seed: int = 0) -> dict:
    streams_of = jax.random.split(jax.random.key(seed), 17)
    return {
        "tokens": noise_with(streams_of[0], (ROWS, SEQ, D), 1.0, 6.0, ((0, 16), (1, 2)), (0, 2, 16, 2.0)),
        "segments": draw_segments(jax.random.fold_in(streams_of[16], 71), 0),
        "fill_length": with_ends(jax.random.randint(streams_of[2], (ROWS,), 5 * SEQ // 8, SEQ + 1), jax.random.fold_in(streams_of[2], 1), 5 * SEQ // 8, SEQ).astype(jnp.int32),
        "query_weight": scatter_about(streams_of[3], (D, D), (D // 2) ** -0.5, 0.375, ((0, 32),)),
        "key_weight": scatter_about(streams_of[4], (D, D), (D // 2) ** -0.5, 0.375, ((0, 32),)),
        "value_weight": scatter_about(streams_of[5], (D, D), D ** -0.5, 0.25, ((0, 32),)),
        "output_weight": scatter_about(streams_of[6], (D, D), (D // 32) ** -0.5, 1.5, ((0, 32),)),
        "query_bias": scatter_about(streams_of[7], (D,), 0.3, 4.0, ((0, 32),)),
        "value_bias": scatter_about(streams_of[8], (D,), 0.3, 4.0, ((0, 32),)),
        "output_bias": scatter_about(streams_of[9], (D,), 0.5, 6.0, ((0, 32),)),
        "inner_weight": scatter_about(streams_of[10], (D, FF), D ** -0.5, 0.25, ((0, 32),)),
        "inner_bias": scatter_about(streams_of[11], (FF,), 0.5, 6.0, ((0, 32),)),
        "outer_weight": scatter_about(streams_of[12], (FF, D), FF ** -0.5, 0.125, ((0, 32),)),
        "outer_bias": scatter_about(streams_of[13], (D,), 0.5, 6.0, ((0, 32),)),
        "residual_gates": jnp.clip(jax.random.uniform(streams_of[14], (2,), jnp.float32, 0.5, 1.5), 0.5, 1.5),
        "cotangent": noise_with(streams_of[15], (ROWS, SEQ, D), 1.0, 6.0, ((0, 16), (1, 2)), (0, 2, 16, 2.0)),
    }


@jax.custom_vjp
def low(v):
    return lax.optimization_barrier(v.astype(jnp.bfloat16)).astype(jnp.float32)

@jax.custom_vjp
def low_back(v):
    return v

def low_keep(v):
    return (low(v), None)

def low_pass(kept, grad):
    return (grad,)

def back_keep(v):
    return (v, None)

def back_low(kept, grad):
    return (low(grad),)
low.defvjp(low_keep, low_pass)
low_back.defvjp(back_keep, back_low)

def matmul(left, right):
    return jnp.dot(left, right, precision=lax.Precision.HIGHEST)

def exact_gelu(value):
    return jax.nn.gelu(value, approximate=False)

def attend_row(queries, keys_all, values_all, seg_row, fill_row):
    places = jnp.arange(SEQ, dtype=jnp.int32)
    same = seg_row[:, None] == seg_row[None, :]
    live = (places[None, :] < fill_row) | (places[None, :] == places[:, None])
    allowed = same & live
    scores = jnp.einsum('qhd,khd->hqk', queries, keys_all, precision=lax.Precision.HIGHEST) * HEAD_DIM ** (-0.5)
    scores = jnp.where(allowed[None, :, :], low_back(scores), -1e+30)
    weights = low(jax.nn.softmax(scores, axis=-1))
    return jnp.einsum('hqk,khd->qhd', weights, values_all, precision=lax.Precision.HIGHEST)

def reference(tokens, segments, fill_length, query_weight, key_weight, value_weight, output_weight, query_bias, value_bias, output_bias, inner_weight, inner_bias, outer_weight, outer_bias, residual_gates, cotangent):
    checked_row = jax.checkpoint(attend_row)
    shaped = (ROWS, SEQ, HEADS, HEAD_DIM)

    def forward(source, query_w, key_w, value_w, output_w, query_b, value_b, output_b, inner_w, inner_b, outer_w, outer_b, gate_pair):
        source = source.reshape(ROWS * SEQ, D)
        queries = low(low_back(matmul(source, query_w) + query_b))
        keys_all = low(low_back(matmul(source, key_w)))
        values_all = low(low_back(matmul(source, value_w) + value_b))
        mixed = lax.map(lambda row_items: checked_row(row_items[0], row_items[1], row_items[2], row_items[3], row_items[4]), (queries.reshape(shaped), keys_all.reshape(shaped), values_all.reshape(shaped), segments, fill_length))
        mixed = low(low_back(mixed.reshape(ROWS * SEQ, D)))
        attn = low_back(matmul(mixed, output_w) + output_b)
        resid = source + gate_pair[0] * attn
        resid_low = low(resid)
        hidden = low_back(matmul(resid_low, inner_w) + inner_b)
        activ = low(exact_gelu(hidden))
        ffn = low_back(matmul(activ, outer_w) + outer_b)
        return (resid + gate_pair[1] * ffn).reshape(ROWS, SEQ, D)
    layer, pullback = jax.vjp(forward, tokens.astype(jnp.float32), query_weight.astype(jnp.float32), key_weight.astype(jnp.float32), value_weight.astype(jnp.float32), output_weight.astype(jnp.float32), query_bias.astype(jnp.float32), value_bias.astype(jnp.float32), output_bias.astype(jnp.float32), inner_weight.astype(jnp.float32), inner_bias.astype(jnp.float32), outer_weight.astype(jnp.float32), outer_bias.astype(jnp.float32), residual_gates.astype(jnp.float32))
    grads = pullback(cotangent.astype(jnp.float32))
    return (layer.astype(jnp.bfloat16), grads[0], grads[1], grads[2], grads[3], grads[4], grads[5], grads[6], grads[7], grads[8], grads[9], grads[10], grads[11], grads[12])
```

```python
import jax
import jax.numpy as jnp
from jax import lax
from jax.experimental import pallas as pl
from jax.experimental.pallas import tpu as pltpu
from jax.sharding import PartitionSpec as P

MESH = pl.DeviceIdType.MESH
BF = jnp.bfloat16
F32 = jnp.float32
HEADS = 8
GROUP = 16
PAIRS = 4
STEPS = 4


def dot(left, right, left_dim, right_dim):
    return lax.dot_general(
        left, right, (((left_dim,), (right_dim,)), ((), ())), preferred_element_type=F32
    )


def gelu_parts(hidden):
    size = jnp.abs(hidden) * 0.7071067811865476
    recip = 1.0 / (1.0 + 0.3275911 * size)
    expo = jnp.exp(-size * size)
    poly = recip * (
        0.127414796
        + recip * (-0.142248368 + recip * (0.7107068705 + recip * (-0.7265760135 + recip * 0.5307027145)))
    )
    tail = poly * expo
    cdf = jnp.where(hidden >= 0, 1.0 - tail, tail)
    return hidden * cdf, cdf + hidden * expo * 0.3989422804014327


def natural(value):
    width = value.shape[-1]
    return value.reshape(8, 4, 16, width).transpose(1, 0, 2, 3).reshape(512, width)


def by_chip(value):
    width = value.shape[-1]
    return value.reshape(4, 8, 16, width).transpose(1, 0, 2, 3).reshape(2, 2, 2, 64, width)


def col_sums(value):
    return dot(jnp.ones((8, value.shape[0]), BF), value, 1, 0)


def layer_kernel(
    tok,
    cot,
    seg,
    fill,
    gates,
    wcat,
    wout_proj,
    win,
    wout,
    layer_o,
    tg_o,
    gq_o,
    gk_o,
    gv_o,
    go_o,
    gi_o,
    gout_o,
    small_o,
    xrow,
    cotv,
    wq,
    wo,
    wf,
    maskb,
    qt,
    kt,
    vt,
    probs,
    st,
    pb,
    mixt,
    attn,
    rlow,
    gffn,
    gmixt,
    dqt,
    dkv,
    rkv,
    gf,
    rcf,
    s1f,
    r1f,
    s2f,
    r2f,
    s3f,
    r3f,
    s3o,
    r3o,
    go,
    rco,
    s1o,
    r1o,
    s2o,
    r2o,
    s3w,
    r3w,
    s1q,
    r1q,
    s2q,
    r2q,
    s3q,
    r3q,
    ksum,
    bb,
    rb,
    biasb,
    send_sem,
    recv_sem,
    local_sem,
):
    ffn, gres = maskb.at[pl.ds(0, 512)], maskb.at[pl.ds(512, 512)]
    hid, gac = st.at[pl.ds(0, 512)], st.at[pl.ds(512, 512)]
    act, ghid = pb.at[0, pl.ds(0, 512)], pb.at[0, pl.ds(512, 512)]

    dp = lax.axis_index("dp")
    c = lax.axis_index("shard")
    lo = lax.rem(dp, GROUP)
    z = lax.div(lo, 4)
    y = lax.rem(lax.div(lo, 2), 2)
    x = lax.rem(lo, 2)
    cc, xx, yy = 1 - c, 1 - x, 1 - y

    def zk(k):
        return lax.rem(z + (k % 4), 4)

    zs = [zk(k) for k in range(4)]
    XP = (dp + 1 - 2 * x, c)
    YP = (dp + 2 - 4 * y, c)
    ZP = [None] + [(dp + 4 * (zs[k] - z), c) for k in (1, 2, 3)]
    SB = (dp, cc)

    def rows(place):
        return pl.ds(pl.multiple_of(place * 16, 16), 16)

    def cols(place):
        return pl.ds(pl.multiple_of(place * 512, 512), 512)

    table = {}
    ids = {}

    def same(ref, dev):
        return (ref, ref, dev)

    for k in (1, 2, 3):
        table["qz", k] = lambda k=k: same(wq.at[y, x, c, rows(z)], ZP[k])
        table["oz", k] = lambda k=k: same(wo.at[y, x, c, rows(z)], ZP[k])
    for k in range(4):
        table["qx", k] = lambda k=k: same(wq.at[y, x, c, rows(zs[(-k) % 4])], XP)
        table["qy", k] = lambda k=k: same(wq.at[y, x, c, rows(zs[(-k) % 4])], YP)
        if k < 2:
            table["qr", k] = lambda k=k: same(wq.at[y, xx, c, rows(zs[(-k) % 4])], YP)
        else:
            table["qr", k] = lambda k=k: same(wq.at[yy, x, c, rows(zs[(-k) % 4])], XP)
    spots = {"me": lambda: (y, x), "x": lambda: (y, xx), "y": lambda: (yy, x), "d": lambda: (yy, xx)}
    for name, spot in spots.items():
        table["qs", name] = lambda spot=spot: same(wq.at[(*spot(), c)], SB)
        table["os", name] = lambda spot=spot: same(wo.at[(*spot(), c)], SB)
    table["ox"] = lambda: same(wo.at[y, x, c], XP)
    table["oy"] = lambda: same(wo.at[y, x, c], YP)
    table["orx"] = lambda: same(wo.at[y, xx, c, pl.ds(0, 32)], YP)
    table["ory"] = lambda: same(wo.at[yy, x, c, pl.ds(32, 32)], XP)
    for s in range(STEPS):
        for k in (1, 2, 3):
            table["fz", s, k] = lambda s=s, k=k: (
                win.at[:, cols(zs[(k + s) % 4])],
                wf.at[s, y, x, c, rows(z)],
                ZP[k],
            )
        if s:
            table["fo", s] = lambda s=s: (wout, wf.at[s, y, x, c, pl.ds(64, 64)], ZP[4 - s])
        table["fx", s] = lambda s=s: same(wf.at[s, y, x, c], XP)
        table["fy", s] = lambda s=s: same(wf.at[s, y, x, c], YP)
        table["frx", s] = lambda s=s: same(wf.at[s, y, xx, c, pl.ds(0, 64)], YP)
        table["fry", s] = lambda s=s: same(wf.at[s, yy, x, c, pl.ds(64, 64)], XP)
        for name, spot in spots.items():
            table["fs", s, name] = lambda s=s, spot=spot: same(wf.at[(s, *spot(), c)], SB)
    table["tok"] = lambda: (xrow.at[pl.ds(0, 512)], xrow.at[pl.ds(512, 512)], SB)
    groups = {}
    for s in range(STEPS):
        groups["f", s] = (gf.at[s], rcf.at[s], s1f.at[s], r1f.at[s], s2f.at[s], r2f.at[s], s3f.at[s], r3f.at[s])
        if s:
            table["o3", s] = lambda s=s: (s3o.at[s - 1], r3o.at[s - 1], ZP[s])
    groups["o"] = (go, rco, s1o, r1o, s2o, r2o, s3w, r3w)
    for p in range(PAIRS):
        gq = gf.at[p, :, :, :, pl.ds(0, 64), pl.ds(0, 384)]
        rcq = rcf.at[p, :, :, pl.ds(0, 64), pl.ds(0, 384)]
        groups["q", p] = (gq, rcq, s1q.at[p], r1q.at[p], s2q.at[p], r2q.at[p], s3q.at[p], r3q.at[p])
        table["kv", p] = lambda p=p: (dkv.at[p % 2, :, :, pl.ds(512, 512)], rkv.at[p], SB)
    for g, (grad, rc, s1, r1, s2, r2, s3, r3) in groups.items():
        table["c", g] = lambda grad=grad, rc=rc: (grad.at[:, :, cc], rc, SB)
        table["a1", g] = lambda s1=s1, r1=r1: (s1.at[0], r1.at[0], XP)
        table["b1", g] = lambda s1=s1, r1=r1: (s1.at[1], r1.at[1], YP)
        table["a2", g] = lambda s2=s2, r2=r2: (s2.at[0], r2.at[0], YP)
        table["b2", g] = lambda s2=s2, r2=r2: (s2.at[1], r2.at[1], XP)
        for k in (1, 2, 3):
            table["z3", g, k] = lambda s3=s3, r3=r3, k=k: (s3.at[k - 1], r3.at[k - 1], ZP[k])
    table["bc"] = lambda: (bb.at[0], rb.at[0], SB)
    table["bx"] = lambda: (bb.at[1], rb.at[1], XP)
    table["by"] = lambda: (bb.at[2], rb.at[2], YP)
    for k in (1, 2, 3):
        table["bz", k] = lambda k=k: (bb.at[3], rb.at[2 + k], ZP[k])
    for place, key in enumerate(table):
        ids[key] = place

    def cp(*key):
        key = key if len(key) > 1 else key[0]
        src, dst, dev = table[key]()
        place = ids[key]
        return pltpu.make_async_remote_copy(
            src_ref=src,
            dst_ref=dst,
            send_sem=send_sem.at[place],
            recv_sem=recv_sem.at[place],
            device_id=dev,
            device_id_type=MESH,
        )

    def start(*key):
        cp(*key).start()

    def recv(*key):
        cp(*key).wait_recv()

    local = [
        (wcat, wq.at[y, x, c, rows(z)]),
        (tok, xrow.at[pl.ds(0, 512)]),
        (cot, cotv),
        (wout_proj, wo.at[y, x, c, rows(z)]),
        (wout, wf.at[0, y, x, c, pl.ds(64, 64)]),
    ] + [(win.at[:, cols(zs[s])], wf.at[s, y, x, c, rows(z)]) for s in range(STEPS)]
    local = [pltpu.make_async_copy(src, dst, local_sem.at[i]) for i, (src, dst) in enumerate(local)]
    for one in local:
        one.start()
    barrier = pltpu.get_barrier_semaphore()
    for dev in (XP, YP, ZP[1], ZP[2], ZP[3], SB):
        pl.semaphore_signal(barrier, inc=1, device_id=dev, device_id_type=MESH)
    pl.semaphore_wait(barrier, 6)

    local[0].wait()
    for k in (1, 2, 3):
        start("qz", k)
    start("qx", 0)
    start("qy", 0)
    local[1].wait()
    start("tok")

    own_seg = seg[:, pl.ds(pl.multiple_of(c * 512, 512), 512)].astype(F32)
    sib_seg = seg[:, pl.ds(pl.multiple_of(cc * 512, 512), 512)].astype(F32)
    used = fill[0]
    for block in range(8):
        half, inside = block // 4, block % 4
        part = (own_seg if half == 0 else sib_seg)[:, inside * 128 : inside * 128 + 128]
        seg_keys = jnp.broadcast_to(part, (128, 128)).T
        seg_keys = jnp.concatenate([seg_keys] * 4, axis=1)
        base = (c if half == 0 else cc) * 512 + inside * 128
        key_at = lax.broadcasted_iota(jnp.int32, (128, 512), 0) + base
        query_at = lax.broadcasted_iota(jnp.int32, (128, 512), 1) + c * 512
        allowed = (seg_keys == own_seg) & ((key_at < used) | (key_at == query_at))
        maskb[block * 128 : block * 128 + 128, :] = jnp.where(allowed, 0.0, -1e30)

    gate_attn = gates[0]
    gate_feed = gates[1]
    local[2].wait()
    upstream = cotv[...].astype(F32)
    gffn[...] = (gate_feed * upstream).astype(BF)

    for k in (1, 2, 3):
        recv("qz", k)
        start("qx", k)
        start("qy", k)
    start("qs", "me")
    for one in local[3:]:
        one.wait()
    for k in (1, 2, 3):
        start("oz", k)
    for s in range(STEPS):
        for k in (1, 2, 3):
            start("fz", s, k)
        if s:
            start("fo", s)
    for k in (0, 1):
        recv("qx", k)
        start("qr", k)
    for k in (2, 3):
        recv("qy", k)
        start("qr", k)
    recv("qx", 2)
    recv("qx", 3)
    start("qs", "x")
    recv("qy", 0)
    recv("qy", 1)
    start("qs", "y")
    for k in (1, 2, 3):
        recv("oz", k)
    start("ox")
    start("oy")
    start("os", "me")
    for k in range(4):
        recv("qr", k)
    start("qs", "d")

    def plane_first(s):
        for k in (1, 2, 3):
            recv("fz", s, k)
        if s:
            recv("fo", s)
        start("fx", s)
        start("fy", s)
        start("fs", s, "me")

    def plane_second(s):
        recv("fx", s)
        start("frx", s)
        start("fs", s, "x")
        recv("fy", s)
        start("fry", s)
        start("fs", s, "y")

    def plane_third(s):
        recv("frx", s)
        recv("fry", s)
        start("fs", s, "d")

    def all_here(s):
        for name in spots:
            recv("fs", s, name)

    plane_first(0)
    for name in spots:
        recv("qs", name)
    recv("tok")

    held = wq[:, :, :, :, pl.ds(1536, 128)].reshape(8, 4, 16, 128).transpose(1, 0, 2, 3).reshape(32, 16, 128)
    biasb[...] = jnp.sum(held.astype(F32), axis=1).astype(BF)

    def bias_row(offset, per, width):
        lane = lax.broadcasted_iota(jnp.int32, (128, width), 0)
        at = lax.broadcasted_iota(jnp.int32, (128, width), 1)
        pick = (lane == offset + lax.rem(at, per)).astype(F32).astype(BF)
        spread = dot(biasb[...], pick, 1, 0)
        owner = lax.broadcasted_iota(jnp.int32, (32, width), 0)
        at = lax.broadcasted_iota(jnp.int32, (32, width), 1)
        return jnp.sum(jnp.where(owner == lax.div(at, per), spread, 0.0), axis=0, keepdims=True)

    first_row = lax.broadcasted_iota(jnp.int32, (16, 512), 0) == 0
    ones_row = jnp.where(first_row, 1.0, 0.0).astype(BF)

    def as_rank_one(row):
        return jnp.where(first_row, jnp.broadcast_to(row, (16, 512)), 0.0).astype(BF)

    bias_q = as_rank_one(bias_row(0, 16, 512))
    bias_v = as_rank_one(bias_row(16, 16, 512))
    for p in range(PAIRS):
        at = slice(p * 128, p * 128 + 128)
        weights = natural(wq[:, :, :, :, p * 384 : p * 384 + 384])
        ours = dot(weights, xrow[0:512], 0, 1)
        theirs = dot(weights[:, 128:384], xrow[512:1024], 0, 1)
        add_q = dot(bias_q[:, at], ones_row, 0, 0)
        add_v = dot(bias_v[:, at], ones_row, 0, 0)
        qt[at] = ((ours[0:128] + add_q).astype(BF).astype(F32) * 0.125).astype(BF)
        kt[at, 0:512] = ours[128:256].astype(BF)
        vt[at, 0:512] = (ours[256:384] + add_v).astype(BF)
        kt[at, 512:1024] = theirs[0:128].astype(BF)
        vt[at, 512:1024] = (theirs[128:256] + add_v).astype(BF)

    def o_second():
        recv("ox")
        start("orx")
        start("os", "x")
        recv("oy")
        start("ory")
        start("os", "y")

    def o_third():
        recv("orx")
        recv("ory")
        start("os", "d")

    o_second()
    plane_first(1)

    def forward_pair(p, carry):
        for j in range(2):
            head = p * 2 + j
            at = pl.ds(pl.multiple_of(head * 64, 64), 64)
            keys, values = kt[at], vt[at]
            for part in range(2):
                lanes = slice(part * 256, part * 256 + 256)
                raw = dot(keys, qt[at, lanes], 0, 0)
                highest = jnp.full((8, 256), -jnp.inf, F32)
                for b in range(8):
                    r = slice(b * 128, b * 128 + 128)
                    score = raw[r] + maskb[r, lanes]
                    st[r, lanes] = score
                    highest = jnp.maximum(highest, jnp.max(score.reshape(16, 8, 256), axis=0))
                highest = jnp.max(highest, axis=0, keepdims=True)
                total = jnp.zeros((8, 256), F32)
                for b in range(8):
                    r = slice(b * 128, b * 128 + 128)
                    expo = jnp.exp(st[r, lanes] - highest)
                    st[r, lanes] = expo
                    total = total + jnp.sum(expo.reshape(16, 8, 256), axis=0)
                scale = 1.0 / jnp.sum(total, axis=0, keepdims=True)
                for b in range(8):
                    r = slice(b * 128, b * 128 + 128)
                    prob = st[r, lanes] * scale
                    probs[head, r, lanes] = prob
                    pb[0, r, lanes] = prob.astype(BF)
                mixt[at, lanes] = dot(values, pb[0, :, lanes], 1, 0).astype(BF)

        @pl.when(p == 0)
        def _():
            o_third()

        @pl.when(p == 1)
        def _():
            plane_second(0)

        @pl.when(p == 2)
        def _():
            plane_first(2)

        @pl.when(p == 3)
        def _():
            plane_second(1)
            plane_first(3)

        return carry

    lax.fori_loop(0, PAIRS, forward_pair, 0)

    for name in spots:
        recv("os", name)
    attn[...] = dot(mixt[...], natural(wo[...]), 0, 0) + bias_row(32, 16, 512)
    resid = xrow[0:512].astype(F32) + gate_attn * attn[...]
    rlow[...] = resid.astype(BF)
    ffn[...] = jnp.zeros((512, 512), F32)
    gres[...] = cotv[...].astype(F32)

    def fold_first(g):
        grad, rc, s1 = groups[g][:3]
        half = rc.shape[2] // 2
        recv("c", g)
        for i in range(2):
            s1[0, i] = (grad[i, xx, c, 0:half] + rc[i, xx, 0:half]).astype(BF)
            s1[1, i] = (grad[yy, i, c, half : 2 * half] + rc[yy, i, half : 2 * half]).astype(BF)
        start("a1", g)
        start("b1", g)

    def fold_second(g):
        grad, rc, s1, r1, s2, r2 = groups[g][:6]
        half = rc.shape[2] // 2
        recv("a1", g)
        s2[0] = (grad[yy, x, c, 0:half] + rc[yy, x, 0:half] + r1[0, yy].astype(F32)).astype(BF)
        start("a2", g)
        recv("b1", g)
        s2[1] = (
            grad[y, xx, c, half : 2 * half] + rc[y, xx, half : 2 * half] + r1[1, xx].astype(F32)
        ).astype(BF)
        start("b2", g)

    def fold_third(g):
        grad, rc, s1, r1, s2, r2, s3, r3 = groups[g]
        half = rc.shape[2] // 2
        width = rc.shape[3]
        recv("a2", g)
        upper = grad[y, x, c, 0:half] + rc[y, x, 0:half] + r1[0, y].astype(F32) + r2[0].astype(F32)
        ksum[0:half, 0:width] = upper
        recv("b2", g)
        lower = (
            grad[y, x, c, half : 2 * half]
            + rc[y, x, half : 2 * half]
            + r1[1, x].astype(F32)
            + r2[1].astype(F32)
        )
        ksum[half : 2 * half, 0:width] = lower
        for k in (1, 2, 3):
            s3[k - 1] = ksum[rows(zs[k]), 0:width].astype(BF)
            start("z3", g, k)

    def ffn_third(s):
        fold_third(("f", s))
        gi_o[:, cols(zs[s])] = ksum[rows(z), :]
        if s:
            s3o[s - 1] = ksum[64:128].astype(BF)
            start("o3", s)
        else:
            gout_o[...] = ksum[64:128]

    def small(row, value):
        bb[0, row : row + 1, 0:512] = value

    bb[0, :, 512:640] = jnp.zeros((8, 128), F32)

    def ffn_step(s):
        plane_third(s)
        all_here(s)
        inner = natural(wf[s, :, :, :, 0:64])
        outer = wf[s, :, :, :, 64:128].reshape(512, 512)
        hid[...] = dot(rlow[...], inner, 1, 0) + chunk_bias[s]
        gac[...] = dot(gffn[...], outer, 1, 1)
        for b in range(8):
            r = slice(b * 64, b * 64 + 64)
            value, slope = gelu_parts(hid[r])
            act[r] = value.astype(BF)
            ghid[r] = (gac[r] * slope).astype(BF)
        ffn[...] += dot(act[...], outer, 1, 0)
        gf[s, :, :, :, 64:128] = dot(act[...], gffn[...], 0, 0).reshape(2, 2, 2, 64, 512)
        gf[s, :, :, :, 0:64] = by_chip(dot(rlow[...], ghid[...], 0, 0))
        start("c", ("f", s))
        gres[...] += dot(ghid[...], inner, 1, 1)
        sums = col_sums(ghid[...])[0:1]
        for row in range(4):
            bb[0, 4 + row : 5 + row, 0:512] = jnp.where(
                zs[s] == row, sums, bb[0, 4 + row : 5 + row, 0:512]
            )

    inner_bias = bias_row(64, 64, 2048)
    parts = [inner_bias[:, i * 512 : i * 512 + 512] for i in range(4)]
    chunk_bias = []
    for s in range(STEPS):
        picked = parts[3]
        for i in range(3):
            picked = jnp.where(zs[s] == i, parts[i], picked)
        chunk_bias.append(picked)
    for row in range(4):
        small(4 + row, jnp.zeros((1, 512), F32))

    ffn_step(0)
    plane_second(2)
    ffn_step(1)
    fold_first(("f", 0))
    plane_second(3)
    ffn_step(2)
    fold_first(("f", 1))
    fold_second(("f", 0))
    ffn_step(3)
    fold_first(("f", 2))
    fold_second(("f", 1))
    ffn_third(0)

    ffn[...] += bias_row(48, 16, 512)
    upstream = cotv[...].astype(F32)
    resid = xrow[0:512].astype(F32) + gate_attn * attn[...]
    rlow[...] = (resid + gate_feed * ffn[...]).astype(BF)
    layer_out = pltpu.make_async_copy(rlow, layer_o, local_sem.at[0])
    layer_out.start()
    feed_part = jnp.sum(jnp.sum(upstream * ffn[...], axis=0, keepdims=True), axis=1, keepdims=True)
    attn_part = jnp.sum(jnp.sum(gres[...] * attn[...], axis=0, keepdims=True), axis=1, keepdims=True)
    bb[0, 0:1, 512:640] = jnp.broadcast_to(attn_part, (1, 128))
    bb[0, 1:2, 512:640] = jnp.broadcast_to(feed_part, (1, 128))
    small(3, col_sums(gffn[...])[0:1])
    gattn = (gate_attn * gres[...]).astype(BF)
    small(2, col_sums(gattn)[0:1])
    go[...] = by_chip(dot(mixt[...], gattn, 1, 0))
    start("c", "o")
    gmixt[...] = dot(natural(wo[...]), gattn, 1, 1).astype(BF)

    def backward_pair(p, carry):
        slot = lax.rem(p, 2)
        for j in range(2):
            head = p * 2 + j
            at = pl.ds(pl.multiple_of(head * 64, 64), 64)
            keys, values = kt[at], vt[at]
            for part in range(2):
                lanes = slice(part * 256, part * 256 + 256)
                up = gmixt[at, lanes]
                raw = dot(values, up, 0, 0)
                total = jnp.zeros((8, 256), F32)
                for b in range(8):
                    r = slice(b * 128, b * 128 + 128)
                    block = raw[r]
                    st[r, lanes] = block
                    total = total + jnp.sum((probs[head, r, lanes] * block).reshape(16, 8, 256), axis=0)
                inner = jnp.sum(total, axis=0, keepdims=True)
                for b in range(8):
                    r = slice(b * 128, b * 128 + 128)
                    prob = probs[head, r, lanes]
                    pb[0, r, lanes] = prob.astype(BF)
                    pb[1, r, lanes] = (prob * (st[r, lanes] - inner)).astype(BF)
                dqt[slot, j * 64 : j * 64 + 64, lanes] = (
                    dot(keys, pb[1, :, lanes], 1, 0) * 0.125
                ).astype(BF)
                grad_k = dot(qt[at, lanes], pb[1, :, lanes], 1, 1)
                grad_v = dot(up, pb[0, :, lanes], 1, 1)
                place = slice(j * 64, j * 64 + 64)
                if part == 0:
                    dkv[slot, 0, place] = grad_k
                    dkv[slot, 1, place] = grad_v
                else:
                    dkv[slot, 0, place] += grad_k
                    dkv[slot, 1, place] += grad_v
        return carry

    def finish_pair(p):
        slot = p % 2
        recv("kv", p)
        grad_k = (dkv[slot, 0, :, 0:512] + rkv[p, 0]).astype(BF)
        grad_v = (dkv[slot, 1, :, 0:512] + rkv[p, 1]).astype(BF)
        both = jnp.concatenate([dqt[slot], grad_k, grad_v], axis=0)
        cp("c", ("f", p)).wait_send()
        gf[p, :, :, :, 0:64, 0:384] = by_chip(dot(xrow[0:512], both, 0, 1))
        start("c", ("q", p))
        weights = natural(wq[:, :, :, :, p * 384 : p * 384 + 384])
        gres[...] += dot(both, weights, 0, 1)
        sums = dot(jnp.ones((8, 512), BF), both, 1, 1)
        bb[0, 0:1, p * 128 : p * 128 + 128] = sums[0:1, 0:128]
        bb[0, 1:2, p * 128 : p * 128 + 128] = sums[0:1, 256:384]

    for p in range(PAIRS):
        if p >= 2:
            cp("kv", p - 2).wait_send()
        lax.fori_loop(p, p + 1, backward_pair, 0)
        start("kv", p)
        if p == 0:
            fold_first(("f", 3))
            fold_second(("f", 2))
            ffn_third(1)
            fold_first("o")
        if p == 1:
            finish_pair(0)
            fold_second(("f", 3))
            ffn_third(2)
            fold_second("o")
        if p == 2:
            finish_pair(1)
            fold_first(("q", 0))
            ffn_third(3)
            fold_third("o")
            go_o[...] = ksum[rows(z), :]
        if p == 3:
            finish_pair(2)
            fold_first(("q", 1))
            fold_second(("q", 0))
    finish_pair(3)
    tg_out = pltpu.make_async_copy(gres, tg_o, local_sem.at[1])
    tg_out.start()

    start("bc")

    def q_third(p):
        fold_third(("q", p))
        at = slice(p * 128, p * 128 + 128)
        gq_o[:, at] = ksum[rows(z), 0:128]
        gk_o[:, at] = ksum[rows(z), 128:256]
        gv_o[:, at] = ksum[rows(z), 256:384]

    def q_last(p):
        at = slice(p * 128, p * 128 + 128)
        for k in (1, 2, 3):
            recv("z3", ("q", p), k)
        more = r3q[p, 0].astype(F32) + r3q[p, 1].astype(F32) + r3q[p, 2].astype(F32)
        gq_o[:, at] += more[:, 0:128]
        gk_o[:, at] += more[:, 128:256]
        gv_o[:, at] += more[:, 256:384]

    recv("bc")
    bb[1] = bb[0] + rb[0]
    start("bx")
    fold_first(("q", 2))
    fold_first(("q", 3))
    fold_second(("q", 1))
    q_third(0)
    recv("bx")
    bb[2] = bb[1] + rb[1]
    start("by")
    fold_second(("q", 2))
    fold_second(("q", 3))
    q_third(1)
    recv("by")
    bb[3] = bb[2] + rb[2]
    for k in (1, 2, 3):
        start("bz", k)
    q_third(2)
    q_third(3)

    for s in range(STEPS):
        for k in (1, 2, 3):
            recv("z3", ("f", s), k)
    for s in range(STEPS):
        more = r3f[(s + 1) % 4, 0].astype(F32)
        for k in (2, 3):
            more = more + r3f[(s + k) % 4, k - 1].astype(F32)
        gi_o[:, cols(zs[s])] += more
    for s in (1, 2, 3):
        recv("o3", s)
        gout_o[...] += r3o[s - 1].astype(F32)
    for k in (1, 2, 3):
        recv("z3", "o", k)
        go_o[...] += r3w[k - 1].astype(F32)
    for p in range(PAIRS):
        q_last(p)
    for k in (1, 2, 3):
        recv("bz", k)
    total = bb[3] + rb[3] + rb[4] + rb[5]
    device = lo * 2 + c
    narrow = pltpu.roll(total[:, 0:512], lax.rem(512 - device * 16, 512), 1)
    wide = pltpu.roll(total[:, 0:512], lax.rem(512 - lax.rem(device, 8) * 64, 512), 1)
    owner = lax.broadcasted_iota(jnp.int32, (8, 128), 0) == 4 + lax.div(device, 8)
    small_o[0:4] = narrow[0:4, 0:128]
    small_o[4:5] = jnp.sum(jnp.where(owner, wide[:, 0:128], 0.0), axis=0, keepdims=True)
    small_o[5:7] = total[0:2, 512:640]
    small_o[7:8] = jnp.zeros((1, 128), F32)

    layer_out.wait()
    tg_out.wait()
    waited = {("kv", 0), ("kv", 1)} | {("c", ("f", p)) for p in range(PAIRS)}
    for key in table:
        if key not in waited:
            (cp(*key) if isinstance(key, tuple) else cp(key)).wait_send()


def scratch():
    v = pltpu.VMEM
    return [
        v((1024, 512), BF),
        v((512, 512), BF),
        v((2, 2, 2, 64, 1664), BF),
        v((2, 2, 2, 64, 512), BF),
        v((4, 2, 2, 2, 128, 512), BF),
        v((1024, 512), F32),
        v((512, 512), BF),
        v((512, 1024), BF),
        v((512, 1024), BF),
        v((8, 1024, 512), F32),
        v((1024, 512), F32),
        v((2, 1024, 512), BF),
        v((512, 512), BF),
        v((512, 512), F32),
        v((512, 512), BF),
        v((512, 512), BF),
        v((512, 512), BF),
        v((2, 128, 512), BF),
        v((2, 2, 128, 1024), F32),
        v((4, 2, 128, 512), F32),
        v((4, 2, 2, 2, 128, 512), F32),
        v((4, 2, 2, 128, 512), F32),
        v((4, 2, 2, 64, 512), BF),
        v((4, 2, 2, 64, 512), BF),
        v((4, 2, 64, 512), BF),
        v((4, 2, 64, 512), BF),
        v((4, 3, 16, 512), BF),
        v((4, 3, 16, 512), BF),
        v((3, 64, 512), BF),
        v((3, 64, 512), BF),
        v((2, 2, 2, 64, 512), F32),
        v((2, 2, 64, 512), F32),
        v((2, 2, 32, 512), BF),
        v((2, 2, 32, 512), BF),
        v((2, 32, 512), BF),
        v((2, 32, 512), BF),
        v((3, 16, 512), BF),
        v((3, 16, 512), BF),
        v((4, 2, 2, 32, 384), BF),
        v((4, 2, 2, 32, 384), BF),
        v((4, 2, 32, 384), BF),
        v((4, 2, 32, 384), BF),
        v((4, 3, 16, 384), BF),
        v((4, 3, 16, 384), BF),
        v((128, 512), F32),
        v((4, 8, 640), F32),
        v((6, 8, 640), F32),
        v((32, 128), BF),
        pltpu.SemaphoreType.DMA((192,)),
        pltpu.SemaphoreType.DMA((192,)),
        pltpu.SemaphoreType.DMA((9,)),
    ]


def on_device(
    tokens,
    segments,
    fill_length,
    query_weight,
    key_weight,
    value_weight,
    output_weight,
    query_bias,
    value_bias,
    output_bias,
    inner_weight,
    inner_bias,
    outer_weight,
    outer_bias,
    residual_gates,
    cotangent,
):
    names = ("dp", "shard")
    several = lax.axis_size("dp") > GROUP
    place = lax.rem(lax.axis_index("dp"), GROUP) * 2 + lax.axis_index("shard")

    def block_of(shard):
        if not several:
            return shard
        whole = lax.all_gather(shard, names, axis=0, tiled=True)
        rows = whole.shape[0] // (2 * GROUP)
        return lax.dynamic_slice_in_dim(whole, place * rows, rows, 0)

    def owned(block):
        if not several:
            return block
        rows = block.shape[0]
        whole = jnp.zeros((rows * 2 * GROUP, *block.shape[1:]), F32)
        whole = lax.dynamic_update_slice_in_dim(whole, block, place * rows, 0)
        return lax.psum_scatter(whole, names, scatter_dimension=0, tiled=True)

    query_weight, key_weight, value_weight, output_weight, inner_weight, outer_weight = map(
        block_of, (query_weight, key_weight, value_weight, output_weight, inner_weight, outer_weight)
    )
    query_bias, value_bias, output_bias, inner_bias, outer_bias = map(
        block_of, (query_bias, value_bias, output_bias, inner_bias, outer_bias)
    )
    pieces = []
    for p in range(PAIRS):
        for weight in (query_weight, key_weight, value_weight):
            pieces.append(weight[:, p * 128 : p * 128 + 128])
    bias = jnp.concatenate([query_bias, value_bias, output_bias, outer_bias, inner_bias])[None, :]
    pieces.append(jnp.pad(bias, ((0, 15), (0, 0))))
    wcat = jnp.concatenate(pieces, axis=1)
    vmem = pl.BlockSpec(memory_space=pltpu.VMEM)
    smem = pl.BlockSpec(memory_space=pltpu.SMEM)
    hbm = pl.BlockSpec(memory_space=pl.ANY)
    shape = jax.ShapeDtypeStruct
    outs = pl.pallas_call(
        layer_kernel,
        out_shape=[
            shape((512, 512), BF),
            shape((512, 512), F32),
            shape((16, 512), F32),
            shape((16, 512), F32),
            shape((16, 512), F32),
            shape((16, 512), F32),
            shape((16, 2048), F32),
            shape((64, 512), F32),
            shape((8, 128), F32),
        ],
        in_specs=[hbm, hbm, vmem, smem, smem, hbm, hbm, hbm, hbm],
        out_specs=[hbm, hbm] + [vmem] * 7,
        scratch_shapes=scratch(),
        compiler_params=pltpu.CompilerParams(
            collective_id=0, has_side_effects=True, vmem_limit_bytes=64 * 2**20 - 2**17
        ),
    )(
        tokens.reshape(512, 512),
        cotangent.reshape(512, 512),
        segments,
        fill_length,
        residual_gates,
        wcat,
        output_weight,
        inner_weight,
        outer_weight,
    )
    layer, token_grads, gq, gk, gv, go, gi, gout, small = outs
    gate_sums = small[5:7, 0]
    if several:
        gate_sums = lax.psum(jnp.where(place == 0, gate_sums, 0.0), names)
    grads = (
        gq,
        gk,
        gv,
        go,
        small[0, 0:16],
        small[1, 0:16],
        small[2, 0:16],
        gi,
        small[4, 0:64],
        gout,
        small[3, 0:16],
    )
    return (layer[None], token_grads[None], *map(owned, grads), gate_sums)


def solution(mesh):
    spread = P(("dp", "shard"))
    return jax.shard_map(
        on_device,
        mesh=mesh,
        in_specs=(
            P("dp", "shard", None),
            P("dp", None),
            P("dp"),
            *([P(("dp", "shard"), None)] * 4),
            *([spread] * 3),
            P(("dp", "shard"), None),
            spread,
            P(("dp", "shard"), None),
            spread,
            P(),
            P("dp", "shard", None),
        ),
        out_specs=(
            P("dp", "shard", None),
            P("dp", "shard", None),
            *([P(("dp", "shard"), None)] * 4),
            *([spread] * 3),
            P(("dp", "shard"), None),
            spread,
            P(("dp", "shard"), None),
            spread,
            P(),
        ),
        check_vma=False,
    )
```

```python
import jax
import jax.numpy as jnp
from jax import lax
from jax.experimental import pallas as pl
from jax.experimental.pallas import tpu as pltpu
from jax.sharding import PartitionSpec as P

MESH = pl.DeviceIdType.MESH
BF = jnp.bfloat16
F32 = jnp.float32
HEADS = 8
GROUP = 16
PAIRS = 4
VMEM_BYTES = 64 * 2**20 - 2**17
PLAN = {
    "start": ("1q0", "zq2", "1q1", "zq3", "1q2", "zf0", "2q0", "3q0", "1q3", "zf1", "2q1",),
    "fwd0": ("2q2", "1f0", "zf2",),
    "fwd1": ("2q3",),
    "proj1": ("3q1", "3q2", "1f1", "zf3", "2f0",),
    "fwd2": ("3q3",),
    "proj2": ("1f2",),
    "fwd5": ("2f1",),
    "proj3": ("3f0", "1f3",),
    "outproj": ("2f2",),
    "ffn0": ("3f1",),
    "ffn1": ("2f3",),
    "ffn2": ("3f2", "3f3", "FF0",),
    "ffn3": ("FF1",),
    "pre": ("SF0",),
    "bwd0": ("FF2",),
    "bwd1": ("SF1",),
    "bwd2": ("TF0", "FF3",),
    "bwd3": ("FO", "SF2",),
    "fin0": ("TF1",),
    "bwd5": ("SF3", "FQ0",),
    "fin1": ("SO", "TF2",),
    "bwd6": ("TF3",),
    "bwd7": ("TO", "SQ0", "FQ1",),
    "prod7": ("TQ0", "SQ1",),
    "fin3": ("TQ1", "FQ2",),
    "last1": ("TQ2",),
}
STEPS = 4


def dot(left, right, left_dim, right_dim):
    return lax.dot_general(
        left, right, (((left_dim,), (right_dim,)), ((), ())), preferred_element_type=F32
    )


def gelu_parts(hidden):
    size = jnp.abs(hidden) * 0.7071067811865476
    recip = 1.0 / (1.0 + 0.3275911 * size)
    expo = jnp.exp(-size * size)
    poly = recip * (
        0.127414796
        + recip * (-0.142248368 + recip * (0.7107068705 + recip * (-0.7265760135 + recip * 0.5307027145)))
    )
    tail = poly * expo
    cdf = jnp.where(hidden >= 0, 1.0 - tail, tail)
    return hidden * cdf, cdf + hidden * expo * 0.3989422804014327


def by_chip(value):
    width = value.shape[-1]
    return value.reshape(4, 8, 16, width).transpose(1, 0, 2, 3).reshape(2, 2, 2, 64, width)


def col_sums(value):
    return dot(jnp.ones((8, value.shape[0]), BF), value, 1, 0)


def layer_kernel(
    tok,
    cot,
    seg,
    fill,
    gates,
    bias_q,
    bias_v,
    bias_o,
    bias_out,
    bias_in,
    wquery,
    wkey,
    wvalue,
    wout_proj,
    win,
    wout,
    layer_o,
    tg_o,
    gq_o,
    gk_o,
    gv_o,
    go_o,
    gi_o,
    gout_o,
    small_o,
    xrow,
    cotv,
    wq_rest,
    wq_last,
    wf,
    qt,
    kt,
    vt,
    probs,
    scales,
    st,
    pb,
    mixt,
    attn,
    rlow,
    ffn,
    gres,
    gffn,
    gmixt,
    dqt,
    dkv,
    rkv,
    gf,
    rcf,
    s1f,
    r1f,
    s2f,
    r2f,
    s3f,
    r3f,
    s3o,
    r3o,
    go,
    rco,
    s1o,
    r1o,
    s2o,
    r2o,
    s3w,
    r3w,
    s1q,
    r1q,
    s2q,
    r2q,
    s3q,
    r3q,
    glast,
    rclast,
    s1d,
    r1d,
    ksum,
    bb,
    rb,
    biasb,
    send_sem,
    recv_sem,
    local_sem,
):
    hid, gac = st.at[pl.ds(0, 512)], st.at[pl.ds(512, 512)]
    act, ghid = pb.at[pl.ds(0, 512)], pb.at[pl.ds(512, 512)]
    wq = [wq_rest.at[p] for p in range(PAIRS - 1)] + [wq_last]

    dp = lax.axis_index("dp")
    c = lax.axis_index("shard")
    lo = lax.rem(dp, GROUP)
    z = lax.div(lo, 4)
    y = lax.rem(lax.div(lo, 2), 2)
    x = lax.rem(lo, 2)
    cc, xx, yy = 1 - c, 1 - x, 1 - y

    def zk(k):
        return lax.rem(z + (k % 4), 4)

    zs = [zk(k) for k in range(4)]
    XP = (dp + 1 - 2 * x, c)
    YP = (dp + 2 - 4 * y, c)
    ZP = [None] + [(dp + 4 * (zs[k] - z), c) for k in (1, 2, 3)]
    DP = (dp + 3 - 2 * x - 4 * y, c)
    SB = (dp, cc)

    def rows(place):
        return pl.ds(pl.multiple_of(place * 16, 16), 16)

    def cols(place):
        return pl.ds(pl.multiple_of(place * 512, 512), 512)

    table = {}
    ids = {}

    def same(ref, dev):
        return (ref, ref, dev)

    for p in range(PAIRS):
        for k in (1, 2, 3):
            table["z", ("q", p), k] = lambda p=p, k=k: (
                wq[p].at[y, x, c, pl.ds(0, 16)],
                wq[p].at[y, x, c, pl.ds(k * 16, 16)],
                ZP[k],
            )
        for name, dev in (("x", XP), ("y", YP), ("d", DP)):
            if p == 0 or name != "d":
                for part, (low, count) in enumerate(((0, 16), (16, 48))):
                    table[name, ("q", p), part] = lambda p=p, low=low, count=count, dev=dev: same(
                        wq[p].at[y, x, c, pl.ds(low, count)], dev
                    )
        table["s", ("q", p), 0] = lambda p=p: same(wq[p].at[y, :, c], SB)
        table["s", ("q", p), 1] = lambda p=p: same(wq[p].at[yy, :, c], SB)
        if p:
            table["rx", ("q", p)] = lambda p=p: same(wq[p].at[y, xx, c, pl.ds(0, 32)], YP)
            table["ry", ("q", p)] = lambda p=p: same(wq[p].at[yy, x, c, pl.ds(32, 32)], XP)
    for s in range(STEPS):
        for k in (1, 2, 3):
            table["z", ("f", s), k] = lambda s=s, k=k: (
                win.at[:, cols(zs[(k + s) % 4])],
                wf.at[s, y, x, c, pl.ds(64 + k * 16, 16)],
                ZP[k],
            )
        if s:
            table["zo", ("f", s)] = lambda s=s: (wout, wf.at[s, y, x, c, pl.ds(16, 64)], ZP[4 - s])
        split = 16 if s else 80
        for name, dev in (("x", XP), ("y", YP)):
            for part, (low, count) in enumerate(((0, split), (split, 128 - split))):
                table[name, ("f", s), part] = lambda s=s, low=low, count=count, dev=dev: same(
                    wf.at[s, y, x, c, pl.ds(low, count)], dev
                )
        table["rx", ("f", s)] = lambda s=s: same(wf.at[s, y, xx, c, pl.ds(0, 64)], YP)
        table["ry", ("f", s)] = lambda s=s: same(wf.at[s, yy, x, c, pl.ds(64, 64)], XP)
        table["s", ("f", s), 0] = lambda s=s: same(wf.at[s, y, :, c], SB)
        table["s", ("f", s), 1] = lambda s=s: same(wf.at[s, yy, :, c], SB)
    table["tok"] = lambda: (xrow.at[pl.ds(0, 512)], xrow.at[pl.ds(512, 512)], SB)
    groups = {}
    LAST = (("q", PAIRS - 2), ("q", PAIRS - 1))
    for s in range(STEPS):
        groups["f", s] = (gf.at[s], rcf.at[s], s1f.at[s], r1f.at[s], s2f.at[s], r2f.at[s], s3f.at[s], r3f.at[s])
        if s:
            table["o3", s] = lambda s=s: (s3o.at[s - 1], r3o.at[s - 1], ZP[s])
    groups["o"] = (go, rco, s1o, r1o, s2o, r2o, s3w, r3w)
    for p in range(PAIRS):
        if p < PAIRS - 1:
            gq = gf.at[p, :, :, :, pl.ds(0, 64), pl.ds(0, 384)]
            rcq = rcf.at[p, :, :, pl.ds(0, 64), pl.ds(0, 384)]
        else:
            gq, rcq = glast, rclast
        groups["q", p] = (gq, rcq, s1q.at[p], r1q.at[p], s2q.at[p], r2q.at[p], s3q.at[p], r3q.at[p])
        if p < PAIRS - 1:
            table["kv", p] = lambda p=p: (dkv.at[p % 2, :, :, pl.ds(512, 512)], rkv.at[p % 2], SB)
        else:
            for j in range(2):
                table["kv", p, j] = lambda p=p, j=j: (
                    dkv.at[p % 2, :, pl.ds(j * 64, 64), pl.ds(512, 512)],
                    rkv.at[p % 2, :, pl.ds(j * 64, 64)],
                    SB,
                )
    for g, (grad, rc, s1, r1, s2, r2, s3, r3) in groups.items():
        table["c", g] = lambda grad=grad, rc=rc: (grad.at[:, :, cc], rc, SB)
        if g in LAST:
            for i, dev in enumerate((XP, YP, DP)):
                table["d1", g, i] = lambda i=i, dev=dev, at=LAST.index(g): (s1d.at[at, i], r1d.at[at, i], dev)
            for k in (1, 2, 3):
                table["z3", g, k] = lambda s3=s3, r3=r3, k=k: (s3.at[k - 1], r3.at[k - 1], ZP[k])
            continue
        table["a1", g] = lambda s1=s1, r1=r1: (s1.at[0], r1.at[0], XP)
        table["b1", g] = lambda s1=s1, r1=r1: (s1.at[1], r1.at[1], YP)
        table["a2", g] = lambda s2=s2, r2=r2: (s2.at[0], r2.at[0], YP)
        table["b2", g] = lambda s2=s2, r2=r2: (s2.at[1], r2.at[1], XP)
        for k in (1, 2, 3):
            table["z3", g, k] = lambda s3=s3, r3=r3, k=k: (s3.at[k - 1], r3.at[k - 1], ZP[k])
    table["bc"] = lambda: (bb.at[0], rb.at[0], SB)
    for i, dev in enumerate((XP, YP, DP)):
        table["bp", i] = lambda i=i, dev=dev: (bb.at[1], rb.at[1 + i], dev)
    for k in (1, 2, 3):
        table["bz", k] = lambda k=k: (bb.at[2], rb.at[3 + k], ZP[k])
    for place, key in enumerate(table):
        ids[key] = place

    def cp(*key):
        key = key if len(key) > 1 else key[0]
        src, dst, dev = table[key]()
        place = ids[key]
        return pltpu.make_async_remote_copy(
            src_ref=src,
            dst_ref=dst,
            send_sem=send_sem.at[place],
            recv_sem=recv_sem.at[place],
            device_id=dev,
            device_id_type=MESH,
        )

    def natural(ref, firsts, columns):
        parts = [
            ref[:, :, :, pl.ds(pl.multiple_of(firsts(lax.rem(z + 4 - other, 4)), 16), 16), columns]
            for other in range(4)
        ]
        return jnp.concatenate([part.reshape(128, part.shape[-1]) for part in parts], axis=0)

    def attention_block(k):
        return k * 16

    def inner_block(k):
        return jnp.where(k == 0, 0, k * 16 + 64)

    def start(*key):
        cp(*key).start()

    def recv(*key):
        cp(*key).wait_recv()

    local = (
        [(tok, xrow.at[pl.ds(0, 512)]), (cot, cotv), (wout, wf.at[0, y, x, c, pl.ds(16, 64)])]
        + [(win.at[:, cols(zs[s])], wf.at[s, y, x, c, pl.ds(0, 16)]) for s in range(STEPS)]
        + [
            (
                ref.at[:, pl.ds(p * 128, 128)],
                (wq[p] if i < 3 or p else wq_last).at[
                    y, x, c, pl.ds(0, 16), pl.ds(i * 128 if i < 3 or p else 512, 128)
                ],
            )
            for p in range(PAIRS)
            for i, ref in enumerate((wquery, wkey, wvalue, wout_proj))
        ]
    )
    local = [pltpu.make_async_copy(src, dst, local_sem.at[i]) for i, (src, dst) in enumerate(local)]
    for one in local[7:] + local[:7]:
        one.start()
    barrier = pltpu.get_barrier_semaphore()
    peers = (XP, YP, DP, ZP[1], ZP[2], ZP[3], SB)
    for dev in peers:
        pl.semaphore_signal(barrier, inc=1, device_id=dev, device_id_type=MESH)

    own_bias = jnp.zeros((16, 128), F32)
    for offset, ref in ((0, bias_q), (16, bias_v), (32, bias_o), (48, bias_out), (64, bias_in)):
        count = ref.shape[0]
        row = jnp.broadcast_to(ref[...].astype(F32).reshape(1, count), (16, count))
        row = jnp.where(lax.broadcasted_iota(jnp.int32, (16, count), 0) == 0, row, 0.0).astype(BF)
        spot = lax.broadcasted_iota(jnp.int32, (count, 128), 0) + offset
        spread = lax.broadcasted_iota(jnp.int32, (count, 128), 1) == spot
        own_bias = own_bias + dot(row, spread.astype(F32).astype(BF), 1, 0)
    wq[0][y, x, c, pl.ds(0, 16), pl.ds(384, 128)] = own_bias.astype(BF)
    for one in local[7:]:
        one.wait()
    pl.semaphore_wait(barrier, len(peers))

    def send_z(g):
        for k in (1, 2, 3):
            start("z", g, k)
        if g[0] == "f" and g[1]:
            start("zo", g)

    def neighbours(g):
        return ("x", "y", "d") if g == ("q", 0) else ("x", "y")

    def send_early(g):
        for name in neighbours(g):
            start(name, g, 0)

    def send_plane(g):
        for k in (1, 2, 3):
            recv("z", g, k)
        if g[0] == "f" and g[1]:
            recv("zo", g)
        for name in neighbours(g):
            start(name, g, 1)

    def send_relay(g):
        for name in ("x", "y"):
            recv(name, g, 0)
            recv(name, g, 1)
            if g != ("q", 0):
                start("r" + name, g)
            if name == "x":
                start("s", g, 0)

    def send_across(g):
        if g == ("q", 0):
            recv("d", g, 0)
            recv("d", g, 1)
        else:
            recv("rx", g)
            recv("ry", g)
        start("s", g, 1)

    def all_here(g):
        recv("s", g, 0)
        recv("s", g, 1)

    Q, F = [("q", p) for p in range(PAIRS)], [("f", s) for s in range(STEPS)]
    send_z(Q[0])
    send_early(Q[0])
    local[0].wait()
    start("tok")
    send_z(Q[1])
    for p in (1, 2, 3):
        send_early(Q[p])
    for one in local[2:7]:
        one.wait()
    for s in range(STEPS):
        send_early(F[s])

    kind = lax.broadcasted_iota(jnp.int32, (16, 512), 0)
    at_own = lax.broadcasted_iota(jnp.int32, (16, 512), 1) + c * 512
    at_sib = lax.broadcasted_iota(jnp.int32, (16, 512), 1) + cc * 512
    own_seg = seg[:, pl.ds(pl.multiple_of(c * 512, 512), 512)]
    sib_seg = seg[:, pl.ds(pl.multiple_of(cc * 512, 512), 512)]
    used = fill[0]
    for half, (segs, spot) in enumerate(((own_seg, at_own), (sib_seg, at_sib))):
        unused = jnp.where(spot >= used, 1.0, 0.0)
        marks = jnp.where(kind == 8, unused, jnp.where(kind == segs, 1.0, 0.0)).astype(BF)
        for head in range(HEADS):
            kt[head, 64:80, half * 512 : half * 512 + 512] = marks
    barred = jnp.where((kind == own_seg) | (kind > 8), 0.0, -1e30).astype(BF)
    for head in range(HEADS):
        qt[head, 64:80] = barred

    gate_attn = gates[0]
    gate_feed = gates[1]
    local[1].wait()
    upstream = cotv[...].astype(F32)
    gffn[...] = (gate_feed * upstream).astype(BF)

    def take(name):
        kind, g = name[0], ({"q": "q", "f": "f", "Q": "q", "F": "f"}.get(name[1]), int(name[2:] or 0))
        if name[1] == "O":
            g = "o"
        if name in done:
            raise ValueError(name)
        done.append(name)
        if kind == "z":
            send_z(g)
        elif kind == "1":
            send_plane(g)
        elif kind == "2":
            send_relay(g)
        elif kind == "3":
            send_across(g)
        elif kind == "F":
            fold_plane(g) if g in LAST else fold_first(g)
        elif kind == "S":
            fold_second(g)
        elif g in LAST:
            fold_column(g)
        elif g == "o":
            fold_third(g)
            go_o[...] = ksum[rows(z), :]
        elif g[0] == "f":
            ffn_third(g[1])
        else:
            q_third(g[1])

    done = []

    def at_point(name):
        for one in PLAN.get(name, ()):
            take(one)

    at_point("start")
    recv("tok")
    all_here(Q[0])

    held = natural(wq[0], attention_block, slice(384, 512)).reshape(32, 16, 128)
    biasb[...] = jnp.sum(held.astype(F32), axis=1).astype(BF)

    def bias_row(offset, per, width):
        lane = lax.broadcasted_iota(jnp.int32, (128, width), 0)
        at = lax.broadcasted_iota(jnp.int32, (128, width), 1)
        pick = (lane == offset + (at & (per - 1))).astype(F32).astype(BF)
        spread = dot(biasb[...], pick, 1, 0)
        owner = lax.broadcasted_iota(jnp.int32, (32, width), 0)
        at = lax.broadcasted_iota(jnp.int32, (32, width), 1)
        return jnp.sum(jnp.where(owner == lax.shift_right_logical(at, per.bit_length() - 1), spread, 0.0), axis=0, keepdims=True)

    first_row = lax.broadcasted_iota(jnp.int32, (16, 512), 0) == 0
    ones_row = jnp.where(first_row, 1.0, 0.0).astype(BF)

    def as_rank_one(row):
        return jnp.where(first_row, jnp.broadcast_to(row, (16, 512)), 0.0).astype(BF)

    bias_q = as_rank_one(bias_row(0, 16, 512))
    bias_v = as_rank_one(bias_row(16, 16, 512))

    def project(p):
        weights = natural(wq[p], attention_block, slice(0, 384))
        ours = dot(weights, xrow[0:512], 0, 1)
        theirs = dot(weights[:, 128:384], xrow[512:1024], 0, 1)
        at = slice(p * 128, p * 128 + 128)
        grown = ours[0:128] + dot(bias_q[:, at], ones_row, 0, 0)
        grown = (grown.astype(BF).astype(F32) * 0.125).astype(BF)
        add_v = dot(bias_v[:, at], ones_row, 0, 0)
        for j in range(2):
            part = slice(j * 64, j * 64 + 64)
            qt[p * 2 + j, 0:64] = grown[part]
            kt[p * 2 + j, 0:64, 0:512] = ours[128 + j * 64 : 192 + j * 64].astype(BF)
            kt[p * 2 + j, 0:64, 512:1024] = theirs[part].astype(BF)
        vt[at, 0:512] = (ours[256:384] + add_v).astype(BF)
        vt[at, 512:1024] = (theirs[128:256] + add_v).astype(BF)

    def half_of(unit):
        return unit // 2, slice(unit % 2 * 256, unit % 2 * 256 + 256)

    def scores_of(unit):
        head, lanes = half_of(unit)
        raw = dot(kt[head], qt[head, :, lanes], 0, 0)
        own = kt[head, 0:64, lanes].astype(F32) * qt[head, 0:64, lanes].astype(F32)
        own = jnp.sum(own, axis=0, keepdims=True)
        highest = jnp.full((8, 256), -jnp.inf, F32)
        for b in range(8):
            r = slice(b * 128, b * 128 + 128)
            block = raw[r]
            if b // 2 == unit % 2 and b < 4:
                diagonal = lax.broadcasted_iota(jnp.int32, (128, 256), 1) == (
                    lax.broadcasted_iota(jnp.int32, (128, 256), 0) + b % 2 * 128
                )
                block = jnp.where(diagonal, own, block)
            st[r, lanes] = block
            highest = jnp.maximum(highest, jnp.max(block.reshape(16, 8, 256), axis=0))
        return jnp.max(highest, axis=0, keepdims=True)

    def attend(unit, highest):
        head, lanes = half_of(unit)
        total = jnp.zeros((8, 256), F32)
        for b in range(8):
            r = slice(b * 128, b * 128 + 128)
            expo = jnp.exp(st[r, lanes] - highest)
            probs[head, r, lanes] = expo
            total = total + jnp.sum(expo.reshape(16, 8, 256), axis=0)
        scale = 1.0 / jnp.sum(total, axis=0, keepdims=True)
        scales[head, :, lanes] = jnp.broadcast_to(scale, (8, 256))
        for b in range(8):
            r = slice(b * 128, b * 128 + 128)
            pb[r, lanes] = (probs[head, r, lanes] * scale).astype(BF)
        at = slice(head * 64, head * 64 + 64)
        mixt[at, lanes] = dot(vt[at], pb[:, lanes], 1, 0).astype(BF)

    for head in range(HEADS):
        first = head * 2
        if head % 2 == 0:
            if head:
                at_point("proj%d" % (head // 2))
                all_here(Q[head // 2])
            project(head // 2)
        at_point("fwd%d" % head)
        if head % 2 == 0:
            highest = scores_of(first)
        later = scores_of(first + 1)
        attend(first, highest)
        if head % 2 == 0:
            highest = scores_of(first + 2)
        attend(first + 1, later)

    at_point("outproj")
    out_weight = jnp.concatenate(
        [natural(wq_last, attention_block, slice(512, 640))] + [natural(wq[p], attention_block, slice(384, 512)) for p in (1, 2, 3)], axis=1
    )
    attn[...] = dot(mixt[...], out_weight, 0, 0) + bias_row(32, 16, 512)
    resid = xrow[0:512].astype(F32) + gate_attn * attn[...]
    rlow[...] = resid.astype(BF)
    ffn[...] = jnp.zeros((512, 512), F32)
    gres[...] = cotv[...].astype(F32)

    def fold_first(g):
        grad, rc, s1 = groups[g][:3]
        half = rc.shape[2] // 2
        recv("c", g)
        for i in range(2):
            s1[0, i] = (grad[i, xx, c, 0:half] + rc[i, xx, 0:half]).astype(BF)
            s1[1, i] = (grad[yy, i, c, half : 2 * half] + rc[yy, i, half : 2 * half]).astype(BF)
        start("a1", g)
        start("b1", g)

    def fold_second(g):
        grad, rc, s1, r1, s2, r2 = groups[g][:6]
        half = rc.shape[2] // 2
        recv("a1", g)
        s2[0] = (grad[yy, x, c, 0:half] + rc[yy, x, 0:half] + r1[0, yy].astype(F32)).astype(BF)
        start("a2", g)
        recv("b1", g)
        s2[1] = (
            grad[y, xx, c, half : 2 * half] + rc[y, xx, half : 2 * half] + r1[1, xx].astype(F32)
        ).astype(BF)
        start("b2", g)

    def fold_third(g):
        grad, rc, s1, r1, s2, r2, s3, r3 = groups[g]
        half = rc.shape[2] // 2
        width = rc.shape[3]
        recv("a2", g)
        upper = grad[y, x, c, 0:half] + rc[y, x, 0:half] + r1[0, y].astype(F32) + r2[0].astype(F32)
        ksum[0:half, 0:width] = upper
        recv("b2", g)
        lower = (
            grad[y, x, c, half : 2 * half]
            + rc[y, x, half : 2 * half]
            + r1[1, x].astype(F32)
            + r2[1].astype(F32)
        )
        ksum[half : 2 * half, 0:width] = lower
        for k in (1, 2, 3):
            s3[k - 1] = ksum[rows(zs[k]), 0:width].astype(BF)
            start("z3", g, k)

    def ffn_third(s):
        fold_third(("f", s))
        gi_o[:, cols(zs[s])] = ksum[rows(z), :]
        if s:
            s3o[s - 1] = ksum[64:128].astype(BF)
            start("o3", s)
        else:
            gout_o[...] = ksum[64:128]

    def small(row, value):
        bb[0, row : row + 1, 0:512] = value

    bb[0, :, 512:640] = jnp.zeros((8, 128), F32)

    def ffn_step(s):
        all_here(F[s])
        inner = natural(wf.at[s], inner_block, slice(0, 512))
        outer = wf[s, :, :, :, 16:80].reshape(512, 512)
        hid[...] = dot(rlow[...], inner, 1, 0) + chunk_bias[s]
        gac[...] = dot(gffn[...], outer, 1, 1)
        for b in range(8):
            r = slice(b * 64, b * 64 + 64)
            value, slope = gelu_parts(hid[r])
            act[r] = value.astype(BF)
            ghid[r] = (gac[r] * slope).astype(BF)
        ffn[...] += dot(act[...], outer, 1, 0)
        gf[s, :, :, :, 64:128] = dot(act[...], gffn[...], 0, 0).reshape(2, 2, 2, 64, 512)
        gf[s, :, :, :, 0:64] = by_chip(dot(rlow[...], ghid[...], 0, 0))
        start("c", ("f", s))
        gres[...] += dot(ghid[...], inner, 1, 1)
        sums = col_sums(ghid[...])[0:1]
        for row in range(4):
            bb[0, 4 + row : 5 + row, 0:512] = jnp.where(
                zs[s] == row, sums, bb[0, 4 + row : 5 + row, 0:512]
            )

    inner_bias = bias_row(64, 64, 2048)
    parts = [inner_bias[:, i * 512 : i * 512 + 512] for i in range(4)]
    chunk_bias = []
    for s in range(STEPS):
        picked = parts[3]
        for i in range(3):
            picked = jnp.where(zs[s] == i, parts[i], picked)
        chunk_bias.append(picked)
    for row in range(4):
        small(4 + row, jnp.zeros((1, 512), F32))

    for s in range(STEPS):
        at_point("ffn%d" % s)
        ffn_step(s)
    at_point("pre")

    waited = set()
    for key in table:
        if key[0] in ("x", "y", "rx", "ry", "s") and key[1][0] == "f":
            cp(*key).wait_send()
            waited.add(key)

    small(3, col_sums(gffn[...])[0:1])
    gattn = (gate_attn * gres[...]).astype(BF)
    small(2, col_sums(gattn)[0:1])
    go[...] = by_chip(dot(mixt[...], gattn, 1, 0))
    start("c", "o")
    gmixt[...] = dot(out_weight, gattn, 1, 1).astype(BF)
    def finish_layer():
        ffn[...] += bias_row(48, 16, 512)
        upstream = cotv[...].astype(F32)
        resid = xrow[0:512].astype(F32) + gate_attn * attn[...]
        rlow[...] = (resid + gate_feed * ffn[...]).astype(BF)
        layer_out = pltpu.make_async_copy(rlow, layer_o, local_sem.at[0])
        layer_out.start()
        feed_part = jnp.sum(jnp.sum(upstream * ffn[...], axis=0, keepdims=True), axis=1, keepdims=True)
        bb[0, 1:2, 512:640] = jnp.broadcast_to(feed_part, (1, 128))
        attn_part = jnp.sum(jnp.sum(gres[...] * attn[...], axis=0, keepdims=True), axis=1, keepdims=True)
        bb[0, 0:1, 512:640] = jnp.broadcast_to(attn_part, (1, 128))
        return layer_out


    def scores_back(unit):
        head, lanes = half_of(unit)
        at = slice(head * 64, head * 64 + 64)
        raw = dot(vt[at], gmixt[at, lanes], 0, 0)
        total = jnp.zeros((8, 256), F32)
        for b in range(8):
            r = slice(b * 128, b * 128 + 128)
            block = raw[r]
            st[r, lanes] = block
            total = total + jnp.sum((probs[head, r, lanes] * block).reshape(16, 8, 256), axis=0)
        return jnp.sum(total, axis=0, keepdims=True) * scales[head, 0:1, lanes]

    def slopes_of(unit, inner):
        head, lanes = half_of(unit)
        scale = scales[head, 0:1, lanes]
        slot = head % 2 * 2
        for b in range(8):
            r = slice(b * 128, b * 128 + 128)
            prob = probs[head, r, lanes] * scale
            place = (b // 4, b // 2 % 2, b % 2, slice(None), lanes)
            wf[(slot, *place)] = prob.astype(BF)
            wf[(slot + 1, *place)] = (prob * (st[r, lanes] - inner)).astype(BF)

    def products_of(head):
        at = slice(head * 64, head * 64 + 64)
        slot = head % 2 * 2
        prob, slope = (wf[i].reshape(1024, 512) for i in (slot, slot + 1))
        place = (head // 2 % 2, slice(None), slice(head % 2 * 64, head % 2 * 64 + 64))
        dkv[place[0], 0, place[2]] = dot(qt[head, 0:64], slope, 1, 1)
        dkv[place[0], 1, place[2]] = dot(gmixt[at], prob, 1, 1)
        if head >= 6:
            assert "FQ1" in done
            start("kv", 3, head - 6)
        dqt[at] = (dot(kt[head, 0:64], slope, 1, 0) * 0.125).astype(BF)

    def finish_pair(p):
        slot = p % 2
        at = slice(p * 128, p * 128 + 128)
        if p < PAIRS - 1:
            recv("kv", p)
        else:
            recv("kv", p, 0)
            recv("kv", p, 1)
        vt[at, 0:512] = (dkv[slot, 0, :, 0:512] + rkv[slot, 0]).astype(BF)
        vt[at, 512:1024] = (dkv[slot, 1, :, 0:512] + rkv[slot, 1]).astype(BF)
        both = jnp.concatenate([dqt[at], vt[at, 0:512], vt[at, 512:1024]], axis=0)
        if p < PAIRS - 1:
            cp("c", F[p]).wait_send()
            gf[p, :, :, :, 0:64, 0:384] = by_chip(dot(xrow[0:512], both, 0, 1))
        else:
            glast[...] = by_chip(dot(xrow[0:512], both, 0, 1))
        start("c", Q[p])
        sums = dot(jnp.ones((8, 512), BF), both, 1, 1)
        bb[0, 0:1, at] = sums[0:1, 0:128]
        bb[0, 1:2, at] = sums[0:1, 256:384]

    def token_part(p):
        at = slice(p * 128, p * 128 + 128)
        both = jnp.concatenate([dqt[at], vt[at, 0:512], vt[at, 512:1024]], axis=0)
        gres[...] += dot(both, natural(wq[p], attention_block, slice(0, 384)), 0, 1)

    def fold_plane(g):
        grad, rc = groups[g][:2]
        recv("c", g)
        for i, (yi, xi) in enumerate(((y, xx), (yy, x), (yy, xx))):
            s1d[LAST.index(g), i] = (grad[yi, xi, c] + rc[yi, xi]).astype(BF)
            start("d1", g, i)

    def fold_column(g):
        grad, rc, s3 = groups[g][0], groups[g][1], groups[g][6]
        for i in range(3):
            recv("d1", g, i)
        come = r1d.at[LAST.index(g)]
        ksum[0:64, 0:384] = (
            grad[y, x, c] + rc[y, x] + (come[0].astype(F32) + come[1].astype(F32) + come[2].astype(F32))
        )
        for k in (1, 2, 3):
            s3[k - 1] = ksum[rows(zs[k]), 0:384].astype(BF)
            start("z3", g, k)
        keep_pair(g[1])

    def q_third(p):
        fold_third(Q[p])
        keep_pair(p)

    def keep_pair(p):
        at = slice(p * 128, p * 128 + 128)
        gq_o[:, at] = ksum[rows(z), 0:128]
        gk_o[:, at] = ksum[rows(z), 128:256]
        gv_o[:, at] = ksum[rows(z), 256:384]

    inner = scores_back(0)
    for head in range(HEADS):
        at_point("bwd%d" % head)
        if head in (5, 7):
            cp("kv", (head - 5) // 2).wait_send()
        if head:
            products_of(head - 1)
        if head in (2, 4, 6):
            p = head // 2 - 1
            assert "TF%d" % p in done and (p < 2 or "FQ%d" % (p - 2) in done)
            start("kv", p)
        later = scores_back(head * 2 + 1)
        slopes_of(head * 2, inner)
        if head < HEADS - 1:
            inner = scores_back(head * 2 + 2)
        slopes_of(head * 2 + 1, later)
        if head in (3, 5, 7):
            p = head // 2 - 1
            at_point("fin%d" % p)
            finish_pair(p)
    at_point("prod7")
    products_of(HEADS - 1)
    at_point("layer")
    layer_out = finish_layer()
    at_point("fin3")
    finish_pair(3)

    start("bc")
    at_point("tok3")
    fold_plane(Q[3])
    recv("bc")
    bb[1] = bb[0] + rb[0]
    for i in range(3):
        start("bp", i)
    at_point("tok")
    for p in range(PAIRS):
        token_part(p)
    tg_out = pltpu.make_async_copy(gres, tg_o, local_sem.at[1])
    tg_out.start()

    def q_last(p):
        at = slice(p * 128, p * 128 + 128)
        for k in (1, 2, 3):
            recv("z3", ("q", p), k)
        more = r3q[p, 0].astype(F32) + r3q[p, 1].astype(F32) + r3q[p, 2].astype(F32)
        gq_o[:, at] += more[:, 0:128]
        gk_o[:, at] += more[:, 128:256]
        gv_o[:, at] += more[:, 256:384]

    at_point("last1")
    fold_column(Q[3])
    at_point("last2")
    for i in range(3):
        recv("bp", i)
    bb[2] = bb[1] + (rb[1] + rb[2] + rb[3])
    for k in (1, 2, 3):
        start("bz", k)
    assert len(done) == 53

    for s in range(STEPS):
        for k in (1, 2, 3):
            recv("z3", ("f", s), k)
    for s in range(STEPS):
        more = r3f[(s + 1) % 4, 0].astype(F32)
        for k in (2, 3):
            more = more + r3f[(s + k) % 4, k - 1].astype(F32)
        gi_o[:, cols(zs[s])] += more
    for s in (1, 2, 3):
        recv("o3", s)
        gout_o[...] += r3o[s - 1].astype(F32)
    for k in (1, 2, 3):
        recv("z3", "o", k)
        go_o[...] += r3w[k - 1].astype(F32)
    for p in range(PAIRS):
        q_last(p)
    for k in (1, 2, 3):
        recv("bz", k)
    total = bb[2] + rb[4] + rb[5] + rb[6]
    device = lo * 2 + c
    narrow = pltpu.roll(total[:, 0:512], lax.rem(512 - device * 16, 512), 1)
    wide = pltpu.roll(total[:, 0:512], lax.rem(512 - lax.rem(device, 8) * 64, 512), 1)
    owner = lax.broadcasted_iota(jnp.int32, (8, 128), 0) == 4 + lax.div(device, 8)
    small_o[0:4] = narrow[0:4, 0:128]
    small_o[4:5] = jnp.sum(jnp.where(owner, wide[:, 0:128], 0.0), axis=0, keepdims=True)
    lane = lax.broadcasted_iota(jnp.int32, (1, 128), 1)
    small_o[5:6] = jnp.where(lane == 0, total[0:1, 512:640], total[1:2, 512:640])
    small_o[6:8] = jnp.zeros((2, 128), F32)

    layer_out.wait()
    tg_out.wait()
    waited |= {("kv", 0), ("kv", 1)} | {("c", F[p]) for p in range(PAIRS - 1)}
    for key in table:
        if key not in waited:
            (cp(*key) if isinstance(key, tuple) else cp(key)).wait_send()


def results_kernel(*refs):
    taken, small, given, held, sem = refs[:8], refs[8], refs[9:23], refs[23:31], refs[31]
    steps = []
    for i in range(8):
        there = given[i].at[0] if i < 2 else given[i]
        steps.append(
            (
                pltpu.make_async_copy(taken[i], held[i], sem.at[i]),
                pltpu.make_async_copy(held[i], there, sem.at[8 + i]),
            )
        )
    for come, _ in steps:
        come.start()
    for row, ref in enumerate(given[8:]):
        ref[...] = small[row, 0 : ref.shape[0]]
    for come, go in steps:
        come.wait()
        go.start()
    for _, go in steps:
        go.wait()


def scratch():
    v = pltpu.VMEM
    return [
        v((1024, 512), BF),
        v((512, 512), BF),
        v((3, 2, 2, 2, 64, 512), BF),
        v((2, 2, 2, 64, 640), BF),
        v((4, 2, 2, 2, 128, 512), BF),
        v((8, 80, 512), BF),
        v((8, 80, 1024), BF),
        v((512, 1024), BF),
        v((8, 1024, 512), F32),
        v((8, 8, 512), F32),
        v((1024, 512), F32),
        v((1024, 512), BF),
        v((512, 512), BF),
        v((512, 512), F32),
        v((512, 512), BF),
        v((512, 512), F32),
        v((512, 512), F32),
        v((512, 512), BF),
        v((512, 512), BF),
        v((512, 512), BF),
        v((2, 2, 128, 1024), F32),
        v((2, 2, 128, 512), F32),
        v((4, 2, 2, 2, 128, 512), F32),
        v((4, 2, 2, 128, 512), F32),
        v((4, 2, 2, 64, 512), BF),
        v((4, 2, 2, 64, 512), BF),
        v((4, 2, 64, 512), BF),
        v((4, 2, 64, 512), BF),
        v((4, 3, 16, 512), BF),
        v((4, 3, 16, 512), BF),
        v((3, 64, 512), BF),
        v((3, 64, 512), BF),
        v((2, 2, 2, 64, 512), F32),
        v((2, 2, 64, 512), F32),
        v((2, 2, 32, 512), BF),
        v((2, 2, 32, 512), BF),
        v((2, 32, 512), BF),
        v((2, 32, 512), BF),
        v((3, 16, 512), BF),
        v((3, 16, 512), BF),
        v((4, 2, 2, 32, 384), BF),
        v((4, 2, 2, 32, 384), BF),
        v((4, 2, 32, 384), BF),
        v((4, 2, 32, 384), BF),
        v((4, 3, 16, 384), BF),
        v((4, 3, 16, 384), BF),
        v((2, 2, 2, 64, 384), F32),
        v((2, 2, 64, 384), F32),
        v((2, 3, 64, 384), BF),
        v((2, 3, 64, 384), BF),
        v((128, 512), F32),
        v((3, 8, 640), F32),
        v((7, 8, 640), F32),
        v((32, 128), BF),
        pltpu.SemaphoreType.DMA((256,)),
        pltpu.SemaphoreType.DMA((256,)),
        pltpu.SemaphoreType.DMA((24,)),
    ]


def on_device(
    tokens,
    segments,
    fill_length,
    query_weight,
    key_weight,
    value_weight,
    output_weight,
    query_bias,
    value_bias,
    output_bias,
    inner_weight,
    inner_bias,
    outer_weight,
    outer_bias,
    residual_gates,
    cotangent,
):
    names = ("dp", "shard")
    several = lax.axis_size("dp") > GROUP
    place = lax.rem(lax.axis_index("dp"), GROUP) * 2 + lax.axis_index("shard")

    def block_of(shard):
        if not several:
            return shard
        whole = lax.all_gather(shard, names, axis=0, tiled=True)
        rows = whole.shape[0] // (2 * GROUP)
        return lax.dynamic_slice_in_dim(whole, place * rows, rows, 0)

    def owned(block):
        if not several:
            return block
        rows = block.shape[0]
        whole = jnp.zeros((rows * 2 * GROUP, *block.shape[1:]), F32)
        whole = lax.dynamic_update_slice_in_dim(whole, block, place * rows, 0)
        return lax.psum_scatter(whole, names, scatter_dimension=0, tiled=True)

    query_weight, key_weight, value_weight, output_weight, inner_weight, outer_weight = map(
        block_of, (query_weight, key_weight, value_weight, output_weight, inner_weight, outer_weight)
    )
    query_bias, value_bias, output_bias, inner_bias, outer_bias = map(
        block_of, (query_bias, value_bias, output_bias, inner_bias, outer_bias)
    )
    vmem = pl.BlockSpec(memory_space=pltpu.VMEM)
    smem = pl.BlockSpec(memory_space=pltpu.SMEM)
    hbm = pl.BlockSpec(memory_space=pl.ANY)
    shape = jax.ShapeDtypeStruct
    outs = pl.pallas_call(
        layer_kernel,
        out_shape=[
            shape((512, 512), BF),
            shape((512, 512), F32),
            shape((16, 512), F32),
            shape((16, 512), F32),
            shape((16, 512), F32),
            shape((16, 512), F32),
            shape((16, 2048), F32),
            shape((64, 512), F32),
            shape((8, 128), F32),
        ],
        in_specs=[hbm, hbm, vmem, smem, smem] + [vmem] * 5 + [hbm] * 6,
        out_specs=[hbm, hbm] + [vmem] * 7,
        scratch_shapes=scratch(),
        compiler_params=pltpu.CompilerParams(
            collective_id=0, has_side_effects=True, vmem_limit_bytes=VMEM_BYTES
        ),
    )(
        tokens.reshape(512, 512),
        cotangent.reshape(512, 512),
        segments,
        fill_length,
        residual_gates,
        query_bias,
        value_bias,
        output_bias,
        outer_bias,
        inner_bias,
        query_weight,
        key_weight,
        value_weight,
        output_weight,
        inner_weight,
        outer_weight,
    )
    flat = [shape(o.shape, o.dtype) for o in outs[2:8]] + [shape((n,), F32) for n in (16, 16, 16, 16, 64, 2)]
    outs = pl.pallas_call(
        results_kernel,
        out_shape=[shape((1, 512, 512), BF), shape((1, 512, 512), F32)] + flat,
        in_specs=[pl.BlockSpec(memory_space=pltpu.HBM)] * 8 + [vmem],
        out_specs=[hbm] * 8 + [vmem] * 6,
        scratch_shapes=[pltpu.VMEM(o.shape, o.dtype) for o in outs[:8]] + [pltpu.SemaphoreType.DMA((16,))],
        compiler_params=pltpu.CompilerParams(vmem_limit_bytes=VMEM_BYTES),
    )(*outs)
    layer, token_grads, gq, gk, gv, go, gi, gout, g_query, g_value, g_output, g_outer, g_inner, gate_sums = outs
    if several:
        gate_sums = lax.psum(jnp.where(place == 0, gate_sums, 0.0), names)
    grads = (gq, gk, gv, go, g_query, g_value, g_output, gi, g_inner, gout, g_outer)
    return (layer, token_grads, *map(owned, grads), gate_sums)


def solution(mesh):
    spread = P(("dp", "shard"))
    return jax.shard_map(
        on_device,
        mesh=mesh,
        in_specs=(
            P("dp", "shard", None),
            P("dp", None),
            P("dp"),
            *([P(("dp", "shard"), None)] * 4),
            *([spread] * 3),
            P(("dp", "shard"), None),
            spread,
            P(("dp", "shard"), None),
            spread,
            P(),
            P("dp", "shard", None),
        ),
        out_specs=(
            P("dp", "shard", None),
            P("dp", "shard", None),
            *([P(("dp", "shard"), None)] * 4),
            *([spread] * 3),
            P(("dp", "shard"), None),
            spread,
            P(("dp", "shard"), None),
            spread,
            P(),
        ),
        check_vma=False,
    )
```

```python
import jax
import jax.numpy as jnp
from jax import lax
from jax.experimental import pallas as pl
from jax.experimental.pallas import tpu as pltpu
from jax.sharding import PartitionSpec as P

MESH = pl.DeviceIdType.MESH
BF = jnp.bfloat16
F32 = jnp.float32
HEADS = 8
GROUP = 16
PAIRS = 4
VMEM_BYTES = 64 * 2**20 - 2**17
PLAN = {
    "fwd0": ("2q2",),
    "fwd1": ("2q3", "zf3", "1f1", "3q1",),
    "proj1": ("2f0",),
    "fwd2": ("3q2",),
    "fwd3": ("3q3", "1f2",),
    "proj3": ("2f1", "1f3",),
    "fwd6": ("3f0",),
    "outproj": ("2f2",),
    "mid0": ("3f1",),
    "ffn1": ("2f3",),
    "mid1": ("3f2",),
    "ffn2": ("FF0", "3f3",),
    "ffn3": ("FF1",),
    "pre": ("SF0",),
    "bwd0": ("FF2",),
    "bwd1": ("SF1",),
    "bwd2": ("TF0",),
    "bwd3": ("FF3",),
    "fin0": ("SF2",),
    "bwd4": ("TF1",),
    "bwd5": ("FO",),
    "fin1": ("FQ0",),
    "bwd6": ("SF3", "TF2",),
    "bwd7": ("FQ1",),
    "fin2": ("SQ0",),
    "prod7": ("TF3", "EP",),
    "layer": ("SO",),
    "fin3": ("FQ2",),
    "tok3": ("EZ", "TQ0", "SQ1", "TO",),
    "last1": ("TQ1", "TQ2",),
    "start": ("zq2", "1q0", "zq3", "1q1", "zf0", "1q2", "zf1", "1q3", "zf2", "2q0", "3q0", "2q1", "1f0",),
}
STEPS = 4


def dot(left, right, left_dim, right_dim):
    return lax.dot_general(
        left, right, (((left_dim,), (right_dim,)), ((), ())), preferred_element_type=F32
    )


def gelu_parts(hidden):
    size = jnp.abs(hidden) * 0.7071067811865476
    recip = 1.0 / (1.0 + 0.3275911 * size)
    expo = jnp.exp(-size * size)
    poly = recip * (
        0.127414796
        + recip * (-0.142248368 + recip * (0.7107068705 + recip * (-0.7265760135 + recip * 0.5307027145)))
    )
    tail = poly * expo
    cdf = jnp.where(hidden >= 0, 1.0 - tail, tail)
    return hidden * cdf, cdf + hidden * expo * 0.3989422804014327


def by_chip(value):
    width = value.shape[-1]
    return value.reshape(4, 8, 16, width).transpose(1, 0, 2, 3).reshape(2, 2, 2, 64, width)


def col_sums(value):
    return dot(jnp.ones((8, value.shape[0]), BF), value, 1, 0)


def layer_kernel(
    tok,
    cot,
    seg_in,
    fill_in,
    gates_in,
    bias_q,
    bias_v,
    bias_o,
    bias_out,
    bias_in,
    wquery,
    wkey,
    wvalue,
    wout_proj,
    win,
    wout,
    layer_o,
    tg_o,
    gq_o,
    gk_o,
    gv_o,
    go_o,
    gi_o,
    gout_o,
    small_o,
    seg,
    fill,
    gates,
    own_q,
    own_v,
    own_o,
    own_out,
    own_in,
    biasf,
    gq_s,
    gk_s,
    gv_s,
    go_s,
    gi_s,
    gout_s,
    small_s,
    xrow,
    cotv,
    wq_rest,
    wq_last,
    wf,
    qt,
    kt,
    vt,
    probs,
    scales,
    st,
    pb,
    mixt,
    attn,
    rlow,
    ffn,
    gres,
    gffn,
    gmixt,
    dqt,
    dkv,
    rkv,
    gf,
    rcf,
    s1f,
    r1f,
    s2f,
    r2f,
    s3f,
    r3f,
    s3o,
    r3o,
    go,
    rco,
    s1o,
    r1o,
    s2o,
    r2o,
    s3w,
    r3w,
    s1q,
    r1q,
    s2q,
    r2q,
    s3q,
    r3q,
    glast,
    rclast,
    s1d,
    r1d,
    ksum,
    bb,
    rb,
    eb,
    re,
    biasb,
    send_sem,
    recv_sem,
    local_sem,
):
    hid, gac = st.at[pl.ds(0, 512)], st.at[pl.ds(512, 512)]
    act, ghid = pb.at[pl.ds(0, 512)], pb.at[pl.ds(512, 512)]
    wq = [wq_rest.at[p] for p in range(PAIRS - 1)] + [wq_last]

    dp = lax.axis_index("dp")
    c = lax.axis_index("shard")
    lo = lax.rem(dp, GROUP)
    z = lax.div(lo, 4)
    y = lax.rem(lax.div(lo, 2), 2)
    x = lax.rem(lo, 2)
    cc, xx, yy = 1 - c, 1 - x, 1 - y

    def zk(k):
        return lax.rem(z + (k % 4), 4)

    zs = [zk(k) for k in range(4)]
    XP = (dp + 1 - 2 * x, c)
    YP = (dp + 2 - 4 * y, c)
    ZP = [None] + [(dp + 4 * (zs[k] - z), c) for k in (1, 2, 3)]
    DP = (dp + 3 - 2 * x - 4 * y, c)
    SB = (dp, cc)

    def rows(place):
        return pl.ds(pl.multiple_of(place * 16, 16), 16)

    def cols(place):
        return pl.ds(pl.multiple_of(place * 512, 512), 512)

    table = {}
    ids = {}

    def same(ref, dev):
        return (ref, ref, dev)

    for p in range(PAIRS):
        for k in (1, 2, 3):
            table["z", ("q", p), k] = lambda p=p, k=k: (
                wq[p].at[y, x, c, pl.ds(0, 16)],
                wq[p].at[y, x, c, pl.ds(k * 16, 16)],
                ZP[k],
            )
        for name, dev in (("x", XP), ("y", YP), ("d", DP)):
            if p == 0 or name != "d":
                for part, (low, count) in enumerate(((0, 16), (16, 48))):
                    table[name, ("q", p), part] = lambda p=p, low=low, count=count, dev=dev: same(
                        wq[p].at[y, x, c, pl.ds(low, count)], dev
                    )
        table["s", ("q", p), 0] = lambda p=p: same(wq[p].at[y, :, c], SB)
        table["s", ("q", p), 1] = lambda p=p: same(wq[p].at[yy, :, c], SB)
        if p:
            table["rx", ("q", p)] = lambda p=p: same(wq[p].at[y, xx, c, pl.ds(0, 32)], YP)
            table["ry", ("q", p)] = lambda p=p: same(wq[p].at[yy, x, c, pl.ds(32, 32)], XP)
    for s in range(STEPS):
        for k in (1, 2, 3):
            table["z", ("f", s), k] = lambda s=s, k=k: (
                win.at[:, cols(zs[(k + s) % 4])],
                wf.at[s, y, x, c, pl.ds(64 + k * 16, 16)],
                ZP[k],
            )
        if s:
            table["zo", ("f", s)] = lambda s=s: (wout, wf.at[s, y, x, c, pl.ds(16, 64)], ZP[4 - s])
        split = 16 if s else 80
        for name, dev in (("x", XP), ("y", YP)):
            for part, (low, count) in enumerate(((0, split), (split, 128 - split))):
                table[name, ("f", s), part] = lambda s=s, low=low, count=count, dev=dev: same(
                    wf.at[s, y, x, c, pl.ds(low, count)], dev
                )
        table["rx", ("f", s)] = lambda s=s: same(wf.at[s, y, xx, c, pl.ds(0, 64)], YP)
        table["ry", ("f", s)] = lambda s=s: same(wf.at[s, yy, x, c, pl.ds(64, 64)], XP)
        table["s", ("f", s), 0] = lambda s=s: same(wf.at[s, y, :, c], SB)
        table["s", ("f", s), 1] = lambda s=s: same(wf.at[s, yy, :, c], SB)
    table["tok"] = lambda: (xrow.at[pl.ds(0, 512)], xrow.at[pl.ds(512, 512)], SB)
    groups = {}
    LAST = (("q", PAIRS - 2), ("q", PAIRS - 1))
    for s in range(STEPS):
        groups["f", s] = (gf.at[s], rcf.at[s], s1f.at[s], r1f.at[s], s2f.at[s], r2f.at[s], s3f.at[s], r3f.at[s])
        if s:
            table["o3", s] = lambda s=s: (s3o.at[s - 1], r3o.at[s - 1], ZP[s])
    groups["o"] = (go, rco, s1o, r1o, s2o, r2o, s3w, r3w)
    for p in range(PAIRS):
        if p < PAIRS - 1:
            gq = gf.at[p, :, :, :, pl.ds(0, 64), pl.ds(0, 384)]
            rcq = rcf.at[p, :, :, pl.ds(0, 64), pl.ds(0, 384)]
        else:
            gq, rcq = glast, rclast
        groups["q", p] = (gq, rcq, s1q.at[p], r1q.at[p], s2q.at[p], r2q.at[p], s3q.at[p], r3q.at[p])
        if p < PAIRS - 1:
            table["kv", p] = lambda p=p: (dkv.at[p % 2, :, :, pl.ds(512, 512)], rkv.at[p % 2], SB)
        else:
            for j in range(2):
                table["kv", p, j] = lambda p=p, j=j: (
                    dkv.at[p % 2, :, pl.ds(j * 64, 64), pl.ds(512, 512)],
                    rkv.at[p % 2, :, pl.ds(j * 64, 64)],
                    SB,
                )
    for g, (grad, rc, s1, r1, s2, r2, s3, r3) in groups.items():
        table["c", g] = lambda grad=grad, rc=rc: (grad.at[:, :, cc], rc, SB)
        if g in LAST:
            for i, dev in enumerate((XP, YP, DP)):
                table["d1", g, i] = lambda i=i, dev=dev, at=LAST.index(g): (s1d.at[at, i], r1d.at[at, i], dev)
            for k in (1, 2, 3):
                table["z3", g, k] = lambda s3=s3, r3=r3, k=k: (s3.at[k - 1], r3.at[k - 1], ZP[k])
            continue
        table["a1", g] = lambda s1=s1, r1=r1: (s1.at[0], r1.at[0], XP)
        table["b1", g] = lambda s1=s1, r1=r1: (s1.at[1], r1.at[1], YP)
        table["a2", g] = lambda s2=s2, r2=r2: (s2.at[0], r2.at[0], YP)
        table["b2", g] = lambda s2=s2, r2=r2: (s2.at[1], r2.at[1], XP)
        for k in (1, 2, 3):
            table["z3", g, k] = lambda s3=s3, r3=r3, k=k: (s3.at[k - 1], r3.at[k - 1], ZP[k])
    for kind, (mine, come) in {"b": (bb, rb), "e": (eb, re)}.items():
        table[kind + "c"] = lambda mine=mine, come=come: (mine.at[0], come.at[0], SB)
        for i, dev in enumerate((XP, YP, DP)):
            table[kind + "p", i] = lambda i=i, dev=dev, mine=mine, come=come: (mine.at[1], come.at[1 + i], dev)
        for k in (1, 2, 3):
            table[kind + "z", k] = lambda k=k, mine=mine, come=come: (mine.at[2], come.at[3 + k], ZP[k])

    def batch(key):
        if not isinstance(key, tuple):
            return key
        kind = {"zo": "z", "rx": "r", "ry": "r", "a1": "1", "b1": "1", "a2": "2", "b2": "2"}.get(key[0], key[0])
        if kind in ("bp", "bz", "ep", "ez", "o3"):
            return kind
        if kind == "z3":
            return "z3" + key[1][0]
        return (kind, key[1])

    for key in table:
        ids.setdefault(batch(key), len(ids))
    weight_batches = [one for one in ids if one[0] in ("z", "x", "y", "d", "r", "s") and isinstance(one, tuple)]
    sum_batches = [one for one in ids if one not in weight_batches and one != "tok"]
    send_ids = {one: i for i, one in enumerate(weight_batches + ["tok"])}
    early = [one for one in weight_batches if one[1][0] == "q"] + [one for one in weight_batches if one[1][0] == "f"]
    late = [("kv", 2), ("kv", 3), "z3q", "bc", "bp", "bz", "ec", "ep", "ez"]
    late += [one for one in sum_batches if isinstance(one[1], tuple) and one[1][0] == "q"]
    for one, place in zip([one for one in sum_batches if one not in late] + late, early):
        send_ids[one] = send_ids[place]
    whole = {"tok": xrow.at[pl.ds(512, 512)]}
    for g in [("q", p) for p in range(PAIRS)] + [("f", s) for s in range(STEPS)]:
        chunk = wq[g[1]] if g[0] == "q" else wf.at[g[1]]
        low = 80 if g == ("f", 0) else 16
        whole["z", g] = chunk.at[y, x, c, pl.ds(low, chunk.shape[3] - low)]
        whole["x", g] = chunk.at[y, xx, c]
        whole["y", g] = chunk.at[yy, x, c]
        whole["d", g] = whole["r", g] = chunk.at[yy, xx, c]
        whole["s", g] = chunk.at[:, :, cc]
    for g, (grad, rc, s1, r1, s2, r2, s3, r3) in groups.items():
        whole["c", g], whole["1", g], whole["2", g] = rc, r1, r2
    for i, g in enumerate(LAST):
        whole["d1", g] = r1d.at[i]
    for p in range(PAIRS):
        whole["kv", p] = rkv.at[p % 2]
    whole |= {"z3f": r3f, "z3q": r3q, "z3o": r3w, "o3": r3o, "bc": rb.at[0], "ec": re.at[0]}
    whole |= {"bp": rb.at[pl.ds(1, 3)], "bz": rb.at[pl.ds(4, 3)], "ep": re.at[pl.ds(1, 3)], "ez": re.at[pl.ds(4, 3)]}

    def start(*key):
        key = key if len(key) > 1 else key[0]
        src, dst, dev = table[key]()
        pltpu.make_async_remote_copy(
            src_ref=src,
            dst_ref=dst,
            send_sem=send_sem.at[send_ids[batch(key)]],
            recv_sem=recv_sem.at[ids[batch(key)]],
            device_id=dev,
            device_id_type=MESH,
        ).start()

    def all_of(one):
        return pltpu.make_async_remote_copy(
            src_ref=whole[one],
            dst_ref=whole[one],
            send_sem=send_sem.at[send_ids[one]],
            recv_sem=recv_sem.at[ids[one]],
            device_id=SB,
            device_id_type=MESH,
        )

    waited = set()

    def recv(*key):
        all_of(key if len(key) > 1 else key[0]).wait_recv()

    def sent(*key):
        one = key if len(key) > 1 else key[0]
        waited.add(one)
        all_of(one).wait_send()

    def natural(ref, firsts, columns):
        parts = [
            ref[:, :, :, pl.ds(pl.multiple_of(firsts(lax.rem(z + 4 - other, 4)), 16), 16), columns]
            for other in range(4)
        ]
        return jnp.concatenate([part.reshape(128, part.shape[-1]) for part in parts], axis=0)

    def attention_block(k):
        return k * 16

    def inner_block(k):
        return jnp.where(k == 0, 0, k * 16 + 64)

    local = (
        [(tok, xrow.at[pl.ds(0, 512)]), (cot, cotv), (wout, wf.at[0, y, x, c, pl.ds(16, 64)])]
        + [(win.at[:, cols(zs[s])], wf.at[s, y, x, c, pl.ds(0, 16)]) for s in range(STEPS)]
        + [
            (
                ref.at[:, pl.ds(p * 128, 128)],
                (wq[p] if i < 3 or p else wq_last).at[
                    y, x, c, pl.ds(0, 16), pl.ds(i * 128 if i < 3 or p else 512, 128)
                ],
            )
            for p in range(PAIRS)
            for i, ref in enumerate((wquery, wkey, wvalue, wout_proj))
        ]
    )
    local = [pltpu.make_async_copy(src, dst, local_sem.at[i]) for i, (src, dst) in enumerate(local)]
    needed = [(bias_q, own_q), (bias_v, own_v), (bias_o, own_o), (bias_out, own_out), (bias_in, own_in)]
    needed += [(seg_in, seg), (fill_in, fill), (gates_in, gates)]
    needed = [pltpu.make_async_copy(src, dst, local_sem.at[len(local) + i]) for i, (src, dst) in enumerate(needed)]
    for one in local[7:11] + needed + local[:7] + local[11:]:
        one.start()
    barrier = pltpu.get_barrier_semaphore()
    peers = (XP, YP, DP, ZP[1], ZP[2], ZP[3], SB)
    for dev in peers:
        pl.semaphore_signal(barrier, inc=1, device_id=dev, device_id_type=MESH)

    biasf[...] = jnp.zeros((8, 128), F32)
    for one in needed:
        one.wait()
    for row, ref in enumerate((own_q, own_v, own_o, own_out, own_in)):
        count = ref.shape[0]
        biasf[row : row + 1, 0:count] = ref[...].astype(F32).reshape(1, count)
    packed = jnp.sum(pltpu.roll(biasf[...], 0, 1, stride=16, stride_axis=0), axis=0, keepdims=True)
    first = lax.broadcasted_iota(jnp.int32, (16, 128), 0) == 0
    own_bias = jnp.where(first, jnp.broadcast_to(packed, (16, 128)), 0.0)
    wq[0][y, x, c, pl.ds(0, 16), pl.ds(384, 128)] = own_bias.astype(BF)
    for one in local[7:11]:
        one.wait()
    pl.semaphore_wait(barrier, len(peers))

    def send_z(g):
        for k in (1, 2, 3):
            start("z", g, k)
        if g[0] == "f" and g[1]:
            start("zo", g)

    def neighbours(g):
        return ("x", "y", "d") if g == ("q", 0) else ("x", "y")

    def send_early(g):
        for name in neighbours(g):
            start(name, g, 0)

    def send_plane(g):
        recv("z", g)
        for name in neighbours(g):
            start(name, g, 1)

    def send_relay(g):
        for name in ("x", "y"):
            recv(name, g)
            if g != ("q", 0):
                start("r" + name, g)
            if name == "x":
                start("s", g, 0)

    def send_across(g):
        if g == ("q", 0):
            recv("d", g)
        else:
            recv("r", g)
        start("s", g, 1)

    def all_here(g):
        recv("s", g)

    Q, F = [("q", p) for p in range(PAIRS)], [("f", s) for s in range(STEPS)]
    send_z(Q[0])
    send_early(Q[0])
    for one in local[11:]:
        one.wait()
    send_z(Q[1])
    local[0].wait()
    start("tok")
    for p in (1, 2, 3):
        send_early(Q[p])
    for one in local[2:7]:
        one.wait()
    for s in range(STEPS):
        send_early(F[s])

    kind = lax.broadcasted_iota(jnp.int32, (16, 512), 0)
    at_own = lax.broadcasted_iota(jnp.int32, (16, 512), 1) + c * 512
    at_sib = lax.broadcasted_iota(jnp.int32, (16, 512), 1) + cc * 512
    own_seg = seg[:, pl.ds(pl.multiple_of(c * 512, 512), 512)]
    sib_seg = seg[:, pl.ds(pl.multiple_of(cc * 512, 512), 512)]
    used = fill[0]
    for half, (segs, spot) in enumerate(((own_seg, at_own), (sib_seg, at_sib))):
        unused = jnp.where(spot >= used, 1.0, 0.0)
        marks = jnp.where(kind == 8, unused, jnp.where(kind == segs, 1.0, 0.0)).astype(BF)
        for head in range(HEADS):
            kt[head, 64:80, half * 512 : half * 512 + 512] = marks
    barred = jnp.where((kind == own_seg) | (kind > 8), 0.0, -1e30).astype(BF)
    for head in range(HEADS):
        qt[head, 64:80] = barred

    gate_attn = gates[0]
    gate_feed = gates[1]
    local[1].wait()
    upstream = cotv[...].astype(F32)
    gffn[...] = (gate_feed * upstream).astype(BF)

    def small_plane():
        recv("ec")
        eb[1] = eb[0] + re[0]
        for i in range(3):
            start("ep", i)

    def small_column():
        recv("ep")
        eb[2] = eb[1] + (re[1] + re[2] + re[3])
        for k in (1, 2, 3):
            start("ez", k)

    def take(name):
        if name in ("EP", "EZ"):
            done.append(name)
            return small_plane() if name == "EP" else small_column()
        kind, g = name[0], ({"q": "q", "f": "f", "Q": "q", "F": "f"}.get(name[1]), int(name[2:] or 0))
        if name[1] == "O":
            g = "o"
        if name in done:
            raise ValueError(name)
        done.append(name)
        if kind == "z":
            send_z(g)
        elif kind == "1":
            send_plane(g)
        elif kind == "2":
            send_relay(g)
        elif kind == "3":
            send_across(g)
        elif kind == "F":
            fold_plane(g) if g in LAST else fold_first(g)
        elif kind == "S":
            fold_second(g)
        elif g in LAST:
            fold_column(g)
        elif g == "o":
            fold_third(g)
            go_s[...] = ksum[rows(z), :]
        elif g[0] == "f":
            ffn_third(g[1])
        else:
            q_third(g[1])

    done, given = [], []

    def give(held, out):
        one = pltpu.make_async_copy(held, out, local_sem.at[len(given)])
        one.start()
        given.append(one)

    def at_point(name):
        for one in PLAN.get(name, ()):
            take(one)

    at_point("start")
    recv("tok")
    all_here(Q[0])

    held = natural(wq[0], attention_block, slice(384, 512)).reshape(32, 16, 128)
    biasb[...] = jnp.sum(held.astype(F32), axis=1).astype(BF)

    def bias_row(offset, per, width):
        lane = lax.broadcasted_iota(jnp.int32, (128, width), 0)
        at = lax.broadcasted_iota(jnp.int32, (128, width), 1)
        pick = (lane == offset + (at & (per - 1))).astype(F32).astype(BF)
        spread = dot(biasb[...], pick, 1, 0)
        owner = lax.broadcasted_iota(jnp.int32, (32, width), 0)
        at = lax.broadcasted_iota(jnp.int32, (32, width), 1)
        return jnp.sum(jnp.where(owner == lax.shift_right_logical(at, per.bit_length() - 1), spread, 0.0), axis=0, keepdims=True)

    first_row = lax.broadcasted_iota(jnp.int32, (16, 512), 0) == 0
    ones_row = jnp.where(first_row, 1.0, 0.0).astype(BF)

    def as_rank_one(row):
        return jnp.where(first_row, jnp.broadcast_to(row, (16, 512)), 0.0).astype(BF)

    bias_q = as_rank_one(bias_row(0, 16, 512))
    bias_v = as_rank_one(bias_row(16, 16, 512))

    def project(p):
        weights = natural(wq[p], attention_block, slice(0, 384))
        ours = dot(weights, xrow[0:512], 0, 1)
        theirs = dot(weights[:, 128:384], xrow[512:1024], 0, 1)
        at = slice(p * 128, p * 128 + 128)
        grown = ours[0:128] + dot(bias_q[:, at], ones_row, 0, 0)
        grown = (grown.astype(BF).astype(F32) * 0.125).astype(BF)
        add_v = dot(bias_v[:, at], ones_row, 0, 0)
        for j in range(2):
            part = slice(j * 64, j * 64 + 64)
            qt[p * 2 + j, 0:64] = grown[part]
            kt[p * 2 + j, 0:64, 0:512] = ours[128 + j * 64 : 192 + j * 64].astype(BF)
            kt[p * 2 + j, 0:64, 512:1024] = theirs[part].astype(BF)
        vt[at, 0:512] = (ours[256:384] + add_v).astype(BF)
        vt[at, 512:1024] = (theirs[128:256] + add_v).astype(BF)

    def half_of(unit):
        return unit // 2, slice(unit % 2 * 256, unit % 2 * 256 + 256)

    def scores_of(unit):
        head, lanes = half_of(unit)
        raw = dot(kt[head], qt[head, :, lanes], 0, 0)
        own = kt[head, 0:64, lanes].astype(F32) * qt[head, 0:64, lanes].astype(F32)
        own = jnp.sum(own, axis=0, keepdims=True)
        highest = jnp.full((8, 256), -jnp.inf, F32)
        for b in range(8):
            r = slice(b * 128, b * 128 + 128)
            block = raw[r]
            if b // 2 == unit % 2 and b < 4:
                diagonal = lax.broadcasted_iota(jnp.int32, (128, 256), 1) == (
                    lax.broadcasted_iota(jnp.int32, (128, 256), 0) + b % 2 * 128
                )
                block = jnp.where(diagonal, own, block)
            st[r, lanes] = block
            highest = jnp.maximum(highest, jnp.max(block.reshape(16, 8, 256), axis=0))
        return jnp.max(highest, axis=0, keepdims=True)

    def attend(unit, highest):
        head, lanes = half_of(unit)
        total = jnp.zeros((8, 256), F32)
        for b in range(8):
            r = slice(b * 128, b * 128 + 128)
            expo = jnp.exp(st[r, lanes] - highest)
            probs[head, r, lanes] = expo
            total = total + jnp.sum(expo.reshape(16, 8, 256), axis=0)
        scale = 1.0 / jnp.sum(total, axis=0, keepdims=True)
        scales[head, :, lanes] = jnp.broadcast_to(scale, (8, 256))
        for b in range(8):
            r = slice(b * 128, b * 128 + 128)
            pb[r, lanes] = (probs[head, r, lanes] * scale).astype(BF)
        at = slice(head * 64, head * 64 + 64)
        mixt[at, lanes] = dot(vt[at], pb[:, lanes], 1, 0).astype(BF)

    for head in range(HEADS):
        first = head * 2
        if head % 2 == 0:
            if head:
                at_point("proj%d" % (head // 2))
                all_here(Q[head // 2])
            project(head // 2)
        at_point("fwd%d" % head)
        if head % 2 == 0:
            highest = scores_of(first)
        later = scores_of(first + 1)
        attend(first, highest)
        if head % 2 == 0:
            highest = scores_of(first + 2)
        attend(first + 1, later)

    at_point("outproj")
    sent("tok")
    for one in weight_batches:
        if one[1][0] == "q":
            sent(*one)
    out_weight = jnp.concatenate(
        [natural(wq_last, attention_block, slice(512, 640))] + [natural(wq[p], attention_block, slice(384, 512)) for p in (1, 2, 3)], axis=1
    )
    attn[...] = dot(mixt[...], out_weight, 0, 0) + bias_row(32, 16, 512)
    resid = xrow[0:512].astype(F32) + gate_attn * attn[...]
    rlow[...] = resid.astype(BF)
    ffn[...] = jnp.zeros((512, 512), F32)
    gres[...] = cotv[...].astype(F32)

    def fold_first(g):
        grad, rc, s1 = groups[g][:3]
        half = rc.shape[2] // 2
        recv("c", g)
        for i in range(2):
            s1[0, i] = (grad[i, xx, c, 0:half] + rc[i, xx, 0:half]).astype(BF)
            s1[1, i] = (grad[yy, i, c, half : 2 * half] + rc[yy, i, half : 2 * half]).astype(BF)
        start("a1", g)
        start("b1", g)

    def fold_second(g):
        grad, rc, s1, r1, s2, r2 = groups[g][:6]
        half = rc.shape[2] // 2
        recv("1", g)
        s2[0] = (grad[yy, x, c, 0:half] + rc[yy, x, 0:half] + r1[0, yy].astype(F32)).astype(BF)
        start("a2", g)
        s2[1] = (
            grad[y, xx, c, half : 2 * half] + rc[y, xx, half : 2 * half] + r1[1, xx].astype(F32)
        ).astype(BF)
        start("b2", g)

    def fold_third(g):
        grad, rc, s1, r1, s2, r2, s3, r3 = groups[g]
        half = rc.shape[2] // 2
        width = rc.shape[3]
        recv("2", g)
        upper = grad[y, x, c, 0:half] + rc[y, x, 0:half] + r1[0, y].astype(F32) + r2[0].astype(F32)
        ksum[0:half, 0:width] = upper
        lower = (
            grad[y, x, c, half : 2 * half]
            + rc[y, x, half : 2 * half]
            + r1[1, x].astype(F32)
            + r2[1].astype(F32)
        )
        ksum[half : 2 * half, 0:width] = lower
        for k in (1, 2, 3):
            s3[k - 1] = ksum[rows(zs[k]), 0:width].astype(BF)
            start("z3", g, k)

    def ffn_third(s):
        fold_third(("f", s))
        gi_s[:, cols(zs[s])] = ksum[rows(z), :]
        if s:
            s3o[s - 1] = ksum[64:128].astype(BF)
            start("o3", s)
        else:
            gout_s[...] = ksum[64:128]

    def small(row, value):
        eb[0, row : row + 1, :] = value

    bb[0] = jnp.zeros((16, 128), F32)
    eb[0] = jnp.zeros((8, 512), F32)

    def ffn_step(s):
        all_here(F[s])
        inner = natural(wf.at[s], inner_block, slice(0, 512))
        outer = wf[s, :, :, :, 16:80].reshape(512, 512)
        hid[...] = dot(rlow[...], inner, 1, 0) + chunk_bias[s]
        gac[...] = dot(gffn[...], outer, 1, 1)
        for b in range(8):
            r = slice(b * 64, b * 64 + 64)
            value, slope = gelu_parts(hid[r])
            act[r] = value.astype(BF)
            ghid[r] = (gac[r] * slope).astype(BF)
        at_point("mid%d" % s)
        ffn[...] += dot(act[...], outer, 1, 0)
        gf[s, :, :, :, 64:128] = dot(act[...], gffn[...], 0, 0).reshape(2, 2, 2, 64, 512)
        gf[s, :, :, :, 0:64] = by_chip(dot(rlow[...], ghid[...], 0, 0))
        start("c", ("f", s))
        gres[...] += dot(ghid[...], inner, 1, 1)
        sums = col_sums(ghid[...])[0:1]
        for row in range(4):
            eb[0, 4 + row : 5 + row, :] = jnp.where(zs[s] == row, sums, eb[0, 4 + row : 5 + row, :])

    inner_bias = bias_row(64, 64, 2048)
    parts = [inner_bias[:, i * 512 : i * 512 + 512] for i in range(4)]
    chunk_bias = []
    for s in range(STEPS):
        picked = parts[3]
        for i in range(3):
            picked = jnp.where(zs[s] == i, parts[i], picked)
        chunk_bias.append(picked)
    for s in range(STEPS):
        at_point("ffn%d" % s)
        ffn_step(s)
    at_point("pre")

    for one in weight_batches:
        if one[1][0] == "f":
            sent(*one)

    small(1, col_sums(gffn[...])[0:1])
    gattn = (gate_attn * gres[...]).astype(BF)
    small(0, col_sums(gattn)[0:1])
    start("ec")
    go[...] = by_chip(dot(mixt[...], gattn, 1, 0))
    start("c", "o")
    gmixt[...] = dot(out_weight, gattn, 1, 1).astype(BF)
    def finish_layer():
        ffn[...] += bias_row(48, 16, 512)
        upstream = cotv[...].astype(F32)
        resid = xrow[0:512].astype(F32) + gate_attn * attn[...]
        rlow[...] = (resid + gate_feed * ffn[...]).astype(BF)
        give(rlow, layer_o)
        feed_part = jnp.sum(jnp.sum(upstream * ffn[...], axis=0, keepdims=True), axis=1, keepdims=True)
        bb[0, 9:10] = jnp.broadcast_to(feed_part, (1, 128))
        attn_part = jnp.sum(jnp.sum(gres[...] * attn[...], axis=0, keepdims=True), axis=1, keepdims=True)
        bb[0, 8:9] = jnp.broadcast_to(attn_part, (1, 128))


    def scores_back(unit):
        head, lanes = half_of(unit)
        at = slice(head * 64, head * 64 + 64)
        raw = dot(vt[at], gmixt[at, lanes], 0, 0)
        total = jnp.zeros((8, 256), F32)
        for b in range(8):
            r = slice(b * 128, b * 128 + 128)
            block = raw[r]
            st[r, lanes] = block
            total = total + jnp.sum((probs[head, r, lanes] * block).reshape(16, 8, 256), axis=0)
        return jnp.sum(total, axis=0, keepdims=True) * scales[head, 0:1, lanes]

    def slopes_of(unit, inner):
        head, lanes = half_of(unit)
        scale = scales[head, 0:1, lanes]
        slot = head % 2 * 2
        for b in range(8):
            r = slice(b * 128, b * 128 + 128)
            prob = probs[head, r, lanes] * scale
            place = (b // 4, b // 2 % 2, b % 2, slice(None), lanes)
            wf[(slot, *place)] = prob.astype(BF)
            wf[(slot + 1, *place)] = (prob * (st[r, lanes] - inner)).astype(BF)

    def products_of(head):
        at = slice(head * 64, head * 64 + 64)
        slot = head % 2 * 2
        prob, slope = (wf[i].reshape(1024, 512) for i in (slot, slot + 1))
        place = (head // 2 % 2, slice(None), slice(head % 2 * 64, head % 2 * 64 + 64))
        dkv[place[0], 0, place[2]] = dot(qt[head, 0:64], slope, 1, 1)
        dkv[place[0], 1, place[2]] = dot(gmixt[at], prob, 1, 1)
        if head >= 6:
            assert "FQ1" in done
            start("kv", 3, head - 6)
        dqt[at] = (dot(kt[head, 0:64], slope, 1, 0) * 0.125).astype(BF)

    def finish_pair(p):
        slot = p % 2
        at = slice(p * 128, p * 128 + 128)
        recv("kv", p)
        vt[at, 0:512] = (dkv[slot, 0, :, 0:512] + rkv[slot, 0]).astype(BF)
        vt[at, 512:1024] = (dkv[slot, 1, :, 0:512] + rkv[slot, 1]).astype(BF)
        both = jnp.concatenate([dqt[at], vt[at, 0:512], vt[at, 512:1024]], axis=0)
        if p < PAIRS - 1:
            sent("c", F[p])
            gf[p, :, :, :, 0:64, 0:384] = by_chip(dot(xrow[0:512], both, 0, 1))
        else:
            glast[...] = by_chip(dot(xrow[0:512], both, 0, 1))
        start("c", Q[p])
        sums = dot(jnp.ones((8, 512), BF), both, 1, 1)
        bb[0, p : p + 1] = sums[0:1, 0:128]
        bb[0, 4 + p : 5 + p] = sums[0:1, 256:384]

    def token_part(p):
        at = slice(p * 128, p * 128 + 128)
        both = jnp.concatenate([dqt[at], vt[at, 0:512], vt[at, 512:1024]], axis=0)
        gres[...] += dot(both, natural(wq[p], attention_block, slice(0, 384)), 0, 1)

    def fold_plane(g):
        grad, rc = groups[g][:2]
        recv("c", g)
        for i, (yi, xi) in enumerate(((y, xx), (yy, x), (yy, xx))):
            s1d[LAST.index(g), i] = (grad[yi, xi, c] + rc[yi, xi]).astype(BF)
            start("d1", g, i)

    def fold_column(g):
        grad, rc, s3 = groups[g][0], groups[g][1], groups[g][6]
        recv("d1", g)
        come = r1d.at[LAST.index(g)]
        ksum[0:64, 0:384] = (
            grad[y, x, c] + rc[y, x] + (come[0].astype(F32) + come[1].astype(F32) + come[2].astype(F32))
        )
        for k in (1, 2, 3):
            s3[k - 1] = ksum[rows(zs[k]), 0:384].astype(BF)
            start("z3", g, k)
        keep_pair(g[1])

    def q_third(p):
        fold_third(Q[p])
        keep_pair(p)

    def keep_pair(p):
        at = slice(p * 128, p * 128 + 128)
        gq_s[:, at] = ksum[rows(z), 0:128]
        gk_s[:, at] = ksum[rows(z), 128:256]
        gv_s[:, at] = ksum[rows(z), 256:384]

    inner = scores_back(0)
    for head in range(HEADS):
        at_point("bwd%d" % head)
        if head in (5, 7):
            sent("kv", (head - 5) // 2)
        if head:
            products_of(head - 1)
        if head in (2, 4, 6):
            p = head // 2 - 1
            assert "TF%d" % p in done and (p < 2 or "FQ%d" % (p - 2) in done)
            start("kv", p)
        later = scores_back(head * 2 + 1)
        slopes_of(head * 2, inner)
        if head < HEADS - 1:
            inner = scores_back(head * 2 + 2)
        slopes_of(head * 2 + 1, later)
        if head in (3, 5, 7):
            p = head // 2 - 1
            at_point("fin%d" % p)
            finish_pair(p)
    at_point("prod7")
    products_of(HEADS - 1)
    at_point("layer")
    finish_layer()
    at_point("fin3")
    finish_pair(3)

    start("bc")
    at_point("tok3")
    fold_plane(Q[3])
    recv("bc")
    bb[1] = bb[0] + rb[0]
    for i in range(3):
        start("bp", i)
    at_point("tok")
    for p in range(PAIRS):
        token_part(p)
    give(gres, tg_o)

    def q_last(p):
        at = slice(p * 128, p * 128 + 128)
        more = r3q[p, 0].astype(F32) + r3q[p, 1].astype(F32) + r3q[p, 2].astype(F32)
        gq_s[:, at] += more[:, 0:128]
        gk_s[:, at] += more[:, 128:256]
        gv_s[:, at] += more[:, 256:384]

    at_point("last1")
    fold_column(Q[3])
    at_point("last2")
    recv("bp")
    bb[2] = bb[1] + (rb[1] + rb[2] + rb[3])
    for k in (1, 2, 3):
        start("bz", k)
    assert len(done) == 55

    recv("z3f")
    for s in range(STEPS):
        more = r3f[(s + 1) % 4, 0].astype(F32)
        for k in (2, 3):
            more = more + r3f[(s + k) % 4, k - 1].astype(F32)
        gi_s[:, cols(zs[s])] += more
    give(gi_s, gi_o)
    recv("o3")
    for s in (1, 2, 3):
        gout_s[...] += r3o[s - 1].astype(F32)
    give(gout_s, gout_o)
    recv("z3o")
    for k in (1, 2, 3):
        go_s[...] += r3w[k - 1].astype(F32)
    give(go_s, go_o)
    recv("z3q")
    for p in range(PAIRS):
        q_last(p)
    give(gq_s, gq_o)
    give(gk_s, gk_o)
    give(gv_s, gv_o)
    recv("ez")
    total = eb[2] + re[4] + re[5] + re[6]
    device = lo * 2 + c
    narrow = pltpu.roll(total, lax.rem(512 - device * 16, 512), 1)
    wide = pltpu.roll(total, lax.rem(512 - lax.rem(device, 8) * 64, 512), 1)
    owner = lax.broadcasted_iota(jnp.int32, (8, 128), 0) == 4 + lax.div(device, 8)
    small_s[2:4] = narrow[0:2, 0:128]
    small_s[4:5] = jnp.sum(jnp.where(owner, wide[:, 0:128], 0.0), axis=0, keepdims=True)
    recv("bz")
    total = bb[2] + rb[4] + rb[5] + rb[6]
    narrow = pltpu.roll(total, lax.rem(128 - lax.rem(device, 8) * 16, 128), 1)
    for row in range(2):
        owner = lax.broadcasted_iota(jnp.int32, (16, 128), 0) == row * 4 + lax.div(device, 8)
        small_s[row : row + 1] = jnp.sum(jnp.where(owner, narrow, 0.0), axis=0, keepdims=True)
    lane = lax.broadcasted_iota(jnp.int32, (1, 128), 1)
    small_s[5:6] = jnp.where(lane == 0, total[8:9], total[9:10])
    small_s[6:8] = jnp.zeros((2, 128), F32)
    give(small_s, small_o)
    for one in given:
        one.wait()
    for one in sum_batches:
        if one not in waited:
            sent(one) if isinstance(one, str) else sent(*one)


def results_kernel(*refs):
    taken, given, held, ends, sem = refs[:9], refs[9:23], refs[23:32], refs[32:38], refs[38]
    come = [pltpu.make_async_copy(taken[i], held[i], sem.at[i]) for i in range(9)]
    go = [
        pltpu.make_async_copy(held[i], given[i].at[0] if i < 2 else given[i], sem.at[9 + i]) for i in range(8)
    ] + [pltpu.make_async_copy(ends[i], given[8 + i], sem.at[17 + i]) for i in range(6)]
    for one in come[8:] + come[:8]:
        one.start()
    come[8].wait()
    for row, ref in enumerate(ends):
        ref[...] = held[8][row, 0 : ref.shape[0]]
        go[8 + row].start()
    for i in (2, 3, 4, 5, 6, 7, 0, 1):
        come[i].wait()
        go[i].start()
    for one in go:
        one.wait()


def scratch():
    v = pltpu.VMEM
    return [
        v((1, 1024), jnp.int32),
        pltpu.SMEM((1,), jnp.int32),
        pltpu.SMEM((2,), F32),
        *[v((16,), BF)] * 4,
        v((64,), BF),
        v((8, 128), F32),
        v((16, 512), F32),
        v((16, 512), F32),
        v((16, 512), F32),
        v((16, 512), F32),
        v((16, 2048), F32),
        v((64, 512), F32),
        v((8, 128), F32),
        v((1024, 512), BF),
        v((512, 512), BF),
        v((3, 2, 2, 2, 64, 512), BF),
        v((2, 2, 2, 64, 640), BF),
        v((4, 2, 2, 2, 128, 512), BF),
        v((8, 80, 512), BF),
        v((8, 80, 1024), BF),
        v((512, 1024), BF),
        v((8, 1024, 512), F32),
        v((8, 8, 512), F32),
        v((1024, 512), F32),
        v((1024, 512), BF),
        v((512, 512), BF),
        v((512, 512), F32),
        v((512, 512), BF),
        v((512, 512), F32),
        v((512, 512), F32),
        v((512, 512), BF),
        v((512, 512), BF),
        v((512, 512), BF),
        v((2, 2, 128, 1024), F32),
        v((2, 2, 128, 512), F32),
        v((4, 2, 2, 2, 128, 512), F32),
        v((4, 2, 2, 128, 512), F32),
        v((4, 2, 2, 64, 512), BF),
        v((4, 2, 2, 64, 512), BF),
        v((4, 2, 64, 512), BF),
        v((4, 2, 64, 512), BF),
        v((4, 3, 16, 512), BF),
        v((4, 3, 16, 512), BF),
        v((3, 64, 512), BF),
        v((3, 64, 512), BF),
        v((2, 2, 2, 64, 512), F32),
        v((2, 2, 64, 512), F32),
        v((2, 2, 32, 512), BF),
        v((2, 2, 32, 512), BF),
        v((2, 32, 512), BF),
        v((2, 32, 512), BF),
        v((3, 16, 512), BF),
        v((3, 16, 512), BF),
        v((4, 2, 2, 32, 384), BF),
        v((4, 2, 2, 32, 384), BF),
        v((4, 2, 32, 384), BF),
        v((4, 2, 32, 384), BF),
        v((4, 3, 16, 384), BF),
        v((4, 3, 16, 384), BF),
        v((2, 2, 2, 64, 384), F32),
        v((2, 2, 64, 384), F32),
        v((2, 3, 64, 384), BF),
        v((2, 3, 64, 384), BF),
        v((128, 512), F32),
        v((3, 16, 128), F32),
        v((7, 16, 128), F32),
        v((3, 8, 512), F32),
        v((7, 8, 512), F32),
        v((32, 128), BF),
        pltpu.SemaphoreType.DMA((41,)),
        pltpu.SemaphoreType.DMA((80,)),
        pltpu.SemaphoreType.DMA((32,)),
    ]


def on_device(
    tokens,
    segments,
    fill_length,
    query_weight,
    key_weight,
    value_weight,
    output_weight,
    query_bias,
    value_bias,
    output_bias,
    inner_weight,
    inner_bias,
    outer_weight,
    outer_bias,
    residual_gates,
    cotangent,
):
    names = ("dp", "shard")
    several = lax.axis_size("dp") > GROUP
    place = lax.rem(lax.axis_index("dp"), GROUP) * 2 + lax.axis_index("shard")

    def block_of(shard):
        if not several:
            return shard
        whole = lax.all_gather(shard, names, axis=0, tiled=True)
        rows = whole.shape[0] // (2 * GROUP)
        return lax.dynamic_slice_in_dim(whole, place * rows, rows, 0)

    def owned(block):
        if not several:
            return block
        rows = block.shape[0]
        whole = jnp.zeros((rows * 2 * GROUP, *block.shape[1:]), F32)
        whole = lax.dynamic_update_slice_in_dim(whole, block, place * rows, 0)
        return lax.psum_scatter(whole, names, scatter_dimension=0, tiled=True)

    query_weight, key_weight, value_weight, output_weight, inner_weight, outer_weight = map(
        block_of, (query_weight, key_weight, value_weight, output_weight, inner_weight, outer_weight)
    )
    query_bias, value_bias, output_bias, inner_bias, outer_bias = map(
        block_of, (query_bias, value_bias, output_bias, inner_bias, outer_bias)
    )
    hbm = pl.BlockSpec(memory_space=pl.ANY)
    shape = jax.ShapeDtypeStruct
    outs = pl.pallas_call(
        layer_kernel,
        out_shape=[
            shape((512, 512), BF),
            shape((512, 512), F32),
            shape((16, 512), F32),
            shape((16, 512), F32),
            shape((16, 512), F32),
            shape((16, 512), F32),
            shape((16, 2048), F32),
            shape((64, 512), F32),
            shape((8, 128), F32),
        ],
        in_specs=[hbm] * 16,
        out_specs=[hbm] * 9,
        scratch_shapes=scratch(),
        compiler_params=pltpu.CompilerParams(
            collective_id=0, has_side_effects=True, vmem_limit_bytes=VMEM_BYTES
        ),
    )(
        tokens.reshape(512, 512),
        cotangent.reshape(512, 512),
        segments,
        fill_length,
        residual_gates,
        query_bias,
        value_bias,
        output_bias,
        outer_bias,
        inner_bias,
        query_weight,
        key_weight,
        value_weight,
        output_weight,
        inner_weight,
        outer_weight,
    )
    flat = [shape(o.shape, o.dtype) for o in outs[2:8]] + [shape((n,), F32) for n in (16, 16, 16, 16, 64, 2)]
    outs = pl.pallas_call(
        results_kernel,
        out_shape=[shape((1, 512, 512), BF), shape((1, 512, 512), F32)] + flat,
        in_specs=[pl.BlockSpec(memory_space=pltpu.HBM)] * 9,
        out_specs=[hbm] * 14,
        scratch_shapes=[pltpu.VMEM(o.shape, o.dtype) for o in outs]
        + [pltpu.VMEM(o.shape, o.dtype) for o in flat[6:]]
        + [pltpu.SemaphoreType.DMA((23,))],
        compiler_params=pltpu.CompilerParams(vmem_limit_bytes=VMEM_BYTES),
    )(*outs)
    layer, token_grads, gq, gk, gv, go, gi, gout, g_query, g_value, g_output, g_outer, g_inner, gate_sums = outs
    if several:
        gate_sums = lax.psum(jnp.where(place == 0, gate_sums, 0.0), names)
    grads = (gq, gk, gv, go, g_query, g_value, g_output, gi, g_inner, gout, g_outer)
    return (layer, token_grads, *map(owned, grads), gate_sums)


def solution(mesh):
    spread = P(("dp", "shard"))
    return jax.shard_map(
        on_device,
        mesh=mesh,
        in_specs=(
            P("dp", "shard", None),
            P("dp", None),
            P("dp"),
            *([P(("dp", "shard"), None)] * 4),
            *([spread] * 3),
            P(("dp", "shard"), None),
            spread,
            P(("dp", "shard"), None),
            spread,
            P(),
            P("dp", "shard", None),
        ),
        out_specs=(
            P("dp", "shard", None),
            P("dp", "shard", None),
            *([P(("dp", "shard"), None)] * 4),
            *([spread] * 3),
            P(("dp", "shard"), None),
            spread,
            P(("dp", "shard"), None),
            spread,
            P(),
        ),
        check_vma=False,
    )
```

```python
import jax
import jax.numpy as jnp
from jax import lax
from jax.experimental import pallas as pl
from jax.experimental.pallas import tpu as pltpu
from jax.sharding import PartitionSpec as P

MESH = pl.DeviceIdType.MESH
BF = jnp.bfloat16
F32 = jnp.float32
HEADS = 8
GROUP = 16
PAIRS = 4
VMEM_BYTES = 64 * 2**20 - 2**17
PLAN = {
    "fwd0": ("2q2",),
    "fwd1": ("2q3", "1f1", "3q1",),
    "proj1": ("2f0",),
    "fwd2": ("3q2",),
    "fwd3": ("3q3", "1f2",),
    "proj3": ("2f1", "1f3",),
    "fwd6": ("3f0",),
    "outproj": ("2f2",),
    "mid0": ("3f1",),
    "ffn1": ("2f3",),
    "mid1": ("3f2",),
    "ffn2": ("FF0", "3f3",),
    "ffn3": ("FF1",),
    "pre": ("SF0",),
    "bwd0": ("FF2",),
    "bwd1": ("SF1",),
    "bwd2": ("TF0",),
    "bwd3": ("FF3",),
    "fin0": ("SF2",),
    "bwd4": ("TF1",),
    "bwd5": ("FO",),
    "fin1": ("FQ0",),
    "bwd6": ("SF3", "TF2",),
    "bwd7": ("FQ1",),
    "fin2": ("SQ0",),
    "prod7": ("TF3", "EP",),
    "layer": ("SO",),
    "fin3": ("FQ2",),
    "tok3": ("EZ", "TQ0", "SQ1", "TO",),
    "last1": ("TQ1", "TQ2",),
    "start": ("zq2", "1q0", "zq3", "zf0", "1q1", "zf1", "1q2", "zf2", "1q3", "zf3", "2q0", "3q0", "2q1", "1f0",),
}
STEPS = 4


def dot(left, right, left_dim, right_dim):
    return lax.dot_general(
        left, right, (((left_dim,), (right_dim,)), ((), ())), preferred_element_type=F32
    )


def gelu_parts(hidden):
    size = jnp.abs(hidden) * 0.7071067811865476
    recip = 1.0 / (1.0 + 0.3275911 * size)
    expo = jnp.exp(-size * size)
    poly = recip * (
        0.127414796
        + recip * (-0.142248368 + recip * (0.7107068705 + recip * (-0.7265760135 + recip * 0.5307027145)))
    )
    tail = poly * expo
    cdf = jnp.where(hidden >= 0, 1.0 - tail, tail)
    return hidden * cdf, cdf + hidden * expo * 0.3989422804014327


def by_chip(value):
    width = value.shape[-1]
    return value.reshape(4, 8, 16, width).transpose(1, 0, 2, 3).reshape(2, 2, 2, 64, width)


def col_sums(value):
    return dot(jnp.ones((8, value.shape[0]), BF), value, 1, 0)


def layer_kernel(
    tok,
    cot,
    seg_in,
    fill_in,
    gates_in,
    bias_q,
    bias_v,
    bias_o,
    bias_out,
    bias_in,
    wquery,
    wkey,
    wvalue,
    wout_proj,
    win,
    wout,
    layer_o,
    tg_o,
    gq_o,
    gk_o,
    gv_o,
    go_o,
    gi_o,
    gout_o,
    small_o,
    seg,
    fill,
    gates,
    own_q,
    own_v,
    own_o,
    own_out,
    own_in,
    biasf,
    gq_s,
    gk_s,
    gv_s,
    go_s,
    gi_s,
    gout_s,
    small_s,
    xrow,
    cotv,
    wq_rest,
    wq_last,
    wf,
    qt,
    kt,
    vt,
    probs,
    scales,
    st,
    pb,
    mixt,
    attn,
    rlow,
    ffn,
    gres,
    gffn,
    gmixt,
    dqt,
    dkv,
    rkv,
    gf,
    rcf,
    s1f,
    r1f,
    s2f,
    r2f,
    s3f,
    r3f,
    s3o,
    r3o,
    go,
    rco,
    s1o,
    r1o,
    s2o,
    r2o,
    s3w,
    r3w,
    s1q,
    r1q,
    s2q,
    r2q,
    s3q,
    r3q,
    glast,
    rclast,
    s1d,
    r1d,
    ksum,
    bb,
    rb,
    eb,
    re,
    biasb,
    send_sem,
    recv_sem,
    local_sem,
):
    hid, gac = st.at[pl.ds(0, 512)], st.at[pl.ds(512, 512)]
    act, ghid = pb.at[pl.ds(0, 512)], pb.at[pl.ds(512, 512)]
    wq = [wq_rest.at[p] for p in range(PAIRS - 1)] + [wq_last]

    dp = lax.axis_index("dp")
    c = lax.axis_index("shard")
    lo = lax.rem(dp, GROUP)
    z = lax.div(lo, 4)
    y = lax.rem(lax.div(lo, 2), 2)
    x = lax.rem(lo, 2)
    cc, xx, yy = 1 - c, 1 - x, 1 - y

    def zk(k):
        return lax.rem(z + (k % 4), 4)

    zs = [zk(k) for k in range(4)]
    XP = (dp + 1 - 2 * x, c)
    YP = (dp + 2 - 4 * y, c)
    ZP = [None] + [(dp + 4 * (zs[k] - z), c) for k in (1, 2, 3)]
    DP = (dp + 3 - 2 * x - 4 * y, c)
    SB = (dp, cc)

    def rows(place):
        return pl.ds(pl.multiple_of(place * 16, 16), 16)

    def cols(place):
        return pl.ds(pl.multiple_of(place * 512, 512), 512)

    table = {}
    ids = {}

    def same(ref, dev):
        return (ref, ref, dev)

    for p in range(PAIRS):
        for k in (1, 2, 3):
            table["z", ("q", p), k] = lambda p=p, k=k: (
                wq[p].at[y, x, c, pl.ds(0, 16)],
                wq[p].at[y, x, c, pl.ds(k * 16, 16)],
                ZP[k],
            )
        for name, dev in (("x", XP), ("y", YP), ("d", DP)):
            if p == 0 or name != "d":
                for part, (low, count) in enumerate(((0, 16), (16, 48))):
                    table[name, ("q", p), part] = lambda p=p, low=low, count=count, dev=dev: same(
                        wq[p].at[y, x, c, pl.ds(low, count)], dev
                    )
        table["s", ("q", p), 0] = lambda p=p: same(wq[p].at[y, :, c], SB)
        table["s", ("q", p), 1] = lambda p=p: same(wq[p].at[yy, :, c], SB)
        if p:
            table["rx", ("q", p)] = lambda p=p: same(wq[p].at[y, xx, c, pl.ds(0, 32)], YP)
            table["ry", ("q", p)] = lambda p=p: same(wq[p].at[yy, x, c, pl.ds(32, 32)], XP)
    for s in range(STEPS):
        for k in (1, 2, 3):
            table["z", ("f", s), k] = lambda s=s, k=k: (
                win.at[:, cols(zs[(k + s) % 4])],
                wf.at[s, y, x, c, pl.ds(64 + k * 16, 16)],
                ZP[k],
            )
        if s:
            table["zo", ("f", s)] = lambda s=s: (wout, wf.at[s, y, x, c, pl.ds(16, 64)], ZP[4 - s])
        split = 16 if s else 80
        for name, dev in (("x", XP), ("y", YP)):
            for part, (low, count) in enumerate(((0, split), (split, 128 - split))):
                table[name, ("f", s), part] = lambda s=s, low=low, count=count, dev=dev: same(
                    wf.at[s, y, x, c, pl.ds(low, count)], dev
                )
        table["rx", ("f", s)] = lambda s=s: same(wf.at[s, y, xx, c, pl.ds(0, 64)], YP)
        table["ry", ("f", s)] = lambda s=s: same(wf.at[s, yy, x, c, pl.ds(64, 64)], XP)
        table["s", ("f", s), 0] = lambda s=s: same(wf.at[s, y, :, c], SB)
        table["s", ("f", s), 1] = lambda s=s: same(wf.at[s, yy, :, c], SB)
    table["tok"] = lambda: (xrow.at[pl.ds(0, 512)], xrow.at[pl.ds(512, 512)], SB)
    groups = {}
    LAST = (("q", PAIRS - 2), ("q", PAIRS - 1))
    for s in range(STEPS):
        groups["f", s] = (gf.at[s], rcf.at[s], s1f.at[s], r1f.at[s], s2f.at[s], r2f.at[s], s3f.at[s], r3f.at[s])
        if s:
            table["o3", s] = lambda s=s: (s3o.at[s - 1], r3o.at[s - 1], ZP[s])
    groups["o"] = (go, rco, s1o, r1o, s2o, r2o, s3w, r3w)
    for p in range(PAIRS):
        if p < PAIRS - 1:
            gq = gf.at[p, :, :, :, pl.ds(0, 64), pl.ds(0, 384)]
            rcq = rcf.at[p, :, :, pl.ds(0, 64), pl.ds(0, 384)]
        else:
            gq, rcq = glast, rclast
        groups["q", p] = (gq, rcq, s1q.at[p], r1q.at[p], s2q.at[p], r2q.at[p], s3q.at[p], r3q.at[p])
        if p < PAIRS - 1:
            table["kv", p] = lambda p=p: (dkv.at[p % 2, :, :, pl.ds(512, 512)], rkv.at[p % 2], SB)
        else:
            for j in range(2):
                table["kv", p, j] = lambda p=p, j=j: (
                    dkv.at[p % 2, :, pl.ds(j * 64, 64), pl.ds(512, 512)],
                    rkv.at[p % 2, :, pl.ds(j * 64, 64)],
                    SB,
                )
    for g, (grad, rc, s1, r1, s2, r2, s3, r3) in groups.items():
        table["c", g] = lambda grad=grad, rc=rc: (grad.at[:, :, cc], rc, SB)
        if g in LAST:
            for i, dev in enumerate((XP, YP, DP)):
                table["d1", g, i] = lambda i=i, dev=dev, at=LAST.index(g): (s1d.at[at, i], r1d.at[at, i], dev)
            for k in (1, 2, 3):
                table["z3", g, k] = lambda s3=s3, r3=r3, k=k: (s3.at[k - 1], r3.at[k - 1], ZP[k])
            continue
        table["a1", g] = lambda s1=s1, r1=r1: (s1.at[0], r1.at[0], XP)
        table["b1", g] = lambda s1=s1, r1=r1: (s1.at[1], r1.at[1], YP)
        table["a2", g] = lambda s2=s2, r2=r2: (s2.at[0], r2.at[0], YP)
        table["b2", g] = lambda s2=s2, r2=r2: (s2.at[1], r2.at[1], XP)
        for k in (1, 2, 3):
            table["z3", g, k] = lambda s3=s3, r3=r3, k=k: (s3.at[k - 1], r3.at[k - 1], ZP[k])
    for kind, (mine, come) in {"b": (bb, rb), "e": (eb, re)}.items():
        table[kind + "c"] = lambda mine=mine, come=come: (mine.at[0], come.at[0], SB)
        for i, dev in enumerate((XP, YP, DP)):
            table[kind + "p", i] = lambda i=i, dev=dev, mine=mine, come=come: (mine.at[1], come.at[1 + i], dev)
        for k in (1, 2, 3):
            table[kind + "z", k] = lambda k=k, mine=mine, come=come: (mine.at[2], come.at[3 + k], ZP[k])

    def batch(key):
        if not isinstance(key, tuple):
            return key
        kind = {"zo": "z", "rx": "r", "ry": "r", "a1": "1", "b1": "1", "a2": "2", "b2": "2"}.get(key[0], key[0])
        if kind in ("bp", "bz", "ep", "ez", "o3"):
            return kind
        if kind == "z3":
            return "z3" + key[1][0]
        return (kind, key[1])

    for key in table:
        ids.setdefault(batch(key), len(ids))
    weight_batches = [one for one in ids if one[0] in ("z", "x", "y", "d", "r", "s") and isinstance(one, tuple)]
    sum_batches = [one for one in ids if one not in weight_batches and one != "tok"]
    send_ids = {one: i for i, one in enumerate(weight_batches + ["tok"])}
    early = [one for one in weight_batches if one[1][0] == "q"] + [one for one in weight_batches if one[1][0] == "f"]
    late = [("kv", 2), ("kv", 3), "z3q", "bc", "bp", "bz", "ec", "ep", "ez"]
    late += [one for one in sum_batches if isinstance(one[1], tuple) and one[1][0] == "q"]
    for one, place in zip([one for one in sum_batches if one not in late] + late, early):
        send_ids[one] = send_ids[place]
    whole = {"tok": xrow.at[pl.ds(512, 512)]}
    for g in [("q", p) for p in range(PAIRS)] + [("f", s) for s in range(STEPS)]:
        chunk = wq[g[1]] if g[0] == "q" else wf.at[g[1]]
        low = 80 if g == ("f", 0) else 16
        whole["z", g] = chunk.at[y, x, c, pl.ds(low, chunk.shape[3] - low)]
        whole["x", g] = chunk.at[y, xx, c]
        whole["y", g] = chunk.at[yy, x, c]
        whole["d", g] = whole["r", g] = chunk.at[yy, xx, c]
        whole["s", g] = chunk.at[:, :, cc]
    for g, (grad, rc, s1, r1, s2, r2, s3, r3) in groups.items():
        whole["c", g], whole["1", g], whole["2", g] = rc, r1, r2
    for i, g in enumerate(LAST):
        whole["d1", g] = r1d.at[i]
    for p in range(PAIRS):
        whole["kv", p] = rkv.at[p % 2]
    whole |= {"z3f": r3f, "z3q": r3q, "z3o": r3w, "o3": r3o, "bc": rb.at[0], "ec": re.at[0]}
    whole |= {"bp": rb.at[pl.ds(1, 3)], "bz": rb.at[pl.ds(4, 3)], "ep": re.at[pl.ds(1, 3)], "ez": re.at[pl.ds(4, 3)]}

    def start(*key):
        key = key if len(key) > 1 else key[0]
        src, dst, dev = table[key]()
        pltpu.make_async_remote_copy(
            src_ref=src,
            dst_ref=dst,
            send_sem=send_sem.at[send_ids[batch(key)]],
            recv_sem=recv_sem.at[ids[batch(key)]],
            device_id=dev,
            device_id_type=MESH,
        ).start()

    def all_of(one):
        return pltpu.make_async_remote_copy(
            src_ref=whole[one],
            dst_ref=whole[one],
            send_sem=send_sem.at[send_ids[one]],
            recv_sem=recv_sem.at[ids[one]],
            device_id=SB,
            device_id_type=MESH,
        )

    waited = set()

    def recv(*key):
        all_of(key if len(key) > 1 else key[0]).wait_recv()

    def sent(*key):
        one = key if len(key) > 1 else key[0]
        waited.add(one)
        all_of(one).wait_send()

    def natural(ref, firsts, columns):
        parts = [
            ref[:, :, :, pl.ds(pl.multiple_of(firsts(lax.rem(z + 4 - other, 4)), 16), 16), columns]
            for other in range(4)
        ]
        return jnp.concatenate([part.reshape(128, part.shape[-1]) for part in parts], axis=0)

    def attention_block(k):
        return k * 16

    def inner_block(k):
        return jnp.where(k == 0, 0, k * 16 + 64)

    barrier = pltpu.get_barrier_semaphore()
    peers = (XP, YP, DP, ZP[1], ZP[2], ZP[3], SB)
    for dev in peers:
        pl.semaphore_signal(barrier, inc=1, device_id=dev, device_id_type=MESH)

    local = (
        [(tok, xrow.at[pl.ds(0, 512)]), (cot, cotv), (wout, wf.at[0, y, x, c, pl.ds(16, 64)])]
        + [(win.at[:, cols(zs[s])], wf.at[s, y, x, c, pl.ds(0, 16)]) for s in range(STEPS)]
        + [
            (
                ref.at[:, pl.ds(p * 128, 128)],
                (wq[p] if i < 3 or p else wq_last).at[
                    y, x, c, pl.ds(0, 16), pl.ds(i * 128 if i < 3 or p else 512, 128)
                ],
            )
            for p in range(PAIRS)
            for i, ref in enumerate((wquery, wkey, wvalue, wout_proj))
        ]
    )
    local = [pltpu.make_async_copy(src, dst, local_sem.at[i]) for i, (src, dst) in enumerate(local)]
    needed = [(bias_q, own_q), (bias_v, own_v), (bias_o, own_o), (bias_out, own_out), (bias_in, own_in)]
    needed += [(seg_in, seg), (fill_in, fill), (gates_in, gates)]
    needed = [pltpu.make_async_copy(src, dst, local_sem.at[len(local) + i]) for i, (src, dst) in enumerate(needed)]
    for one in needed[:5] + local[7:11] + local[11:] + local[:7] + needed[5:]:
        one.start()

    biasf[...] = jnp.zeros((8, 128), F32)
    for one in needed[:5]:
        one.wait()
    for row, ref in enumerate((own_q, own_v, own_o, own_out, own_in)):
        count = ref.shape[0]
        biasf[row : row + 1, 0:count] = ref[...].astype(F32).reshape(1, count)
    packed = jnp.sum(pltpu.roll(biasf[...], 0, 1, stride=16, stride_axis=0), axis=0, keepdims=True)
    first = lax.broadcasted_iota(jnp.int32, (16, 128), 0) == 0
    own_bias = jnp.where(first, jnp.broadcast_to(packed, (16, 128)), 0.0)
    wq[0][y, x, c, pl.ds(0, 16), pl.ds(384, 128)] = own_bias.astype(BF)
    for one in local[7:11]:
        one.wait()
    pl.semaphore_wait(barrier, len(peers))

    def send_z(g):
        for k in (3, 2, 1):
            start("z", g, k)
        if g[0] == "f" and g[1]:
            start("zo", g)

    def neighbours(g):
        return ("x", "y", "d") if g == ("q", 0) else ("x", "y")

    def send_early(g):
        for name in neighbours(g):
            start(name, g, 0)

    def send_plane(g):
        recv("z", g)
        for name in neighbours(g):
            start(name, g, 1)
        if g == ("q", 0):
            for s in (1, 2, 3):
                send_early(F[s])

    def send_relay(g):
        for name in ("x", "y"):
            recv(name, g)
            if g != ("q", 0):
                start("r" + name, g)
            if name == "x":
                start("s", g, 0)

    def send_across(g):
        if g == ("q", 0):
            recv("d", g)
        else:
            recv("r", g)
        start("s", g, 1)

    def all_here(g):
        recv("s", g)

    Q, F = [("q", p) for p in range(PAIRS)], [("f", s) for s in range(STEPS)]
    send_z(Q[0])
    send_early(Q[0])
    for one in local[11:]:
        one.wait()
    send_z(Q[1])
    local[0].wait()
    start("tok")
    for p in (1, 2, 3):
        send_early(Q[p])
    for one in local[2:7]:
        one.wait()
    send_early(F[0])

    for one in needed[5:]:
        one.wait()
    kind = lax.broadcasted_iota(jnp.int32, (16, 512), 0)
    at_own = lax.broadcasted_iota(jnp.int32, (16, 512), 1) + c * 512
    at_sib = lax.broadcasted_iota(jnp.int32, (16, 512), 1) + cc * 512
    own_seg = seg[:, pl.ds(pl.multiple_of(c * 512, 512), 512)]
    sib_seg = seg[:, pl.ds(pl.multiple_of(cc * 512, 512), 512)]
    used = fill[0]
    for half, (segs, spot) in enumerate(((own_seg, at_own), (sib_seg, at_sib))):
        unused = jnp.where(spot >= used, 1.0, 0.0)
        marks = jnp.where(kind == 8, unused, jnp.where(kind == segs, 1.0, 0.0)).astype(BF)
        for head in range(HEADS):
            kt[head, 64:80, half * 512 : half * 512 + 512] = marks
    barred = jnp.where((kind == own_seg) | (kind > 8), 0.0, -1e30).astype(BF)
    for head in range(HEADS):
        qt[head, 64:80] = barred

    gate_attn = gates[0]
    gate_feed = gates[1]
    local[1].wait()
    upstream = cotv[...].astype(F32)
    gffn[...] = (gate_feed * upstream).astype(BF)

    def small_plane():
        recv("ec")
        eb[1] = eb[0] + re[0]
        for i in range(3):
            start("ep", i)

    def small_column():
        recv("ep")
        eb[2] = eb[1] + (re[1] + re[2] + re[3])
        for k in (1, 2, 3):
            start("ez", k)

    def take(name):
        if name in ("EP", "EZ"):
            done.append(name)
            return small_plane() if name == "EP" else small_column()
        kind, g = name[0], ({"q": "q", "f": "f", "Q": "q", "F": "f"}.get(name[1]), int(name[2:] or 0))
        if name[1] == "O":
            g = "o"
        if name in done:
            raise ValueError(name)
        done.append(name)
        if kind == "z":
            send_z(g)
        elif kind == "1":
            send_plane(g)
        elif kind == "2":
            send_relay(g)
        elif kind == "3":
            send_across(g)
        elif kind == "F":
            fold_plane(g) if g in LAST else fold_first(g)
        elif kind == "S":
            fold_second(g)
        elif g in LAST:
            fold_column(g)
        elif g == "o":
            fold_third(g)
            go_s[...] = ksum[rows(z), :]
        elif g[0] == "f":
            ffn_third(g[1])
        else:
            q_third(g[1])

    done, given = [], []

    def give(held, out):
        one = pltpu.make_async_copy(held, out, local_sem.at[len(given)])
        one.start()
        given.append(one)

    def at_point(name):
        for one in PLAN.get(name, ()):
            take(one)

    at_point("start")
    recv("tok")
    all_here(Q[0])

    held = natural(wq[0], attention_block, slice(384, 512)).reshape(32, 16, 128)
    biasb[...] = jnp.sum(held.astype(F32), axis=1).astype(BF)

    def bias_row(offset, per, width):
        lane = lax.broadcasted_iota(jnp.int32, (128, width), 0)
        at = lax.broadcasted_iota(jnp.int32, (128, width), 1)
        pick = (lane == offset + (at & (per - 1))).astype(F32).astype(BF)
        spread = dot(biasb[...], pick, 1, 0)
        owner = lax.broadcasted_iota(jnp.int32, (32, width), 0)
        at = lax.broadcasted_iota(jnp.int32, (32, width), 1)
        return jnp.sum(jnp.where(owner == lax.shift_right_logical(at, per.bit_length() - 1), spread, 0.0), axis=0, keepdims=True)

    first_row = lax.broadcasted_iota(jnp.int32, (16, 512), 0) == 0
    ones_row = jnp.where(first_row, 1.0, 0.0).astype(BF)

    def as_rank_one(row):
        return jnp.where(first_row, jnp.broadcast_to(row, (16, 512)), 0.0).astype(BF)

    bias_q = as_rank_one(bias_row(0, 16, 512))
    bias_v = as_rank_one(bias_row(16, 16, 512))

    def project(p):
        weights = natural(wq[p], attention_block, slice(0, 384))
        ours = dot(weights, xrow[0:512], 0, 1)
        theirs = dot(weights[:, 128:384], xrow[512:1024], 0, 1)
        at = slice(p * 128, p * 128 + 128)
        grown = ours[0:128] + dot(bias_q[:, at], ones_row, 0, 0)
        grown = (grown.astype(BF).astype(F32) * 0.125).astype(BF)
        add_v = dot(bias_v[:, at], ones_row, 0, 0)
        for j in range(2):
            part = slice(j * 64, j * 64 + 64)
            qt[p * 2 + j, 0:64] = grown[part]
            kt[p * 2 + j, 0:64, 0:512] = ours[128 + j * 64 : 192 + j * 64].astype(BF)
            kt[p * 2 + j, 0:64, 512:1024] = theirs[part].astype(BF)
        vt[at, 0:512] = (ours[256:384] + add_v).astype(BF)
        vt[at, 512:1024] = (theirs[128:256] + add_v).astype(BF)

    def half_of(unit):
        return unit // 2, slice(unit % 2 * 256, unit % 2 * 256 + 256)

    def scores_of(unit):
        head, lanes = half_of(unit)
        raw = dot(kt[head], qt[head, :, lanes], 0, 0)
        own = kt[head, 0:64, lanes].astype(F32) * qt[head, 0:64, lanes].astype(F32)
        own = jnp.sum(own, axis=0, keepdims=True)
        highest = jnp.full((8, 256), -jnp.inf, F32)
        for b in range(8):
            r = slice(b * 128, b * 128 + 128)
            block = raw[r]
            if b // 2 == unit % 2 and b < 4:
                diagonal = lax.broadcasted_iota(jnp.int32, (128, 256), 1) == (
                    lax.broadcasted_iota(jnp.int32, (128, 256), 0) + b % 2 * 128
                )
                block = jnp.where(diagonal, own, block)
            st[r, lanes] = block
            highest = jnp.maximum(highest, jnp.max(block.reshape(16, 8, 256), axis=0))
        return jnp.max(highest, axis=0, keepdims=True)

    def attend(unit, highest):
        head, lanes = half_of(unit)
        total = jnp.zeros((8, 256), F32)
        for b in range(8):
            r = slice(b * 128, b * 128 + 128)
            expo = jnp.exp(st[r, lanes] - highest)
            probs[head, r, lanes] = expo
            total = total + jnp.sum(expo.reshape(16, 8, 256), axis=0)
        scale = 1.0 / jnp.sum(total, axis=0, keepdims=True)
        scales[head, :, lanes] = jnp.broadcast_to(scale, (8, 256))
        for b in range(8):
            r = slice(b * 128, b * 128 + 128)
            pb[r, lanes] = (probs[head, r, lanes] * scale).astype(BF)
        at = slice(head * 64, head * 64 + 64)
        mixt[at, lanes] = dot(vt[at], pb[:, lanes], 1, 0).astype(BF)

    for head in range(HEADS):
        first = head * 2
        if head % 2 == 0:
            if head:
                at_point("proj%d" % (head // 2))
                all_here(Q[head // 2])
            project(head // 2)
        at_point("fwd%d" % head)
        if head % 2 == 0:
            highest = scores_of(first)
        later = scores_of(first + 1)
        attend(first, highest)
        if head % 2 == 0:
            highest = scores_of(first + 2)
        attend(first + 1, later)

    at_point("outproj")
    sent("tok")
    for one in weight_batches:
        if one[1][0] == "q":
            sent(*one)
    out_weight = jnp.concatenate(
        [natural(wq_last, attention_block, slice(512, 640))] + [natural(wq[p], attention_block, slice(384, 512)) for p in (1, 2, 3)], axis=1
    )
    attn[...] = dot(mixt[...], out_weight, 0, 0) + bias_row(32, 16, 512)
    resid = xrow[0:512].astype(F32) + gate_attn * attn[...]
    rlow[...] = resid.astype(BF)
    ffn[...] = jnp.zeros((512, 512), F32)
    gres[...] = cotv[...].astype(F32)

    def fold_first(g):
        grad, rc, s1 = groups[g][:3]
        half = rc.shape[2] // 2
        recv("c", g)
        for i in range(2):
            s1[0, i] = (grad[i, xx, c, 0:half] + rc[i, xx, 0:half]).astype(BF)
            s1[1, i] = (grad[yy, i, c, half : 2 * half] + rc[yy, i, half : 2 * half]).astype(BF)
        start("a1", g)
        start("b1", g)

    def fold_second(g):
        grad, rc, s1, r1, s2, r2 = groups[g][:6]
        half = rc.shape[2] // 2
        recv("1", g)
        s2[0] = (grad[yy, x, c, 0:half] + rc[yy, x, 0:half] + r1[0, yy].astype(F32)).astype(BF)
        start("a2", g)
        s2[1] = (
            grad[y, xx, c, half : 2 * half] + rc[y, xx, half : 2 * half] + r1[1, xx].astype(F32)
        ).astype(BF)
        start("b2", g)

    def fold_third(g):
        grad, rc, s1, r1, s2, r2, s3, r3 = groups[g]
        half = rc.shape[2] // 2
        width = rc.shape[3]
        recv("2", g)
        upper = grad[y, x, c, 0:half] + rc[y, x, 0:half] + r1[0, y].astype(F32) + r2[0].astype(F32)
        ksum[0:half, 0:width] = upper
        lower = (
            grad[y, x, c, half : 2 * half]
            + rc[y, x, half : 2 * half]
            + r1[1, x].astype(F32)
            + r2[1].astype(F32)
        )
        ksum[half : 2 * half, 0:width] = lower
        for k in (1, 2, 3):
            s3[k - 1] = ksum[rows(zs[k]), 0:width].astype(BF)
            start("z3", g, k)

    def ffn_third(s):
        fold_third(("f", s))
        gi_s[:, cols(zs[s])] = ksum[rows(z), :]
        if s:
            s3o[s - 1] = ksum[64:128].astype(BF)
            start("o3", s)
        else:
            gout_s[...] = ksum[64:128]

    def small(row, value):
        eb[0, row : row + 1, :] = value

    bb[0] = jnp.zeros((16, 128), F32)
    eb[0] = jnp.zeros((8, 512), F32)

    def ffn_step(s):
        all_here(F[s])
        inner = natural(wf.at[s], inner_block, slice(0, 512))
        outer = wf[s, :, :, :, 16:80].reshape(512, 512)
        hid[...] = dot(rlow[...], inner, 1, 0) + chunk_bias[s]
        gac[...] = dot(gffn[...], outer, 1, 1)
        for b in range(8):
            r = slice(b * 64, b * 64 + 64)
            value, slope = gelu_parts(hid[r])
            act[r] = value.astype(BF)
            ghid[r] = (gac[r] * slope).astype(BF)
        at_point("mid%d" % s)
        ffn[...] += dot(act[...], outer, 1, 0)
        gf[s, :, :, :, 64:128] = dot(act[...], gffn[...], 0, 0).reshape(2, 2, 2, 64, 512)
        gf[s, :, :, :, 0:64] = by_chip(dot(rlow[...], ghid[...], 0, 0))
        start("c", ("f", s))
        gres[...] += dot(ghid[...], inner, 1, 1)
        sums = col_sums(ghid[...])[0:1]
        for row in range(4):
            eb[0, 4 + row : 5 + row, :] = jnp.where(zs[s] == row, sums, eb[0, 4 + row : 5 + row, :])

    inner_bias = bias_row(64, 64, 2048)
    parts = [inner_bias[:, i * 512 : i * 512 + 512] for i in range(4)]
    chunk_bias = []
    for s in range(STEPS):
        picked = parts[3]
        for i in range(3):
            picked = jnp.where(zs[s] == i, parts[i], picked)
        chunk_bias.append(picked)
    for s in range(STEPS):
        at_point("ffn%d" % s)
        ffn_step(s)
    at_point("pre")

    for one in weight_batches:
        if one[1][0] == "f":
            sent(*one)

    small(1, col_sums(gffn[...])[0:1])
    gattn = (gate_attn * gres[...]).astype(BF)
    small(0, col_sums(gattn)[0:1])
    start("ec")
    go[...] = by_chip(dot(mixt[...], gattn, 1, 0))
    start("c", "o")
    gmixt[...] = dot(out_weight, gattn, 1, 1).astype(BF)
    def finish_layer():
        ffn[...] += bias_row(48, 16, 512)
        upstream = cotv[...].astype(F32)
        resid = xrow[0:512].astype(F32) + gate_attn * attn[...]
        rlow[...] = (resid + gate_feed * ffn[...]).astype(BF)
        give(rlow, layer_o)
        feed_part = jnp.sum(jnp.sum(upstream * ffn[...], axis=0, keepdims=True), axis=1, keepdims=True)
        bb[0, 9:10] = jnp.broadcast_to(feed_part, (1, 128))
        attn_part = jnp.sum(jnp.sum(gres[...] * attn[...], axis=0, keepdims=True), axis=1, keepdims=True)
        bb[0, 8:9] = jnp.broadcast_to(attn_part, (1, 128))


    def scores_back(unit):
        head, lanes = half_of(unit)
        at = slice(head * 64, head * 64 + 64)
        raw = dot(vt[at], gmixt[at, lanes], 0, 0)
        total = jnp.zeros((8, 256), F32)
        for b in range(8):
            r = slice(b * 128, b * 128 + 128)
            block = raw[r]
            st[r, lanes] = block
            total = total + jnp.sum((probs[head, r, lanes] * block).reshape(16, 8, 256), axis=0)
        return jnp.sum(total, axis=0, keepdims=True) * scales[head, 0:1, lanes]

    def slopes_of(unit, inner):
        head, lanes = half_of(unit)
        scale = scales[head, 0:1, lanes]
        slot = head % 2 * 2
        for b in range(8):
            r = slice(b * 128, b * 128 + 128)
            prob = probs[head, r, lanes] * scale
            place = (b // 4, b // 2 % 2, b % 2, slice(None), lanes)
            wf[(slot, *place)] = prob.astype(BF)
            wf[(slot + 1, *place)] = (prob * (st[r, lanes] - inner)).astype(BF)

    def products_of(head):
        at = slice(head * 64, head * 64 + 64)
        slot = head % 2 * 2
        prob, slope = (wf[i].reshape(1024, 512) for i in (slot, slot + 1))
        place = (head // 2 % 2, slice(None), slice(head % 2 * 64, head % 2 * 64 + 64))
        dkv[place[0], 0, place[2]] = dot(qt[head, 0:64], slope, 1, 1)
        dkv[place[0], 1, place[2]] = dot(gmixt[at], prob, 1, 1)
        if head >= 6:
            assert "FQ1" in done
            start("kv", 3, head - 6)
        dqt[at] = (dot(kt[head, 0:64], slope, 1, 0) * 0.125).astype(BF)

    def finish_pair(p):
        slot = p % 2
        at = slice(p * 128, p * 128 + 128)
        recv("kv", p)
        vt[at, 0:512] = (dkv[slot, 0, :, 0:512] + rkv[slot, 0]).astype(BF)
        vt[at, 512:1024] = (dkv[slot, 1, :, 0:512] + rkv[slot, 1]).astype(BF)
        both = jnp.concatenate([dqt[at], vt[at, 0:512], vt[at, 512:1024]], axis=0)
        if p < PAIRS - 1:
            sent("c", F[p])
            gf[p, :, :, :, 0:64, 0:384] = by_chip(dot(xrow[0:512], both, 0, 1))
        else:
            glast[...] = by_chip(dot(xrow[0:512], both, 0, 1))
        start("c", Q[p])
        sums = dot(jnp.ones((8, 512), BF), both, 1, 1)
        bb[0, p : p + 1] = sums[0:1, 0:128]
        bb[0, 4 + p : 5 + p] = sums[0:1, 256:384]

    def token_part(p):
        at = slice(p * 128, p * 128 + 128)
        both = jnp.concatenate([dqt[at], vt[at, 0:512], vt[at, 512:1024]], axis=0)
        gres[...] += dot(both, natural(wq[p], attention_block, slice(0, 384)), 0, 1)

    def fold_plane(g):
        grad, rc = groups[g][:2]
        recv("c", g)
        for i, (yi, xi) in enumerate(((y, xx), (yy, x), (yy, xx))):
            s1d[LAST.index(g), i] = (grad[yi, xi, c] + rc[yi, xi]).astype(BF)
            start("d1", g, i)

    def fold_column(g):
        grad, rc, s3 = groups[g][0], groups[g][1], groups[g][6]
        recv("d1", g)
        come = r1d.at[LAST.index(g)]
        ksum[0:64, 0:384] = (
            grad[y, x, c] + rc[y, x] + (come[0].astype(F32) + come[1].astype(F32) + come[2].astype(F32))
        )
        for k in (1, 2, 3):
            s3[k - 1] = ksum[rows(zs[k]), 0:384].astype(BF)
            start("z3", g, k)
        keep_pair(g[1])

    def q_third(p):
        fold_third(Q[p])
        keep_pair(p)

    def keep_pair(p):
        at = slice(p * 128, p * 128 + 128)
        gq_s[:, at] = ksum[rows(z), 0:128]
        gk_s[:, at] = ksum[rows(z), 128:256]
        gv_s[:, at] = ksum[rows(z), 256:384]

    inner = scores_back(0)
    for head in range(HEADS):
        at_point("bwd%d" % head)
        if head in (5, 7):
            sent("kv", (head - 5) // 2)
        if head:
            products_of(head - 1)
        if head in (2, 4, 6):
            p = head // 2 - 1
            assert "TF%d" % p in done and (p < 2 or "FQ%d" % (p - 2) in done)
            start("kv", p)
        later = scores_back(head * 2 + 1)
        slopes_of(head * 2, inner)
        if head < HEADS - 1:
            inner = scores_back(head * 2 + 2)
        slopes_of(head * 2 + 1, later)
        if head in (3, 5, 7):
            p = head // 2 - 1
            at_point("fin%d" % p)
            finish_pair(p)
    at_point("prod7")
    products_of(HEADS - 1)
    at_point("layer")
    finish_layer()
    at_point("fin3")
    finish_pair(3)

    start("bc")
    at_point("tok3")
    fold_plane(Q[3])
    recv("bc")
    bb[1] = bb[0] + rb[0]
    for i in range(3):
        start("bp", i)
    at_point("tok")
    for p in range(PAIRS):
        token_part(p)
    give(gres, tg_o)

    def q_last(p):
        at = slice(p * 128, p * 128 + 128)
        more = r3q[p, 0].astype(F32) + r3q[p, 1].astype(F32) + r3q[p, 2].astype(F32)
        gq_s[:, at] += more[:, 0:128]
        gk_s[:, at] += more[:, 128:256]
        gv_s[:, at] += more[:, 256:384]

    at_point("last1")
    fold_column(Q[3])
    at_point("last2")
    recv("bp")
    bb[2] = bb[1] + (rb[1] + rb[2] + rb[3])
    for k in (1, 2, 3):
        start("bz", k)
    assert len(done) == 55

    recv("z3f")
    for s in range(STEPS):
        more = r3f[(s + 1) % 4, 0].astype(F32)
        for k in (2, 3):
            more = more + r3f[(s + k) % 4, k - 1].astype(F32)
        gi_s[:, cols(zs[s])] += more
    give(gi_s, gi_o)
    recv("o3")
    for s in (1, 2, 3):
        gout_s[...] += r3o[s - 1].astype(F32)
    give(gout_s, gout_o)
    recv("z3o")
    for k in (1, 2, 3):
        go_s[...] += r3w[k - 1].astype(F32)
    give(go_s, go_o)
    recv("ez")
    total = eb[2] + re[4] + re[5] + re[6]
    device = lo * 2 + c
    narrow = pltpu.roll(total, lax.rem(512 - device * 16, 512), 1)
    wide = pltpu.roll(total, lax.rem(512 - lax.rem(device, 8) * 64, 512), 1)
    owner = lax.broadcasted_iota(jnp.int32, (8, 128), 0) == 4 + lax.div(device, 8)
    small_s[2:4] = narrow[0:2, 0:128]
    small_s[4:5] = jnp.sum(jnp.where(owner, wide[:, 0:128], 0.0), axis=0, keepdims=True)
    recv("z3q")
    for p in range(PAIRS):
        q_last(p)
    give(gq_s, gq_o)
    give(gk_s, gk_o)
    give(gv_s, gv_o)
    recv("bz")
    total = bb[2] + rb[4] + rb[5] + rb[6]
    narrow = pltpu.roll(total, lax.rem(128 - lax.rem(device, 8) * 16, 128), 1)
    for row in range(2):
        owner = lax.broadcasted_iota(jnp.int32, (16, 128), 0) == row * 4 + lax.div(device, 8)
        small_s[row : row + 1] = jnp.sum(jnp.where(owner, narrow, 0.0), axis=0, keepdims=True)
    lane = lax.broadcasted_iota(jnp.int32, (1, 128), 1)
    small_s[5:6] = jnp.where(lane == 0, total[8:9], total[9:10])
    small_s[6:8] = jnp.zeros((2, 128), F32)
    give(small_s, small_o)
    for one in sum_batches:
        if one not in waited:
            sent(one) if isinstance(one, str) else sent(*one)
    for one in given:
        one.wait()


def results_kernel(*refs):
    taken, given, held, ends, sem = refs[:9], refs[9:23], refs[23:32], refs[32:38], refs[38]
    moves = []
    for i in (8, 2, 3, 4, 5, 6, 7, 0, 1):
        rows, parts = taken[i].shape[0], {0: 2, 1: 4}.get(i, 1)
        for part in range(parts):
            at = pl.ds(part * rows // parts, rows // parts)
            there = None if i == 8 else (given[i].at[0] if i < 2 else given[i]).at[at]
            moves.append((taken[i].at[at], held[i].at[at], there))
    come = [pltpu.make_async_copy(src, mid, sem.at[n]) for n, (src, mid, _) in enumerate(moves)]
    for one in come:
        one.start()
    go = []
    for n, (_, mid, dst) in enumerate(moves):
        come[n].wait()
        if n == 0:
            for row, ref in enumerate(ends):
                ref[...] = held[8][row, 0 : ref.shape[0]]
                go.append(pltpu.make_async_copy(ref, given[8 + row], sem.at[len(moves) + row]))
                go[-1].start()
        else:
            go.append(pltpu.make_async_copy(mid, dst, sem.at[len(moves) + 6 + n]))
            go[-1].start()
    for one in go:
        one.wait()


def scratch():
    v = pltpu.VMEM
    return [
        v((1, 1024), jnp.int32),
        pltpu.SMEM((1,), jnp.int32),
        pltpu.SMEM((2,), F32),
        *[v((16,), BF)] * 4,
        v((64,), BF),
        v((8, 128), F32),
        v((16, 512), F32),
        v((16, 512), F32),
        v((16, 512), F32),
        v((16, 512), F32),
        v((16, 2048), F32),
        v((64, 512), F32),
        v((8, 128), F32),
        v((1024, 512), BF),
        v((512, 512), BF),
        v((3, 2, 2, 2, 64, 512), BF),
        v((2, 2, 2, 64, 640), BF),
        v((4, 2, 2, 2, 128, 512), BF),
        v((8, 80, 512), BF),
        v((8, 80, 1024), BF),
        v((512, 1024), BF),
        v((8, 1024, 512), F32),
        v((8, 8, 512), F32),
        v((1024, 512), F32),
        v((1024, 512), BF),
        v((512, 512), BF),
        v((512, 512), F32),
        v((512, 512), BF),
        v((512, 512), F32),
        v((512, 512), F32),
        v((512, 512), BF),
        v((512, 512), BF),
        v((512, 512), BF),
        v((2, 2, 128, 1024), F32),
        v((2, 2, 128, 512), F32),
        v((4, 2, 2, 2, 128, 512), F32),
        v((4, 2, 2, 128, 512), F32),
        v((4, 2, 2, 64, 512), BF),
        v((4, 2, 2, 64, 512), BF),
        v((4, 2, 64, 512), BF),
        v((4, 2, 64, 512), BF),
        v((4, 3, 16, 512), BF),
        v((4, 3, 16, 512), BF),
        v((3, 64, 512), BF),
        v((3, 64, 512), BF),
        v((2, 2, 2, 64, 512), F32),
        v((2, 2, 64, 512), F32),
        v((2, 2, 32, 512), BF),
        v((2, 2, 32, 512), BF),
        v((2, 32, 512), BF),
        v((2, 32, 512), BF),
        v((3, 16, 512), BF),
        v((3, 16, 512), BF),
        v((4, 2, 2, 32, 384), BF),
        v((4, 2, 2, 32, 384), BF),
        v((4, 2, 32, 384), BF),
        v((4, 2, 32, 384), BF),
        v((4, 3, 16, 384), BF),
        v((4, 3, 16, 384), BF),
        v((2, 2, 2, 64, 384), F32),
        v((2, 2, 64, 384), F32),
        v((2, 3, 64, 384), BF),
        v((2, 3, 64, 384), BF),
        v((128, 512), F32),
        v((3, 16, 128), F32),
        v((7, 16, 128), F32),
        v((3, 8, 512), F32),
        v((7, 8, 512), F32),
        v((32, 128), BF),
        pltpu.SemaphoreType.DMA((41,)),
        pltpu.SemaphoreType.DMA((80,)),
        pltpu.SemaphoreType.DMA((32,)),
    ]


def on_device(
    tokens,
    segments,
    fill_length,
    query_weight,
    key_weight,
    value_weight,
    output_weight,
    query_bias,
    value_bias,
    output_bias,
    inner_weight,
    inner_bias,
    outer_weight,
    outer_bias,
    residual_gates,
    cotangent,
):
    names = ("dp", "shard")
    several = lax.axis_size("dp") > GROUP
    place = lax.rem(lax.axis_index("dp"), GROUP) * 2 + lax.axis_index("shard")

    def block_of(shard):
        if not several:
            return shard
        whole = lax.all_gather(shard, names, axis=0, tiled=True)
        rows = whole.shape[0] // (2 * GROUP)
        return lax.dynamic_slice_in_dim(whole, place * rows, rows, 0)

    def owned(block):
        if not several:
            return block
        rows = block.shape[0]
        whole = jnp.zeros((rows * 2 * GROUP, *block.shape[1:]), F32)
        whole = lax.dynamic_update_slice_in_dim(whole, block, place * rows, 0)
        return lax.psum_scatter(whole, names, scatter_dimension=0, tiled=True)

    query_weight, key_weight, value_weight, output_weight, inner_weight, outer_weight = map(
        block_of, (query_weight, key_weight, value_weight, output_weight, inner_weight, outer_weight)
    )
    query_bias, value_bias, output_bias, inner_bias, outer_bias = map(
        block_of, (query_bias, value_bias, output_bias, inner_bias, outer_bias)
    )
    hbm = pl.BlockSpec(memory_space=pl.ANY)
    shape = jax.ShapeDtypeStruct
    outs = pl.pallas_call(
        layer_kernel,
        out_shape=[
            shape((512, 512), BF),
            shape((512, 512), F32),
            shape((16, 512), F32),
            shape((16, 512), F32),
            shape((16, 512), F32),
            shape((16, 512), F32),
            shape((16, 2048), F32),
            shape((64, 512), F32),
            shape((8, 128), F32),
        ],
        in_specs=[hbm] * 16,
        out_specs=[hbm] * 9,
        scratch_shapes=scratch(),
        compiler_params=pltpu.CompilerParams(
            collective_id=0, has_side_effects=True, vmem_limit_bytes=VMEM_BYTES
        ),
    )(
        tokens.reshape(512, 512),
        cotangent.reshape(512, 512),
        segments,
        fill_length,
        residual_gates,
        query_bias,
        value_bias,
        output_bias,
        outer_bias,
        inner_bias,
        query_weight,
        key_weight,
        value_weight,
        output_weight,
        inner_weight,
        outer_weight,
    )
    flat = [shape(o.shape, o.dtype) for o in outs[2:8]] + [shape((n,), F32) for n in (16, 16, 16, 16, 64, 2)]
    outs = pl.pallas_call(
        results_kernel,
        out_shape=[shape((1, 512, 512), BF), shape((1, 512, 512), F32)] + flat,
        in_specs=[pl.BlockSpec(memory_space=pltpu.HBM)] * 9,
        out_specs=[hbm] * 14,
        scratch_shapes=[pltpu.VMEM(o.shape, o.dtype) for o in outs]
        + [pltpu.VMEM(o.shape, o.dtype) for o in flat[6:]]
        + [pltpu.SemaphoreType.DMA((33,))],
        compiler_params=pltpu.CompilerParams(vmem_limit_bytes=VMEM_BYTES),
    )(*outs)
    layer, token_grads, gq, gk, gv, go, gi, gout, g_query, g_value, g_output, g_outer, g_inner, gate_sums = outs
    if several:
        gate_sums = lax.psum(jnp.where(place == 0, gate_sums, 0.0), names)
    grads = (gq, gk, gv, go, g_query, g_value, g_output, gi, g_inner, gout, g_outer)
    return (layer, token_grads, *map(owned, grads), gate_sums)


def solution(mesh):
    spread = P(("dp", "shard"))
    return jax.shard_map(
        on_device,
        mesh=mesh,
        in_specs=(
            P("dp", "shard", None),
            P("dp", None),
            P("dp"),
            *([P(("dp", "shard"), None)] * 4),
            *([spread] * 3),
            P(("dp", "shard"), None),
            spread,
            P(("dp", "shard"), None),
            spread,
            P(),
            P("dp", "shard", None),
        ),
        out_specs=(
            P("dp", "shard", None),
            P("dp", "shard", None),
            *([P(("dp", "shard"), None)] * 4),
            *([spread] * 3),
            P(("dp", "shard"), None),
            spread,
            P(("dp", "shard"), None),
            spread,
            P(),
        ),
        check_vma=False,
    )
```

```python
import jax
import jax.numpy as jnp
from jax import lax
from jax.experimental import pallas as pl
from jax.experimental.pallas import tpu as pltpu
from jax.sharding import PartitionSpec as P

MESH = pl.DeviceIdType.MESH
BF = jnp.bfloat16
F32 = jnp.float32
HEADS = 8
GROUP = 16
PAIRS = 4
VMEM_BYTES = 64 * 2**20 - 2**17
PLAN = {
    "fwd0": ("2q2",),
    "fwd1": ("2q3", "1f1", "3q1",),
    "proj1": ("2f0",),
    "fwd2": ("3q2",),
    "fwd3": ("3q3", "1f2",),
    "proj3": ("2f1", "1f3",),
    "fwd6": ("3f0",),
    "outproj": ("2f2",),
    "mid0": ("3f1",),
    "ffn1": ("2f3",),
    "mid1": ("3f2",),
    "ffn2": ("FF0", "3f3",),
    "ffn3": ("FF1",),
    "pre": ("SF0",),
    "bwd0": ("FF2",),
    "bwd1": ("SF1",),
    "bwd2": ("TF0",),
    "bwd3": ("FF3",),
    "fin0": ("SF2",),
    "bwd4": ("TF1",),
    "bwd5": ("FO",),
    "fin1": ("FQ0",),
    "bwd6": ("SF3", "TF2",),
    "bwd7": ("FQ1",),
    "fin2": ("SQ0",),
    "prod7": ("TF3",),
    "layer": ("EP", "SO",),
    "fin3": ("FQ2",),
    "tok3": ("EZ", "TQ0", "SQ1", "TO",),
    "last1": ("TQ1", "TQ2",),
    "start": ("zq2", "1q0", "zq3", "zf0", "1q1", "zf1", "1q2", "zf2", "1q3", "zf3", "2q0", "3q0", "2q1", "1f0",),
}
STEPS = 4


def dot(left, right, left_dim, right_dim):
    return lax.dot_general(
        left, right, (((left_dim,), (right_dim,)), ((), ())), preferred_element_type=F32
    )


def gelu_parts(hidden):
    size = jnp.abs(hidden) * 0.7071067811865476
    recip = 1.0 / (1.0 + 0.3275911 * size)
    expo = jnp.exp(-size * size)
    poly = recip * (
        0.127414796
        + recip * (-0.142248368 + recip * (0.7107068705 + recip * (-0.7265760135 + recip * 0.5307027145)))
    )
    tail = poly * expo
    cdf = jnp.where(hidden >= 0, 1.0 - tail, tail)
    return hidden * cdf, cdf + hidden * expo * 0.3989422804014327


def by_chip(value):
    width = value.shape[-1]
    return value.reshape(4, 8, 16, width).transpose(1, 0, 2, 3).reshape(2, 2, 2, 64, width)


def col_sums(value):
    return dot(jnp.ones((8, value.shape[0]), BF), value, 1, 0)


def layer_kernel(
    tok,
    cot,
    seg_in,
    fill_in,
    gates_in,
    bias_q,
    bias_v,
    bias_o,
    bias_out,
    bias_in,
    wquery,
    wkey,
    wvalue,
    wout_proj,
    win,
    wout,
    layer_o,
    tg_o,
    gq_o,
    gk_o,
    gv_o,
    go_o,
    gi_o,
    gout_o,
    small_o,
    seg,
    fill,
    gates,
    own_q,
    own_v,
    own_o,
    own_out,
    own_in,
    biasf,
    gq_s,
    gk_s,
    gv_s,
    go_s,
    gi_s,
    gout_s,
    small_s,
    xrow,
    cotv,
    wq_rest,
    wq_last,
    wf,
    qt,
    kt,
    vt,
    probs,
    scales,
    st,
    pb,
    mixt,
    attn,
    rlow,
    ffn,
    gres,
    gffn,
    gmixt,
    dqt,
    dkv,
    rkv,
    gf,
    rcf,
    s1f,
    r1f,
    s2f,
    r2f,
    s3f,
    r3f,
    s3o,
    r3o,
    go,
    rco,
    s1o,
    r1o,
    s2o,
    r2o,
    s3w,
    r3w,
    s1q,
    r1q,
    s2q,
    r2q,
    s3q,
    r3q,
    glast,
    rclast,
    s1d,
    r1d,
    ksum,
    bb,
    rb,
    eb,
    re,
    biasb,
    send_sem,
    recv_sem,
    local_sem,
):
    hid, gac = st.at[pl.ds(0, 512)], st.at[pl.ds(512, 512)]
    act, ghid = pb.at[pl.ds(0, 512)], pb.at[pl.ds(512, 512)]
    wq = [wq_rest.at[p] for p in range(PAIRS - 1)] + [wq_last]

    dp = lax.axis_index("dp")
    c = lax.axis_index("shard")
    lo = lax.rem(dp, GROUP)
    z = lax.div(lo, 4)
    y = lax.rem(lax.div(lo, 2), 2)
    x = lax.rem(lo, 2)
    cc, xx, yy = 1 - c, 1 - x, 1 - y

    def zk(k):
        return lax.rem(z + (k % 4), 4)

    zs = [zk(k) for k in range(4)]
    XP = (dp + 1 - 2 * x, c)
    YP = (dp + 2 - 4 * y, c)
    ZP = [None] + [(dp + 4 * (zs[k] - z), c) for k in (1, 2, 3)]
    DP = (dp + 3 - 2 * x - 4 * y, c)
    SB = (dp, cc)

    def rows(place):
        return pl.ds(pl.multiple_of(place * 16, 16), 16)

    def cols(place):
        return pl.ds(pl.multiple_of(place * 512, 512), 512)

    table = {}
    ids = {}

    def same(ref, dev):
        return (ref, ref, dev)

    for p in range(PAIRS):
        for k in (1, 2, 3):
            table["z", ("q", p), k] = lambda p=p, k=k: (
                wq[p].at[y, x, c, pl.ds(0, 16)],
                wq[p].at[y, x, c, pl.ds(k * 16, 16)],
                ZP[k],
            )
        for name, dev in (("x", XP), ("y", YP), ("d", DP)):
            if p == 0 or name != "d":
                for part, (low, count) in enumerate(((0, 16), (16, 48))):
                    table[name, ("q", p), part] = lambda p=p, low=low, count=count, dev=dev: same(
                        wq[p].at[y, x, c, pl.ds(low, count)], dev
                    )
        table["s", ("q", p), 0] = lambda p=p: same(wq[p].at[y, :, c], SB)
        table["s", ("q", p), 1] = lambda p=p: same(wq[p].at[yy, :, c], SB)
        if p:
            table["rx", ("q", p)] = lambda p=p: same(wq[p].at[y, xx, c, pl.ds(0, 32)], YP)
            table["ry", ("q", p)] = lambda p=p: same(wq[p].at[yy, x, c, pl.ds(32, 32)], XP)
    for s in range(STEPS):
        for k in (1, 2, 3):
            table["z", ("f", s), k] = lambda s=s, k=k: (
                win.at[:, cols(zs[(k + s) % 4])],
                wf.at[s, y, x, c, pl.ds(64 + k * 16, 16)],
                ZP[k],
            )
        if s:
            table["zo", ("f", s)] = lambda s=s: (wout, wf.at[s, y, x, c, pl.ds(16, 64)], ZP[4 - s])
        split = 16 if s else 80
        for name, dev in (("x", XP), ("y", YP)):
            for part, (low, count) in enumerate(((0, split), (split, 128 - split))):
                table[name, ("f", s), part] = lambda s=s, low=low, count=count, dev=dev: same(
                    wf.at[s, y, x, c, pl.ds(low, count)], dev
                )
        table["rx", ("f", s)] = lambda s=s: same(wf.at[s, y, xx, c, pl.ds(0, 64)], YP)
        table["ry", ("f", s)] = lambda s=s: same(wf.at[s, yy, x, c, pl.ds(64, 64)], XP)
        table["s", ("f", s), 0] = lambda s=s: same(wf.at[s, y, :, c], SB)
        table["s", ("f", s), 1] = lambda s=s: same(wf.at[s, yy, :, c], SB)
    table["tok"] = lambda: (xrow.at[pl.ds(0, 512)], xrow.at[pl.ds(512, 512)], SB)
    groups = {}
    LAST = (("q", PAIRS - 2), ("q", PAIRS - 1))
    for s in range(STEPS):
        groups["f", s] = (gf.at[s], rcf.at[s], s1f.at[s], r1f.at[s], s2f.at[s], r2f.at[s], s3f.at[s], r3f.at[s])
        if s:
            table["o3", s] = lambda s=s: (s3o.at[s - 1], r3o.at[s - 1], ZP[s])
    groups["o"] = (go, rco, s1o, r1o, s2o, r2o, s3w, r3w)
    for p in range(PAIRS):
        if p < PAIRS - 1:
            gq = gf.at[p, :, :, :, pl.ds(0, 64), pl.ds(0, 384)]
            rcq = rcf.at[p, :, :, pl.ds(0, 64), pl.ds(0, 384)]
        else:
            gq, rcq = glast, rclast
        groups["q", p] = (gq, rcq, s1q.at[p], r1q.at[p], s2q.at[p], r2q.at[p], s3q.at[p], r3q.at[p])
        if p < PAIRS - 1:
            table["kv", p] = lambda p=p: (dkv.at[p % 2, :, :, pl.ds(512, 512)], rkv.at[p % 2], SB)
        else:
            for j in range(2):
                table["kv", p, j] = lambda p=p, j=j: (
                    dkv.at[p % 2, :, pl.ds(j * 64, 64), pl.ds(512, 512)],
                    rkv.at[p % 2, :, pl.ds(j * 64, 64)],
                    SB,
                )
    for g, (grad, rc, s1, r1, s2, r2, s3, r3) in groups.items():
        table["c", g] = lambda grad=grad, rc=rc: (grad.at[:, :, cc], rc, SB)
        if g in LAST:
            for i, dev in enumerate((XP, YP, DP)):
                table["d1", g, i] = lambda i=i, dev=dev, at=LAST.index(g): (s1d.at[at, i], r1d.at[at, i], dev)
            for k in (1, 2, 3):
                table["z3", g, k] = lambda s3=s3, r3=r3, k=k: (s3.at[k - 1], r3.at[k - 1], ZP[k])
            continue
        table["a1", g] = lambda s1=s1, r1=r1: (s1.at[0], r1.at[0], XP)
        table["b1", g] = lambda s1=s1, r1=r1: (s1.at[1], r1.at[1], YP)
        table["a2", g] = lambda s2=s2, r2=r2: (s2.at[0], r2.at[0], YP)
        table["b2", g] = lambda s2=s2, r2=r2: (s2.at[1], r2.at[1], XP)
        for k in (1, 2, 3):
            table["z3", g, k] = lambda s3=s3, r3=r3, k=k: (s3.at[k - 1], r3.at[k - 1], ZP[k])
    for kind, (mine, come) in {"b": (bb, rb), "e": (eb, re)}.items():
        table[kind + "c"] = lambda mine=mine, come=come: (mine.at[0], come.at[0], SB)
        for i, dev in enumerate((XP, YP, DP)):
            table[kind + "p", i] = lambda i=i, dev=dev, mine=mine, come=come: (mine.at[1], come.at[1 + i], dev)
        for k in (1, 2, 3):
            table[kind + "z", k] = lambda k=k, mine=mine, come=come: (mine.at[2], come.at[3 + k], ZP[k])

    def batch(key):
        if not isinstance(key, tuple):
            return key
        kind = {"zo": "z", "rx": "r", "ry": "r", "a1": "1", "b1": "1", "a2": "2", "b2": "2"}.get(key[0], key[0])
        if kind in ("bp", "bz", "ep", "ez", "o3"):
            return kind
        if kind == "z3":
            return "z3" + key[1][0]
        return (kind, key[1])

    for key in table:
        ids.setdefault(batch(key), len(ids))
    weight_batches = [one for one in ids if one[0] in ("z", "x", "y", "d", "r", "s") and isinstance(one, tuple)]
    sum_batches = [one for one in ids if one not in weight_batches and one != "tok"]
    send_ids = {one: i for i, one in enumerate(weight_batches + ["tok"])}
    early = [one for one in weight_batches if one[1][0] == "q"] + [one for one in weight_batches if one[1][0] == "f"]
    late = [("kv", 2), ("kv", 3), "z3q", "bc", "bp", "bz", "ec", "ep", "ez"]
    late += [one for one in sum_batches if isinstance(one[1], tuple) and one[1][0] == "q"]
    for one, place in zip([one for one in sum_batches if one not in late] + late, early):
        send_ids[one] = send_ids[place]
    whole = {"tok": xrow.at[pl.ds(512, 512)]}
    for g in [("q", p) for p in range(PAIRS)] + [("f", s) for s in range(STEPS)]:
        chunk = wq[g[1]] if g[0] == "q" else wf.at[g[1]]
        low = 80 if g == ("f", 0) else 16
        whole["z", g] = chunk.at[y, x, c, pl.ds(low, chunk.shape[3] - low)]
        whole["x", g] = chunk.at[y, xx, c]
        whole["y", g] = chunk.at[yy, x, c]
        whole["d", g] = whole["r", g] = chunk.at[yy, xx, c]
        whole["s", g] = chunk.at[:, :, cc]
    for g, (grad, rc, s1, r1, s2, r2, s3, r3) in groups.items():
        whole["c", g], whole["1", g], whole["2", g] = rc, r1, r2
    for i, g in enumerate(LAST):
        whole["d1", g] = r1d.at[i]
    for p in range(PAIRS):
        whole["kv", p] = rkv.at[p % 2]
    whole |= {"z3f": r3f, "z3q": r3q, "z3o": r3w, "o3": r3o, "bc": rb.at[0], "ec": re.at[0]}
    whole |= {"bp": rb.at[pl.ds(1, 3)], "bz": rb.at[pl.ds(4, 3)], "ep": re.at[pl.ds(1, 3)], "ez": re.at[pl.ds(4, 3)]}

    def start(*key):
        key = key if len(key) > 1 else key[0]
        src, dst, dev = table[key]()
        pltpu.make_async_remote_copy(
            src_ref=src,
            dst_ref=dst,
            send_sem=send_sem.at[send_ids[batch(key)]],
            recv_sem=recv_sem.at[ids[batch(key)]],
            device_id=dev,
            device_id_type=MESH,
        ).start()

    def all_of(one):
        return pltpu.make_async_remote_copy(
            src_ref=whole[one],
            dst_ref=whole[one],
            send_sem=send_sem.at[send_ids[one]],
            recv_sem=recv_sem.at[ids[one]],
            device_id=SB,
            device_id_type=MESH,
        )

    waited = set()

    def recv(*key):
        all_of(key if len(key) > 1 else key[0]).wait_recv()

    def sent(*key):
        one = key if len(key) > 1 else key[0]
        waited.add(one)
        all_of(one).wait_send()

    def natural(ref, firsts, columns):
        parts = [
            ref[:, :, :, pl.ds(pl.multiple_of(firsts(lax.rem(z + 4 - other, 4)), 16), 16), columns]
            for other in range(4)
        ]
        return jnp.concatenate([part.reshape(128, part.shape[-1]) for part in parts], axis=0)

    def attention_block(k):
        return k * 16

    def inner_block(k):
        return jnp.where(k == 0, 0, k * 16 + 64)

    barrier = pltpu.get_barrier_semaphore()
    peers = (XP, YP, DP, ZP[1], ZP[2], ZP[3], SB)
    for dev in peers:
        pl.semaphore_signal(barrier, inc=1, device_id=dev, device_id_type=MESH)

    local = (
        [(tok, xrow.at[pl.ds(0, 512)]), (cot, cotv), (wout, wf.at[0, y, x, c, pl.ds(16, 64)])]
        + [(win.at[:, cols(zs[s])], wf.at[s, y, x, c, pl.ds(0, 16)]) for s in range(STEPS)]
        + [
            (
                ref.at[:, pl.ds(p * 128, 128)],
                (wq[p] if i < 3 or p else wq_last).at[
                    y, x, c, pl.ds(0, 16), pl.ds(i * 128 if i < 3 or p else 512, 128)
                ],
            )
            for p in range(PAIRS)
            for i, ref in enumerate((wquery, wkey, wvalue, wout_proj))
        ]
    )
    local = [pltpu.make_async_copy(src, dst, local_sem.at[i]) for i, (src, dst) in enumerate(local)]
    needed = [(bias_q, own_q), (bias_v, own_v), (bias_o, own_o), (bias_out, own_out), (bias_in, own_in)]
    needed += [(seg_in, seg), (fill_in, fill), (gates_in, gates)]
    needed = [pltpu.make_async_copy(src, dst, local_sem.at[len(local) + i]) for i, (src, dst) in enumerate(needed)]
    for one in needed[:5] + local[7:11] + local[11:] + local[:7] + needed[5:]:
        one.start()

    biasf[...] = jnp.zeros((8, 128), F32)
    for one in needed[:5]:
        one.wait()
    for row, ref in enumerate((own_q, own_v, own_o, own_out, own_in)):
        count = ref.shape[0]
        biasf[row : row + 1, 0:count] = ref[...].astype(F32).reshape(1, count)
    packed = jnp.sum(pltpu.roll(biasf[...], 0, 1, stride=16, stride_axis=0), axis=0, keepdims=True)
    first = lax.broadcasted_iota(jnp.int32, (16, 128), 0) == 0
    own_bias = jnp.where(first, jnp.broadcast_to(packed, (16, 128)), 0.0)
    wq[0][y, x, c, pl.ds(0, 16), pl.ds(384, 128)] = own_bias.astype(BF)
    for one in local[7:11]:
        one.wait()
    pl.semaphore_wait(barrier, len(peers))

    def send_z(g):
        for k in (3, 2, 1):
            start("z", g, k)
        if g[0] == "f" and g[1]:
            start("zo", g)

    def neighbours(g):
        return ("x", "y", "d") if g == ("q", 0) else ("x", "y")

    def send_early(g):
        for name in neighbours(g):
            start(name, g, 0)

    def send_plane(g):
        recv("z", g)
        for name in neighbours(g):
            start(name, g, 1)
        if g == ("q", 0):
            for s in (1, 2, 3):
                send_early(F[s])

    def send_relay(g):
        for name in ("x", "y"):
            recv(name, g)
            if g != ("q", 0):
                start("r" + name, g)
            if name == "x":
                start("s", g, 0)

    def send_across(g):
        if g == ("q", 0):
            recv("d", g)
        else:
            recv("r", g)
        start("s", g, 1)

    def all_here(g):
        recv("s", g)

    Q, F = [("q", p) for p in range(PAIRS)], [("f", s) for s in range(STEPS)]
    send_z(Q[0])
    send_early(Q[0])
    for one in local[11:]:
        one.wait()
    send_z(Q[1])
    local[0].wait()
    start("tok")
    for p in (1, 2, 3):
        send_early(Q[p])
    for one in local[2:7]:
        one.wait()
    send_early(F[0])

    for one in needed[5:]:
        one.wait()
    kind = lax.broadcasted_iota(jnp.int32, (16, 512), 0)
    at_own = lax.broadcasted_iota(jnp.int32, (16, 512), 1) + c * 512
    at_sib = lax.broadcasted_iota(jnp.int32, (16, 512), 1) + cc * 512
    own_seg = seg[:, pl.ds(pl.multiple_of(c * 512, 512), 512)]
    sib_seg = seg[:, pl.ds(pl.multiple_of(cc * 512, 512), 512)]
    used = fill[0]
    for half, (segs, spot) in enumerate(((own_seg, at_own), (sib_seg, at_sib))):
        unused = jnp.where(spot >= used, 1.0, 0.0)
        marks = jnp.where(kind == 8, unused, jnp.where(kind == segs, 1.0, 0.0)).astype(BF)
        for head in range(HEADS):
            kt[head, 64:80, half * 512 : half * 512 + 512] = marks
    barred = jnp.where((kind == own_seg) | (kind > 8), 0.0, -1e30).astype(BF)
    for head in range(HEADS):
        qt[head, 64:80] = barred

    gate_attn = gates[0]
    gate_feed = gates[1]
    local[1].wait()
    upstream = cotv[...].astype(F32)
    gffn[...] = (gate_feed * upstream).astype(BF)

    def small_plane():
        recv("ec")
        eb[1] = eb[0] + re[0]
        for i in range(3):
            start("ep", i)

    def small_column():
        recv("ep")
        eb[2] = eb[1] + (re[1] + re[2] + re[3])
        for k in (1, 2, 3):
            start("ez", k)

    def take(name):
        if name in ("EP", "EZ"):
            done.append(name)
            return small_plane() if name == "EP" else small_column()
        kind, g = name[0], ({"q": "q", "f": "f", "Q": "q", "F": "f"}.get(name[1]), int(name[2:] or 0))
        if name[1] == "O":
            g = "o"
        if name in done:
            raise ValueError(name)
        done.append(name)
        if kind == "z":
            send_z(g)
        elif kind == "1":
            send_plane(g)
        elif kind == "2":
            send_relay(g)
        elif kind == "3":
            send_across(g)
        elif kind == "F":
            fold_plane(g) if g in LAST else fold_first(g)
        elif kind == "S":
            fold_second(g)
        elif g in LAST:
            fold_column(g)
        elif g == "o":
            fold_third(g)
            go_s[...] = ksum[rows(z), :]
        elif g[0] == "f":
            ffn_third(g[1])
        else:
            q_third(g[1])

    done, given = [], []

    def give(held, out):
        one = pltpu.make_async_copy(held, out, local_sem.at[len(given)])
        one.start()
        given.append(one)

    def at_point(name):
        for one in PLAN.get(name, ()):
            take(one)

    at_point("start")
    recv("tok")
    all_here(Q[0])

    held = natural(wq[0], attention_block, slice(384, 512)).reshape(32, 16, 128)
    biasb[...] = jnp.sum(held.astype(F32), axis=1).astype(BF)

    def bias_row(offset, per, width):
        lane = lax.broadcasted_iota(jnp.int32, (128, width), 0)
        at = lax.broadcasted_iota(jnp.int32, (128, width), 1)
        pick = (lane == offset + (at & (per - 1))).astype(F32).astype(BF)
        spread = dot(biasb[...], pick, 1, 0)
        owner = lax.broadcasted_iota(jnp.int32, (32, width), 0)
        at = lax.broadcasted_iota(jnp.int32, (32, width), 1)
        return jnp.sum(jnp.where(owner == lax.shift_right_logical(at, per.bit_length() - 1), spread, 0.0), axis=0, keepdims=True)

    first_row = lax.broadcasted_iota(jnp.int32, (16, 512), 0) == 0
    ones_row = jnp.where(first_row, 1.0, 0.0).astype(BF)

    def as_rank_one(row):
        return jnp.where(first_row, jnp.broadcast_to(row, (16, 512)), 0.0).astype(BF)

    bias_q = as_rank_one(bias_row(0, 16, 512))
    bias_v = as_rank_one(bias_row(16, 16, 512))

    def project(p):
        weights = natural(wq[p], attention_block, slice(0, 384))
        ours = dot(weights, xrow[0:512], 0, 1)
        theirs = dot(weights[:, 128:384], xrow[512:1024], 0, 1)
        at = slice(p * 128, p * 128 + 128)
        grown = ours[0:128] + dot(bias_q[:, at], ones_row, 0, 0)
        grown = (grown.astype(BF).astype(F32) * 0.125).astype(BF)
        add_v = dot(bias_v[:, at], ones_row, 0, 0)
        for j in range(2):
            part = slice(j * 64, j * 64 + 64)
            qt[p * 2 + j, 0:64] = grown[part]
            kt[p * 2 + j, 0:64, 0:512] = ours[128 + j * 64 : 192 + j * 64].astype(BF)
            kt[p * 2 + j, 0:64, 512:1024] = theirs[part].astype(BF)
        vt[at, 0:512] = (ours[256:384] + add_v).astype(BF)
        vt[at, 512:1024] = (theirs[128:256] + add_v).astype(BF)

    def half_of(unit):
        return unit // 2, slice(unit % 2 * 256, unit % 2 * 256 + 256)

    def scores_of(unit):
        head, lanes = half_of(unit)
        raw = dot(kt[head], qt[head, :, lanes], 0, 0)
        own = kt[head, 0:64, lanes].astype(F32) * qt[head, 0:64, lanes].astype(F32)
        own = jnp.sum(own, axis=0, keepdims=True)
        highest = jnp.full((8, 256), -jnp.inf, F32)
        for b in range(8):
            r = slice(b * 128, b * 128 + 128)
            block = raw[r]
            if b // 2 == unit % 2 and b < 4:
                diagonal = lax.broadcasted_iota(jnp.int32, (128, 256), 1) == (
                    lax.broadcasted_iota(jnp.int32, (128, 256), 0) + b % 2 * 128
                )
                block = jnp.where(diagonal, own, block)
            st[r, lanes] = block
            highest = jnp.maximum(highest, jnp.max(block.reshape(16, 8, 256), axis=0))
        return jnp.max(highest, axis=0, keepdims=True)

    def attend(unit, highest):
        head, lanes = half_of(unit)
        total = jnp.zeros((8, 256), F32)
        for b in range(8):
            r = slice(b * 128, b * 128 + 128)
            expo = jnp.exp(st[r, lanes] - highest)
            probs[head, r, lanes] = expo
            total = total + jnp.sum(expo.reshape(16, 8, 256), axis=0)
        scale = 1.0 / jnp.sum(total, axis=0, keepdims=True)
        scales[head, :, lanes] = jnp.broadcast_to(scale, (8, 256))
        for b in range(8):
            r = slice(b * 128, b * 128 + 128)
            pb[r, lanes] = (probs[head, r, lanes] * scale).astype(BF)
        at = slice(head * 64, head * 64 + 64)
        mixt[at, lanes] = dot(vt[at], pb[:, lanes], 1, 0).astype(BF)

    for head in range(HEADS):
        first = head * 2
        if head % 2 == 0:
            if head:
                at_point("proj%d" % (head // 2))
                all_here(Q[head // 2])
            project(head // 2)
        at_point("fwd%d" % head)
        if head % 2 == 0:
            highest = scores_of(first)
        later = scores_of(first + 1)
        attend(first, highest)
        if head % 2 == 0:
            highest = scores_of(first + 2)
        attend(first + 1, later)

    at_point("outproj")
    sent("tok")
    for one in weight_batches:
        if one[1][0] == "q":
            sent(*one)
    out_weight = jnp.concatenate(
        [natural(wq_last, attention_block, slice(512, 640))] + [natural(wq[p], attention_block, slice(384, 512)) for p in (1, 2, 3)], axis=1
    )
    attn[...] = dot(mixt[...], out_weight, 0, 0) + bias_row(32, 16, 512)
    resid = xrow[0:512].astype(F32) + gate_attn * attn[...]
    rlow[...] = resid.astype(BF)
    ffn[...] = jnp.zeros((512, 512), F32)
    gres[...] = cotv[...].astype(F32)

    def fold_first(g):
        grad, rc, s1 = groups[g][:3]
        half = rc.shape[2] // 2
        recv("c", g)
        for i in range(2):
            s1[0, i] = (grad[i, xx, c, 0:half] + rc[i, xx, 0:half]).astype(BF)
            s1[1, i] = (grad[yy, i, c, half : 2 * half] + rc[yy, i, half : 2 * half]).astype(BF)
        start("a1", g)
        start("b1", g)

    def fold_second(g):
        grad, rc, s1, r1, s2, r2 = groups[g][:6]
        half = rc.shape[2] // 2
        recv("1", g)
        s2[0] = (grad[yy, x, c, 0:half] + rc[yy, x, 0:half] + r1[0, yy].astype(F32)).astype(BF)
        start("a2", g)
        s2[1] = (
            grad[y, xx, c, half : 2 * half] + rc[y, xx, half : 2 * half] + r1[1, xx].astype(F32)
        ).astype(BF)
        start("b2", g)

    def fold_third(g):
        grad, rc, s1, r1, s2, r2, s3, r3 = groups[g]
        half = rc.shape[2] // 2
        width = rc.shape[3]
        recv("2", g)
        upper = grad[y, x, c, 0:half] + rc[y, x, 0:half] + r1[0, y].astype(F32) + r2[0].astype(F32)
        ksum[0:half, 0:width] = upper
        lower = (
            grad[y, x, c, half : 2 * half]
            + rc[y, x, half : 2 * half]
            + r1[1, x].astype(F32)
            + r2[1].astype(F32)
        )
        ksum[half : 2 * half, 0:width] = lower
        for k in (1, 2, 3):
            s3[k - 1] = ksum[rows(zs[k]), 0:width].astype(BF)
            start("z3", g, k)

    def ffn_third(s):
        fold_third(("f", s))
        gi_s[:, cols(zs[s])] = ksum[rows(z), :]
        if s:
            s3o[s - 1] = ksum[64:128].astype(BF)
            start("o3", s)
        else:
            gout_s[...] = ksum[64:128]

    def small(row, value):
        eb[0, row : row + 1, :] = value

    bb[0] = jnp.zeros((16, 128), F32)
    eb[0] = jnp.zeros((8, 512), F32)

    def ffn_step(s):
        all_here(F[s])
        inner = natural(wf.at[s], inner_block, slice(0, 512))
        outer = wf[s, :, :, :, 16:80].reshape(512, 512)
        hid[...] = dot(rlow[...], inner, 1, 0) + chunk_bias[s]
        gac[...] = dot(gffn[...], outer, 1, 1)
        for b in range(8):
            r = slice(b * 64, b * 64 + 64)
            value, slope = gelu_parts(hid[r])
            act[r] = value.astype(BF)
            ghid[r] = (gac[r] * slope).astype(BF)
        at_point("mid%d" % s)
        ffn[...] += dot(act[...], outer, 1, 0)
        gf[s, :, :, :, 64:128] = dot(act[...], gffn[...], 0, 0).reshape(2, 2, 2, 64, 512)
        gf[s, :, :, :, 0:64] = by_chip(dot(rlow[...], ghid[...], 0, 0))
        start("c", ("f", s))
        gres[...] += dot(ghid[...], inner, 1, 1)
        sums = col_sums(ghid[...])[0:1]
        for row in range(4):
            eb[0, 4 + row : 5 + row, :] = jnp.where(zs[s] == row, sums, eb[0, 4 + row : 5 + row, :])

    inner_bias = bias_row(64, 64, 2048)
    parts = [inner_bias[:, i * 512 : i * 512 + 512] for i in range(4)]
    chunk_bias = []
    for s in range(STEPS):
        picked = parts[3]
        for i in range(3):
            picked = jnp.where(zs[s] == i, parts[i], picked)
        chunk_bias.append(picked)
    for s in range(STEPS):
        at_point("ffn%d" % s)
        ffn_step(s)
    at_point("pre")

    for one in weight_batches:
        if one[1][0] == "f":
            sent(*one)

    small(1, col_sums(gffn[...])[0:1])
    gattn = (gate_attn * gres[...]).astype(BF)
    small(0, col_sums(gattn)[0:1])
    start("ec")
    go[...] = by_chip(dot(mixt[...], gattn, 1, 0))
    start("c", "o")
    gmixt[...] = dot(out_weight, gattn, 1, 1).astype(BF)
    def finish_layer():
        ffn[...] += bias_row(48, 16, 512)
        upstream = cotv[...].astype(F32)
        resid = xrow[0:512].astype(F32) + gate_attn * attn[...]
        rlow[...] = (resid + gate_feed * ffn[...]).astype(BF)
        give(rlow, layer_o)
        feed_part = jnp.sum(jnp.sum(upstream * ffn[...], axis=0, keepdims=True), axis=1, keepdims=True)
        bb[0, 9:10] = jnp.broadcast_to(feed_part, (1, 128))
        attn_part = jnp.sum(jnp.sum(gres[...] * attn[...], axis=0, keepdims=True), axis=1, keepdims=True)
        bb[0, 8:9] = jnp.broadcast_to(attn_part, (1, 128))


    def scores_back(unit):
        head, lanes = half_of(unit)
        at = slice(head * 64, head * 64 + 64)
        raw = dot(vt[at], gmixt[at, lanes], 0, 0)
        total = jnp.zeros((8, 256), F32)
        for b in range(8):
            r = slice(b * 128, b * 128 + 128)
            block = raw[r]
            st[r, lanes] = block
            total = total + jnp.sum((probs[head, r, lanes] * block).reshape(16, 8, 256), axis=0)
        return jnp.sum(total, axis=0, keepdims=True) * scales[head, 0:1, lanes]

    def slopes_of(unit, inner):
        head, lanes = half_of(unit)
        scale = scales[head, 0:1, lanes]
        slot = head % 2 * 2
        for b in range(8):
            r = slice(b * 128, b * 128 + 128)
            prob = probs[head, r, lanes] * scale
            place = (b // 4, b // 2 % 2, b % 2, slice(None), lanes)
            wf[(slot, *place)] = prob.astype(BF)
            wf[(slot + 1, *place)] = (prob * (st[r, lanes] - inner)).astype(BF)

    def products_of(head):
        at = slice(head * 64, head * 64 + 64)
        slot = head % 2 * 2
        prob, slope = (wf[i].reshape(1024, 512) for i in (slot, slot + 1))
        place = (head // 2 % 2, slice(None), slice(head % 2 * 64, head % 2 * 64 + 64))
        dkv[place[0], 0, place[2]] = dot(qt[head, 0:64], slope, 1, 1)
        dkv[place[0], 1, place[2]] = dot(gmixt[at], prob, 1, 1)
        if head >= 6:
            assert "FQ1" in done
            start("kv", 3, head - 6)
        dqt[at] = (dot(kt[head, 0:64], slope, 1, 0) * 0.125).astype(BF)

    def finish_pair(p):
        slot = p % 2
        at = slice(p * 128, p * 128 + 128)
        recv("kv", p)
        vt[at, 0:512] = (dkv[slot, 0, :, 0:512] + rkv[slot, 0]).astype(BF)
        vt[at, 512:1024] = (dkv[slot, 1, :, 0:512] + rkv[slot, 1]).astype(BF)
        both = jnp.concatenate([dqt[at], vt[at, 0:512], vt[at, 512:1024]], axis=0)
        if p < PAIRS - 1:
            sent("c", F[p])
            gf[p, :, :, :, 0:64, 0:384] = by_chip(dot(xrow[0:512], both, 0, 1))
        else:
            glast[...] = by_chip(dot(xrow[0:512], both, 0, 1))
        start("c", Q[p])
        sums = dot(jnp.ones((8, 512), BF), both, 1, 1)
        bb[0, p : p + 1] = sums[0:1, 0:128]
        bb[0, 4 + p : 5 + p] = sums[0:1, 256:384]

    def token_part(p):
        at = slice(p * 128, p * 128 + 128)
        both = jnp.concatenate([dqt[at], vt[at, 0:512], vt[at, 512:1024]], axis=0)
        gres[...] += dot(both, natural(wq[p], attention_block, slice(0, 384)), 0, 1)

    def fold_plane(g):
        grad, rc = groups[g][:2]
        recv("c", g)
        for i, (yi, xi) in enumerate(((y, xx), (yy, x), (yy, xx))):
            s1d[LAST.index(g), i] = (grad[yi, xi, c] + rc[yi, xi]).astype(BF)
            start("d1", g, i)

    def fold_column(g):
        grad, rc, s3 = groups[g][0], groups[g][1], groups[g][6]
        recv("d1", g)
        come = r1d.at[LAST.index(g)]
        ksum[0:64, 0:384] = (
            grad[y, x, c] + rc[y, x] + (come[0].astype(F32) + come[1].astype(F32) + come[2].astype(F32))
        )
        for k in (1, 2, 3):
            s3[k - 1] = ksum[rows(zs[k]), 0:384].astype(BF)
            start("z3", g, k)
        keep_pair(g[1])

    def q_third(p):
        fold_third(Q[p])
        keep_pair(p)

    def keep_pair(p):
        at = slice(p * 128, p * 128 + 128)
        gq_s[:, at] = ksum[rows(z), 0:128]
        gk_s[:, at] = ksum[rows(z), 128:256]
        gv_s[:, at] = ksum[rows(z), 256:384]

    inner = scores_back(0)
    for head in range(HEADS):
        at_point("bwd%d" % head)
        if head in (5, 7):
            sent("kv", (head - 5) // 2)
        if head:
            products_of(head - 1)
        if head in (2, 4, 6):
            p = head // 2 - 1
            assert "TF%d" % p in done and (p < 2 or "FQ%d" % (p - 2) in done)
            start("kv", p)
        later = scores_back(head * 2 + 1)
        slopes_of(head * 2, inner)
        if head < HEADS - 1:
            inner = scores_back(head * 2 + 2)
        slopes_of(head * 2 + 1, later)
        if head in (3, 5, 7):
            p = head // 2 - 1
            at_point("fin%d" % p)
            finish_pair(p)
    at_point("prod7")
    products_of(HEADS - 1)
    at_point("layer")
    finish_layer()
    at_point("fin3")
    finish_pair(3)

    start("bc")
    at_point("tok3")
    fold_plane(Q[3])
    recv("bc")
    bb[1] = bb[0] + rb[0]
    for i in range(3):
        start("bp", i)
    at_point("tok")
    for p in range(PAIRS):
        token_part(p)
    give(gres, tg_o)

    def q_last(p):
        at = slice(p * 128, p * 128 + 128)
        more = r3q[p, 0].astype(F32) + r3q[p, 1].astype(F32) + r3q[p, 2].astype(F32)
        gq_s[:, at] += more[:, 0:128]
        gk_s[:, at] += more[:, 128:256]
        gv_s[:, at] += more[:, 256:384]

    at_point("last1")
    fold_column(Q[3])
    at_point("last2")
    recv("bp")
    bb[2] = bb[1] + (rb[1] + rb[2] + rb[3])
    for k in (1, 2, 3):
        start("bz", k)
    assert len(done) == 55

    recv("z3f")
    for s in range(STEPS):
        more = r3f[(s + 1) % 4, 0].astype(F32)
        for k in (2, 3):
            more = more + r3f[(s + k) % 4, k - 1].astype(F32)
        gi_s[:, cols(zs[s])] += more
    give(gi_s, gi_o)
    recv("o3")
    for s in (1, 2, 3):
        gout_s[...] += r3o[s - 1].astype(F32)
    give(gout_s, gout_o)
    recv("z3o")
    for k in (1, 2, 3):
        go_s[...] += r3w[k - 1].astype(F32)
    give(go_s, go_o)
    recv("ez")
    total = eb[2] + re[4] + re[5] + re[6]
    device = lo * 2 + c
    narrow = pltpu.roll(total, lax.rem(512 - device * 16, 512), 1)
    wide = pltpu.roll(total, lax.rem(512 - lax.rem(device, 8) * 64, 512), 1)
    owner = lax.broadcasted_iota(jnp.int32, (8, 128), 0) == 4 + lax.div(device, 8)
    small_s[2:4] = narrow[0:2, 0:128]
    small_s[4:5] = jnp.sum(jnp.where(owner, wide[:, 0:128], 0.0), axis=0, keepdims=True)
    recv("z3q")
    for p in range(PAIRS):
        q_last(p)
    give(gq_s, gq_o)
    give(gk_s, gk_o)
    give(gv_s, gv_o)
    recv("bz")
    total = bb[2] + rb[4] + rb[5] + rb[6]
    narrow = pltpu.roll(total, lax.rem(128 - lax.rem(device, 8) * 16, 128), 1)
    for row in range(2):
        owner = lax.broadcasted_iota(jnp.int32, (16, 128), 0) == row * 4 + lax.div(device, 8)
        small_s[row : row + 1] = jnp.sum(jnp.where(owner, narrow, 0.0), axis=0, keepdims=True)
    lane = lax.broadcasted_iota(jnp.int32, (1, 128), 1)
    small_s[5:6] = jnp.where(lane == 0, total[8:9], total[9:10])
    small_s[6:8] = jnp.zeros((2, 128), F32)
    give(small_s, small_o)
    for one in sum_batches:
        if one not in waited:
            sent(one) if isinstance(one, str) else sent(*one)
    for one in given:
        one.wait()


def results_kernel(*refs):
    taken, given, held, ends, sem = refs[:9], refs[9:23], refs[23:32], refs[32:38], refs[38]
    moves = []
    for i in (8, 2, 3, 4, 5, 6, 7, 0, 1):
        rows, parts = taken[i].shape[0], {0: 4, 1: 8}.get(i, 1)
        for part in range(parts):
            at = pl.ds(part * rows // parts, rows // parts)
            there = None if i == 8 else (given[i].at[0] if i < 2 else given[i]).at[at]
            moves.append((taken[i].at[at], held[i].at[at], there))
    come = [pltpu.make_async_copy(src, mid, sem.at[n]) for n, (src, mid, _) in enumerate(moves)]
    for one in come:
        one.start()
    go = []
    for n, (_, mid, dst) in enumerate(moves):
        come[n].wait()
        if n == 0:
            for row, ref in enumerate(ends):
                ref[...] = held[8][row, 0 : ref.shape[0]]
                go.append(pltpu.make_async_copy(ref, given[8 + row], sem.at[len(moves) + row]))
                go[-1].start()
        else:
            go.append(pltpu.make_async_copy(mid, dst, sem.at[len(moves) + 6 + n]))
            go[-1].start()
    for one in go:
        one.wait()


def scratch():
    v = pltpu.VMEM
    return [
        v((1, 1024), jnp.int32),
        pltpu.SMEM((1,), jnp.int32),
        pltpu.SMEM((2,), F32),
        *[v((16,), BF)] * 4,
        v((64,), BF),
        v((8, 128), F32),
        v((16, 512), F32),
        v((16, 512), F32),
        v((16, 512), F32),
        v((16, 512), F32),
        v((16, 2048), F32),
        v((64, 512), F32),
        v((8, 128), F32),
        v((1024, 512), BF),
        v((512, 512), BF),
        v((3, 2, 2, 2, 64, 512), BF),
        v((2, 2, 2, 64, 640), BF),
        v((4, 2, 2, 2, 128, 512), BF),
        v((8, 80, 512), BF),
        v((8, 80, 1024), BF),
        v((512, 1024), BF),
        v((8, 1024, 512), F32),
        v((8, 8, 512), F32),
        v((1024, 512), F32),
        v((1024, 512), BF),
        v((512, 512), BF),
        v((512, 512), F32),
        v((512, 512), BF),
        v((512, 512), F32),
        v((512, 512), F32),
        v((512, 512), BF),
        v((512, 512), BF),
        v((512, 512), BF),
        v((2, 2, 128, 1024), F32),
        v((2, 2, 128, 512), F32),
        v((4, 2, 2, 2, 128, 512), F32),
        v((4, 2, 2, 128, 512), F32),
        v((4, 2, 2, 64, 512), BF),
        v((4, 2, 2, 64, 512), BF),
        v((4, 2, 64, 512), BF),
        v((4, 2, 64, 512), BF),
        v((4, 3, 16, 512), BF),
        v((4, 3, 16, 512), BF),
        v((3, 64, 512), BF),
        v((3, 64, 512), BF),
        v((2, 2, 2, 64, 512), F32),
        v((2, 2, 64, 512), F32),
        v((2, 2, 32, 512), BF),
        v((2, 2, 32, 512), BF),
        v((2, 32, 512), BF),
        v((2, 32, 512), BF),
        v((3, 16, 512), BF),
        v((3, 16, 512), BF),
        v((4, 2, 2, 32, 384), BF),
        v((4, 2, 2, 32, 384), BF),
        v((4, 2, 32, 384), BF),
        v((4, 2, 32, 384), BF),
        v((4, 3, 16, 384), BF),
        v((4, 3, 16, 384), BF),
        v((2, 2, 2, 64, 384), F32),
        v((2, 2, 64, 384), F32),
        v((2, 3, 64, 384), BF),
        v((2, 3, 64, 384), BF),
        v((128, 512), F32),
        v((3, 16, 128), F32),
        v((7, 16, 128), F32),
        v((3, 8, 512), F32),
        v((7, 8, 512), F32),
        v((32, 128), BF),
        pltpu.SemaphoreType.DMA((41,)),
        pltpu.SemaphoreType.DMA((80,)),
        pltpu.SemaphoreType.DMA((32,)),
    ]


def on_device(
    tokens,
    segments,
    fill_length,
    query_weight,
    key_weight,
    value_weight,
    output_weight,
    query_bias,
    value_bias,
    output_bias,
    inner_weight,
    inner_bias,
    outer_weight,
    outer_bias,
    residual_gates,
    cotangent,
):
    names = ("dp", "shard")
    several = lax.axis_size("dp") > GROUP
    place = lax.rem(lax.axis_index("dp"), GROUP) * 2 + lax.axis_index("shard")

    def block_of(shard):
        if not several:
            return shard
        whole = lax.all_gather(shard, names, axis=0, tiled=True)
        rows = whole.shape[0] // (2 * GROUP)
        return lax.dynamic_slice_in_dim(whole, place * rows, rows, 0)

    def owned(block):
        if not several:
            return block
        rows = block.shape[0]
        whole = jnp.zeros((rows * 2 * GROUP, *block.shape[1:]), F32)
        whole = lax.dynamic_update_slice_in_dim(whole, block, place * rows, 0)
        return lax.psum_scatter(whole, names, scatter_dimension=0, tiled=True)

    query_weight, key_weight, value_weight, output_weight, inner_weight, outer_weight = map(
        block_of, (query_weight, key_weight, value_weight, output_weight, inner_weight, outer_weight)
    )
    query_bias, value_bias, output_bias, inner_bias, outer_bias = map(
        block_of, (query_bias, value_bias, output_bias, inner_bias, outer_bias)
    )
    hbm = pl.BlockSpec(memory_space=pl.ANY)
    shape = jax.ShapeDtypeStruct
    outs = pl.pallas_call(
        layer_kernel,
        out_shape=[
            shape((512, 512), BF),
            shape((512, 512), F32),
            shape((16, 512), F32),
            shape((16, 512), F32),
            shape((16, 512), F32),
            shape((16, 512), F32),
            shape((16, 2048), F32),
            shape((64, 512), F32),
            shape((8, 128), F32),
        ],
        in_specs=[hbm] * 16,
        out_specs=[hbm] * 9,
        scratch_shapes=scratch(),
        compiler_params=pltpu.CompilerParams(
            collective_id=0, has_side_effects=True, vmem_limit_bytes=VMEM_BYTES
        ),
    )(
        tokens.reshape(512, 512),
        cotangent.reshape(512, 512),
        segments,
        fill_length,
        residual_gates,
        query_bias,
        value_bias,
        output_bias,
        outer_bias,
        inner_bias,
        query_weight,
        key_weight,
        value_weight,
        output_weight,
        inner_weight,
        outer_weight,
    )
    flat = [shape(o.shape, o.dtype) for o in outs[2:8]] + [shape((n,), F32) for n in (16, 16, 16, 16, 64, 2)]
    outs = pl.pallas_call(
        results_kernel,
        out_shape=[shape((1, 512, 512), BF), shape((1, 512, 512), F32)] + flat,
        in_specs=[pl.BlockSpec(memory_space=pltpu.HBM)] * 9,
        out_specs=[hbm] * 14,
        scratch_shapes=[pltpu.VMEM(o.shape, o.dtype) for o in outs]
        + [pltpu.VMEM(o.shape, o.dtype) for o in flat[6:]]
        + [pltpu.SemaphoreType.DMA((45,))],
        compiler_params=pltpu.CompilerParams(vmem_limit_bytes=VMEM_BYTES),
    )(*outs)
    layer, token_grads, gq, gk, gv, go, gi, gout, g_query, g_value, g_output, g_outer, g_inner, gate_sums = outs
    if several:
        gate_sums = lax.psum(jnp.where(place == 0, gate_sums, 0.0), names)
    grads = (gq, gk, gv, go, g_query, g_value, g_output, gi, g_inner, gout, g_outer)
    return (layer, token_grads, *map(owned, grads), gate_sums)


def solution(mesh):
    spread = P(("dp", "shard"))
    return jax.shard_map(
        on_device,
        mesh=mesh,
        in_specs=(
            P("dp", "shard", None),
            P("dp", None),
            P("dp"),
            *([P(("dp", "shard"), None)] * 4),
            *([spread] * 3),
            P(("dp", "shard"), None),
            spread,
            P(("dp", "shard"), None),
            spread,
            P(),
            P("dp", "shard", None),
        ),
        out_specs=(
            P("dp", "shard", None),
            P("dp", "shard", None),
            *([P(("dp", "shard"), None)] * 4),
            *([spread] * 3),
            P(("dp", "shard"), None),
            spread,
            P(("dp", "shard"), None),
            spread,
            P(),
        ),
        check_vma=False,
    )
```
